128 devices in a mesh: dp: 8 (over z_lo, y), ctx: 16 (over z_hi, x, core).
Axes of the slice: x: 4, y: 4, z: 4 (z_hi: 2, z_lo: 2; z = z_hi * 2 + z_lo), core: 2. Of those that a mesh axis runs over, the one named last changes fastest.
Arguments:
- inputs: bfloat16 [16384, 2048], P(('dp', 'ctx')), may hold values from -6 to 6
- positions: int32 [16384], P(('dp', 'ctx')), may hold values from 0 to 1919, as said below
- cotangent: bfloat16 [16384, 2048], P(('dp', 'ctx')), may hold values from -6 to 6
- w_query: bfloat16 [2048, 2048], P('dp'), may hold values from -0.125 to 0.125
- w_key: bfloat16 [2048, 256], P('dp'), may hold values from -0.125 to 0.125
- w_value: bfloat16 [2048, 256], P('dp'), may hold values from -0.125 to 0.125
- w_out: bfloat16 [2048, 2048], P('dp'), may hold values from -0.75 to 0.75
- w_gate: bfloat16 [2048, 5632], P('dp'), may hold values from -0.125 to 0.125
- w_up: bfloat16 [2048, 5632], P('dp'), may hold values from -0.125 to 0.125
- w_down: bfloat16 [5632, 2048], P('dp'), may hold values from -0.15625 to 0.15625
- gain_attn: bfloat16 [2048], P('dp'), may hold values from 0.25 to 1.75
- gain_mlp: bfloat16 [2048], P('dp'), may hold values from 0.25 to 1.75
Outputs:
- output: bfloat16 [16384, 2048], P(('dp', 'ctx'))
- grad_inputs: float32 [16384, 2048], P(('dp', 'ctx'))
- grad_query: float32 [2048, 2048], P('dp')
- grad_key: float32 [2048, 256], P('dp')
- grad_value: float32 [2048, 256], P('dp')
- grad_out: float32 [2048, 2048], P('dp')
- grad_gate: float32 [2048, 5632], P('dp')
- grad_up: float32 [2048, 5632], P('dp')
- grad_down: float32 [5632, 2048], P('dp')
- grad_gain_attn: float32 [2048], P('dp')
- grad_gain_mlp: float32 [2048], P('dp')
The draws below stay inside these ranges and needn't reach their ends.
Inputs may be any that keep to these rules, and one draw needn't show every extreme that they name: Within each sequence positions count up from 0 inside three contiguous documents: a first one begins the sequence and ends inside its first 128 tokens, a second one of exactly 1920 tokens follows it, and a third one fills the rest.
All inputs are finite; a program needn't handle non-finite values.
Results may differ from the reference program's by a relative error of at most 0.03.
Values may be sent and summed in bfloat16 or wider, within the bound.
No kernel may reach another device: no remote copies, remote signals or barrier semaphores. Data moves between devices by JAX's collectives and lax.ppermute only.
A program may use at most 320 MiB of HBM per device.

```python
import math
import jax
import jax.numpy as jnp
from jax import lax

D = 2048
HEADS = 32
KV_HEADS = 4
HEAD_DIM = 64
FF = 5632
TOK_DEV = 128
LENGTH = 2048
SEQS = 8
TOKENS = 16384


def draw_positions(key, part):
    key = jax.random.fold_in(key, 11)
    head_end = jax.random.randint(key, (SEQS, 1), 1, TOK_DEV)
    tail_start = head_end + (LENGTH - TOK_DEV)
    seq_index = jnp.arange(LENGTH, dtype=jnp.int32)[None, :]
    doc_begin = jnp.where(seq_index < head_end, 0, jnp.where(seq_index < tail_start, head_end, tail_start))
    return (seq_index - doc_begin).reshape(TOKENS).astype(jnp.int32)


def block_levels(stream_key, shape, split, least, high):
    factor_of, own = 1.0, jax.random.fold_in(stream_key, 6)
    for axis_at, shards_of in split:
        draws = jnp.exp(jax.random.uniform(jax.random.fold_in(own, axis_at), (shards_of,), jnp.float32, least / len(split), high / len(split)))
        factor_of = factor_of * jnp.repeat(draws, shape[axis_at] // shards_of).reshape([-1 if axis == axis_at else 1 for axis in range(len(shape))])
    return factor_of


def centred(key, shape, width, reach, shards=(), kind=jnp.bfloat16):
    values = width * jax.random.normal(key, shape, jnp.float32)
    if shards:
        values = values * block_levels(key, shape, shards, -0.22, 0.18)
    return jnp.clip(values, -reach, reach).astype(kind)


def setup_inputs(seed: int = 0) -> dict:
    streams_of = jax.random.split(jax.random.key(seed), 13)
    return {
        "inputs": centred(streams_of[0], (TOKENS, D), 1.0, 6.0, ((0, 128),)),
        "positions": draw_positions(jax.random.fold_in(streams_of[12], 71), 0),
        "cotangent": centred(streams_of[2], (TOKENS, D), 1.0, 6.0, ((0, 128),)),
        "w_query": centred(streams_of[3], (D, HEADS * HEAD_DIM), D ** -0.5, 0.125, ((0, 8),)),
        "w_key": centred(streams_of[4], (D, KV_HEADS * HEAD_DIM), D ** -0.5, 0.125, ((0, 8),)),
        "w_value": centred(streams_of[5], (D, KV_HEADS * HEAD_DIM), D ** -0.5, 0.125, ((0, 8),)),
        "w_out": centred(streams_of[6], (HEADS * HEAD_DIM, D), (HEADS * HEAD_DIM // 32) ** -0.5, 0.75, ((0, 8),)),
        "w_gate": centred(streams_of[7], (D, FF), D ** -0.5, 0.125, ((0, 8),)),
        "w_up": centred(streams_of[8], (D, FF), D ** -0.5, 0.125, ((0, 8),)),
        "w_down": centred(streams_of[9], (FF, D), (FF // 4) ** -0.5, 0.15625, ((0, 8),)),
        "gain_attn": jnp.clip(1.0 + 0.15 * jax.random.normal(streams_of[10], (D,), jnp.float32), 0.25, 1.75).astype(jnp.bfloat16),
        "gain_mlp": jnp.clip(1.0 + 0.15 * jax.random.normal(streams_of[11], (D,), jnp.float32), 0.25, 1.75).astype(jnp.bfloat16),
    }


EPSILON = 1e-05
THETA = 10000.0
HIGH = lax.Precision.HIGHEST

@jax.custom_vjp
def low(v):
    return lax.optimization_barrier(v.astype(jnp.bfloat16)).astype(jnp.float32)

@jax.custom_vjp
def low_back(v):
    return v

def low_keep(v):
    return (low(v), None)

def low_pass(kept, grad):
    return (grad,)

def back_keep(v):
    return (v, None)

def back_low(kept, grad):
    return (low(grad),)
low.defvjp(low_keep, low_pass)
low_back.defvjp(back_keep, back_low)

def matmul(left_rows, right_rows):
    return jnp.dot(left_rows, right_rows, precision=HIGH, preferred_element_type=jnp.float32)

def rms_scale(values):
    return lax.rsqrt(lax.optimization_barrier(jnp.mean(values * values, axis=-1, keepdims=True)) + EPSILON)

def rotary_tables(positions, head_size):
    half_size = head_size // 2
    frequency = THETA ** (-(jnp.arange(half_size, dtype=jnp.float32) * 2.0 / head_size))
    angles = positions.astype(jnp.float32)[:, None] * frequency[None, :]
    return (jnp.cos(angles)[:, None, :], jnp.sin(angles)[:, None, :])

def rotate(values, cosine, sine_table):
    half_size = values.shape[-1] // 2
    first_half = values[..., :half_size]
    second_half = values[..., half_size:]
    return jnp.concatenate([first_half * cosine - second_half * sine_table, second_half * cosine + first_half * sine_table], axis=-1)

def attention(query_rows, keys, values_kv, positions):
    length = query_rows.shape[0]
    per_group = HEADS // KV_HEADS
    keys_full = jnp.repeat(keys, per_group, axis=1)
    values_full = jnp.repeat(values_kv, per_group, axis=1)
    block_rows = 512 if length % 512 == 0 else length
    key_index = jnp.arange(length, dtype=jnp.int32)
    doc_start = key_index - positions
    scores_scale_factor = 1.0 / math.sqrt(HEAD_DIM)

    def one_block(block_item):
        query_block, block_start = block_item
        query_index = block_start + jnp.arange(block_rows, dtype=jnp.int32)
        starts_here = lax.dynamic_slice_in_dim(doc_start, block_start, block_rows)
        attention_scores = low_back(jnp.einsum('thd,shd->hts', query_block, keys_full, precision=HIGH)) * scores_scale_factor
        allowed = (key_index[None, :] <= query_index[:, None]) & (key_index[None, :] >= starts_here[:, None])
        attention_scores = jnp.where(allowed[None], attention_scores, -1e+30)
        probability = low(jax.nn.softmax(attention_scores, axis=-1))
        return jnp.einsum('hts,shd->thd', probability, values_full, precision=HIGH)
    blocks = query_rows.reshape(length // block_rows, block_rows, HEADS, HEAD_DIM)
    starts = jnp.arange(length // block_rows, dtype=jnp.int32) * block_rows
    outputs = lax.map(jax.checkpoint(one_block), (blocks, starts))
    return outputs.reshape(length, HEADS * HEAD_DIM)

def decoder_layer(tokens_seq, positions_seq, weights):
    w_query, w_key, w_value, w_out, w_gate, w_up, w_down, gain_attn, gain_mlp = weights
    length = tokens_seq.shape[0]
    cosine, sine_table = rotary_tables(positions_seq, HEAD_DIM)
    normed = low(tokens_seq * rms_scale(tokens_seq) * gain_attn)
    query_raw = low_back(matmul(normed, w_query)).reshape(length, HEADS, HEAD_DIM)
    key_raw = low_back(matmul(normed, w_key)).reshape(length, KV_HEADS, HEAD_DIM)
    value_raw = low_back(matmul(normed, w_value)).reshape(length, KV_HEADS, HEAD_DIM)
    query_rows = low(rotate(query_raw, cosine, sine_table))
    keys = low(rotate(key_raw, cosine, sine_table))
    values_kv = low(value_raw)
    mixed = low(low_back(attention(query_rows, keys, values_kv, positions_seq)))
    residual = tokens_seq + low_back(matmul(mixed, w_out))
    normed_mlp = low(residual * rms_scale(residual) * gain_mlp)
    gate_proj = low_back(matmul(normed_mlp, w_gate))
    up_proj = low_back(matmul(normed_mlp, w_up))
    hidden = low(jax.nn.silu(gate_proj) * up_proj)
    return residual + low_back(matmul(hidden, w_down))

def reference(inputs, positions, cotangent, w_query, w_key, w_value, w_out, w_gate, w_up, w_down, gain_attn, gain_mlp):
    weights_f32 = (w_query.astype(jnp.float32), w_key.astype(jnp.float32), w_value.astype(jnp.float32), w_out.astype(jnp.float32), w_gate.astype(jnp.float32), w_up.astype(jnp.float32), w_down.astype(jnp.float32), gain_attn.astype(jnp.float32), gain_mlp.astype(jnp.float32))

    def forward(tokens_all, weights):
        seq_tokens = tokens_all.reshape(SEQS, LENGTH, D)
        seq_positions = positions.reshape(SEQS, LENGTH)

        def per_sequence(state_none, seq_item):
            return (state_none, decoder_layer(seq_item[0], seq_item[1], weights))
        outputs = lax.scan(per_sequence, jnp.zeros((), jnp.float32), (seq_tokens, seq_positions))[1]
        return outputs.reshape(TOKENS, D)
    result, pullback = jax.vjp(forward, inputs.astype(jnp.float32), weights_f32)
    grad_tokens, attention_weight_gradient = pullback(cotangent.astype(jnp.float32))
    return (result.astype(jnp.bfloat16), grad_tokens, attention_weight_gradient[0], attention_weight_gradient[1], attention_weight_gradient[2], attention_weight_gradient[3], attention_weight_gradient[4], attention_weight_gradient[5], attention_weight_gradient[6], attention_weight_gradient[7], attention_weight_gradient[8])
```

```python
import functools
import math

import jax
import jax.numpy as jnp
from jax import lax
from jax.experimental import pallas as pl
from jax.experimental.pallas import tpu as pltpu
from jax.sharding import Mesh, PartitionSpec as P

D = 2048
HEADS = 32
KV_HEADS = 4
HEAD_DIM = 64
FF = 5632
LENGTH = 2048
MIDDLE = 1920
EPSILON = 1e-05
THETA = 10000.0
NEG_LARGE = -1e30

AXES = ("zl", "y", "zh", "x", "core")
Z_RING = ("zl", "zh")
GROUP = 8
TOK = 128
HALF = GROUP * TOK
CHUNK = D // GROUP
FF_OWN = FF // GROUP
Q_OWN = HEADS * HEAD_DIM // GROUP
HEADS_OWN = HEADS // GROUP
KEY_CHUNK = 256
ROWS_Q = HEADS_OWN * TOK

F32 = jnp.float32
BF16 = jnp.bfloat16


def ring(values, axis, step):
    if axis == Z_RING:
        spot = [(z % 2) * 2 + z // 2 for z in range(4)]
        return lax.ppermute(values, axis, [(spot[z], spot[(z + step) % 4]) for z in range(4)])
    count = lax.axis_size(axis)
    return lax.ppermute(values, axis, [(i, (i + step) % count) for i in range(count)])


def rail_gather(block):
    half = block.shape[0] // 2
    ahead = ring(block, "x", -1)
    behind = ring(block, "x", 1)
    far = jnp.concatenate([ring(ahead[:half], "x", -1), ring(behind[half:], "x", 1)])
    return [block, ahead, far, behind]


def group_gather(block):
    rail = jnp.concatenate(rail_gather(block))
    return jnp.concatenate([rail, ring(rail, "core", 1)])


def group_scatter(own_rail, other_rail):
    total = own_rail + ring(other_rail.astype(BF16), "core", 1).astype(F32)
    rows = total.shape[0] // 4
    half = rows // 2
    here, ahead, far, behind = [total[i * rows : (i + 1) * rows] for i in range(4)]
    far = far.astype(BF16)
    from_behind = ring(far[:half], "x", 1).astype(F32)
    from_ahead = ring(far[half:], "x", -1).astype(F32)
    ahead = jnp.concatenate([ahead[:half] + from_behind, ahead[half:]]).astype(BF16)
    behind = jnp.concatenate([behind[:half], behind[half:] + from_ahead]).astype(BF16)
    return here + ring(ahead, "x", 1).astype(F32) + ring(behind, "x", -1).astype(F32)


def weight_gather(piece, axis):
    first = jnp.concatenate([piece, ring(piece, "y", -1)], axis=axis)
    second = jnp.concatenate([ring(piece, "y", 2), ring(piece, "y", 1)], axis=axis)
    return jnp.concatenate(
        [first, second, ring(first, Z_RING, 1), ring(second, Z_RING, -1)], axis=axis
    )


def weight_scatter(partial, axis):
    size = partial.shape[axis] // 8

    def part(start, count):
        return lax.slice_in_dim(partial, start * size, (start + count) * size, axis=axis)

    from_below = ring(part(4, 2).astype(BF16), Z_RING, 1).astype(F32)
    from_above = ring(part(6, 2).astype(BF16), Z_RING, -1).astype(F32)
    first = part(0, 2).astype(F32) + from_below
    second = part(2, 2).astype(F32) + from_above

    def cut(values, at):
        return lax.slice_in_dim(values, at * size, (at + 1) * size, axis=axis)

    total = (
        cut(first, 0)
        + ring(cut(first, 1).astype(BF16), "y", 1).astype(F32)
        + ring(cut(second, 0).astype(BF16), "y", 2).astype(F32)
        + ring(cut(second, 1).astype(BF16), "y", -1).astype(F32)
    ).astype(BF16)
    return (total.astype(F32) + ring(total, "zh", 1).astype(F32)).astype(BF16)


def swap_roles(values):
    return lax.ppermute(
        values,
        ("zl", "y", "x", "core"),
        [(a * GROUP + b, b * GROUP + a) for a in range(GROUP) for b in range(GROUP)],
    )


def to_relative(rows, zl, y):
    half = D // 2
    low, high = rows[:, :half], rows[:, half:]
    flipped = zl == 1
    parts = [jnp.where(flipped, high, low), jnp.where(flipped, low, high)]

    def roll(part, by):
        return jnp.concatenate([part[:, by * CHUNK :], part[:, : by * CHUNK]], axis=1)

    parts = [jnp.where((y & 1) == 1, roll(part, 1), part) for part in parts]
    parts = [jnp.where((y & 2) == 2, roll(part, 2), part) for part in parts]
    return jnp.concatenate(parts, axis=1)


def to_absolute(rows, zl, y):
    half = D // 2

    def roll(part, by):
        return jnp.concatenate([part[:, by * CHUNK :], part[:, : by * CHUNK]], axis=1)

    parts = [rows[:, :half], rows[:, half:]]
    parts = [jnp.where((y & 1) == 1, roll(part, 3), part) for part in parts]
    parts = [jnp.where((y & 2) == 2, roll(part, 2), part) for part in parts]
    flipped = zl == 1
    return jnp.concatenate(
        [jnp.where(flipped, parts[1], parts[0]), jnp.where(flipped, parts[0], parts[1])],
        axis=1,
    )


def tokens_to_natural(columns, x, core):
    width = 4 * TOK
    rails = [columns[:, :width], columns[:, width:]]

    def roll(part, by):
        return jnp.concatenate([part[:, by * TOK :], part[:, : by * TOK]], axis=1)

    rails = [jnp.where((x & 1) == 1, roll(part, 3), part) for part in rails]
    rails = [jnp.where((x & 2) == 2, roll(part, 2), part) for part in rails]
    flipped = core == 1
    even, odd = (
        jnp.where(flipped, rails[1], rails[0]),
        jnp.where(flipped, rails[0], rails[1]),
    )
    return jnp.concatenate(
        [
            part[:, i * TOK : (i + 1) * TOK]
            for i in range(4)
            for part in (even, odd)
        ],
        axis=1,
    )


def tokens_to_relative(columns, x, core):
    blocks = [columns[:, i * TOK : (i + 1) * TOK] for i in range(GROUP)]
    even = jnp.concatenate(blocks[0::2], axis=1)
    odd = jnp.concatenate(blocks[1::2], axis=1)
    flipped = core == 1
    rails = [jnp.where(flipped, odd, even), jnp.where(flipped, even, odd)]

    def roll(part, by):
        return jnp.concatenate([part[:, by * TOK :], part[:, : by * TOK]], axis=1)

    rails = [jnp.where((x & 1) == 1, roll(part, 1), part) for part in rails]
    rails = [jnp.where((x & 2) == 2, roll(part, 2), part) for part in rails]
    return jnp.concatenate(rails, axis=1)


def heads_side_by_side(block):
    return jnp.concatenate(
        [block[i * HEAD_DIM : (i + 1) * HEAD_DIM] for i in range(HEADS_OWN)], axis=1
    )


def heads_stacked(block):
    return jnp.concatenate(
        [block[:, i * TOK : (i + 1) * TOK] for i in range(HEADS_OWN)], axis=0
    )


def block_bounds(meta, j):
    half_at, place = meta[0], meta[2 + j]
    first = jnp.where(half_at == 1, 0, HALF // KEY_CHUNK)
    last = HALF // KEY_CHUNK + place * TOK // KEY_CHUNK
    every = (half_at == 1) & (place == GROUP - 1)
    return first, last, every


def allowed_keys(meta, j, chunk):
    half_at, head_end, place = meta[0], meta[1], meta[2 + j]
    shape = (KEY_CHUNK, ROWS_Q)
    column = lax.broadcasted_iota(jnp.int32, (1, ROWS_Q), 1)
    query = half_at * HALF + place * TOK + (column & (TOK - 1))
    start = jnp.where(
        query < head_end,
        0,
        jnp.where(query < head_end + MIDDLE, head_end, head_end + MIDDLE),
    )
    key = (
        lax.broadcasted_iota(jnp.int32, shape, 0)
        + chunk * KEY_CHUNK
        + (half_at - 1) * HALF
    )
    return (key <= query) & (key >= start)


def dot_kn(left, right):
    return jnp.dot(left, right, preferred_element_type=F32)


def dot_nt(left, right):
    return lax.dot_general(
        left, right, (((1,), (1,)), ((), ())), preferred_element_type=F32
    )


def forward_kernel(meta, q_ref, k_ref, v_ref, out_ref, lse_ref, top_ref, acc_ref):
    j = pl.program_id(0)
    query = heads_side_by_side(q_ref[...])
    first, last, every = block_bounds(meta, j)
    top_ref[...] = jnp.full_like(top_ref, NEG_LARGE)
    acc_ref[...] = jnp.zeros_like(acc_ref)

    def step(chunk, masked):
        at = pl.multiple_of(chunk * KEY_CHUNK, KEY_CHUNK)
        scores = dot_kn(k_ref[pl.ds(at, KEY_CHUNK), :], query)
        if masked:
            scores = jnp.where(allowed_keys(meta, j, chunk), scores, NEG_LARGE)
        old = top_ref[...]
        new = jnp.maximum(old, jnp.max(scores, axis=0, keepdims=True))
        weights = jnp.exp(scores - new).astype(BF16)
        acc_ref[...] = acc_ref[...] * jnp.exp(old - new) + dot_kn(
            v_ref[:, pl.ds(at, KEY_CHUNK)], weights
        )
        top_ref[...] = new

    def body(chunk, carry):
        masked = every | (chunk == first) | (chunk == last)

        @pl.when(masked)
        def _():
            step(chunk, True)

        @pl.when(jnp.logical_not(masked))
        def _():
            step(chunk, False)

        return carry

    lax.fori_loop(first, last + 1, body, 0)
    total = acc_ref[HEAD_DIM : HEAD_DIM + 1, :]
    out_ref[...] = heads_stacked(acc_ref[:HEAD_DIM, :] / total)
    lse_ref[...] = jnp.broadcast_to(top_ref[...] + jnp.log(total), lse_ref.shape)


def backward_kernel(
    meta, q_ref, g_ref, o_ref, lse_ref, k_ref, v_ref, kt_ref, dq_ref, dk_ref, dv_ref, acc_ref
):
    j = pl.program_id(0)

    @pl.when(j == 0)
    def _():
        dk_ref[...] = jnp.zeros_like(dk_ref)
        dv_ref[...] = jnp.zeros_like(dv_ref)

    query = heads_side_by_side(q_ref[...])
    grad = heads_side_by_side(g_ref[...])
    mixed = heads_side_by_side(o_ref[...])
    delta = jnp.sum(grad.astype(F32) * mixed, axis=0, keepdims=True)
    lse = lse_ref[0:1, :]
    first, last, every = block_bounds(meta, j)
    acc_ref[...] = jnp.zeros_like(acc_ref)

    def step(chunk, masked):
        at = pl.multiple_of(chunk * KEY_CHUNK, KEY_CHUNK)
        rows = pl.ds(at, KEY_CHUNK)
        scores = dot_kn(k_ref[rows, :], query)
        grad_probs = dot_kn(v_ref[rows, :], grad)
        if masked:
            scores = jnp.where(allowed_keys(meta, j, chunk), scores, NEG_LARGE)
        probs = jnp.exp(scores - lse)
        grad_scores = (probs * (grad_probs - delta)).astype(BF16)
        acc_ref[...] += dot_kn(kt_ref[:, rows], grad_scores)
        dk_ref[:, rows] += dot_nt(query, grad_scores)
        dv_ref[:, rows] += dot_nt(grad, probs.astype(BF16))

    def body(chunk, carry):
        masked = every | (chunk == first) | (chunk == last)

        @pl.when(masked)
        def _():
            step(chunk, True)

        @pl.when(jnp.logical_not(masked))
        def _():
            step(chunk, False)

        return carry

    lax.fori_loop(first, last + 1, body, 0)
    dq_ref[...] = heads_stacked(acc_ref[...] * (1.0 / math.sqrt(HEAD_DIM)))


def whole(shape):
    return pl.BlockSpec(shape, lambda j, meta: (0,) * len(shape))


def token_block(rows):
    return pl.BlockSpec((rows, TOK), lambda j, meta: (0, j))


V_ROWS = 80
LSE_ROWS = 8


def attend(meta, query_t, keys, values_t):
    ones = jnp.ones((1, 2 * HALF), BF16)
    pad = jnp.zeros((V_ROWS - HEAD_DIM - 1, 2 * HALF), BF16)
    values_ones = jnp.concatenate([values_t, ones, pad])
    return pl.pallas_call(
        forward_kernel,
        grid_spec=pltpu.PrefetchScalarGridSpec(
            num_scalar_prefetch=1,
            grid=(GROUP,),
            in_specs=[
                token_block(Q_OWN),
                whole((2 * HALF, HEAD_DIM)),
                whole((V_ROWS, 2 * HALF)),
            ],
            out_specs=[
                token_block(Q_OWN),
                pl.BlockSpec((LSE_ROWS, ROWS_Q), lambda j, meta: (j, 0)),
            ],
            scratch_shapes=[
                pltpu.VMEM((1, ROWS_Q), F32),
                pltpu.VMEM((V_ROWS, ROWS_Q), F32),
            ],
        ),
        out_shape=[
            jax.ShapeDtypeStruct((Q_OWN, HALF), F32),
            jax.ShapeDtypeStruct((GROUP * LSE_ROWS, ROWS_Q), F32),
        ],
        compiler_params=pltpu.CompilerParams(vmem_limit_bytes=32 * 1024 * 1024),
        name="attend",
    )(meta, query_t, keys, values_ones)


def attend_back(meta, query_t, grad_t, attn_t, lse, keys, values, keys_t):
    return pl.pallas_call(
        backward_kernel,
        grid_spec=pltpu.PrefetchScalarGridSpec(
            num_scalar_prefetch=1,
            grid=(GROUP,),
            in_specs=[
                token_block(Q_OWN),
                token_block(Q_OWN),
                token_block(Q_OWN),
                pl.BlockSpec((LSE_ROWS, ROWS_Q), lambda j, meta: (j, 0)),
                whole((2 * HALF, HEAD_DIM)),
                whole((2 * HALF, HEAD_DIM)),
                whole((HEAD_DIM, 2 * HALF)),
            ],
            out_specs=[
                token_block(Q_OWN),
                whole((HEAD_DIM, 2 * HALF)),
                whole((HEAD_DIM, 2 * HALF)),
            ],
            scratch_shapes=[pltpu.VMEM((HEAD_DIM, ROWS_Q), F32)],
        ),
        out_shape=[
            jax.ShapeDtypeStruct((Q_OWN, HALF), F32),
            jax.ShapeDtypeStruct((HEAD_DIM, 2 * HALF), F32),
            jax.ShapeDtypeStruct((HEAD_DIM, 2 * HALF), F32),
        ],
        compiler_params=pltpu.CompilerParams(vmem_limit_bytes=32 * 1024 * 1024),
        name="attend_back",
    )(meta, query_t, grad_t, attn_t, lse, keys, values, keys_t)


def assemble_kernel(widths, place, *refs):
    pieces, outs, stack = refs[:8], refs[8:-1], refs[-1]
    for i, piece in enumerate(pieces):
        stack[place[i]] = piece[...]
    for at in range(GROUP):
        values = stack[at].astype(F32)
        start = 0
        for out, width in zip(outs, widths, strict=True):
            out[:, at * width : (at + 1) * width] = values[:, start : start + width]
            start += width


def assemble(place, pieces, widths, rows):
    count, width = pieces[0].shape
    return pl.pallas_call(
        functools.partial(assemble_kernel, widths),
        grid_spec=pltpu.PrefetchScalarGridSpec(
            num_scalar_prefetch=1,
            grid=(count // rows,),
            in_specs=[pl.BlockSpec((rows, width), lambda i, place: (i, 0))] * 8,
            out_specs=[
                pl.BlockSpec((rows, GROUP * w), lambda i, place: (i, 0)) for w in widths
            ],
            scratch_shapes=[pltpu.VMEM((GROUP, rows, width), BF16)],
        ),
        out_shape=[jax.ShapeDtypeStruct((count, GROUP * w), F32) for w in widths],
        compiler_params=pltpu.CompilerParams(vmem_limit_bytes=32 * 1024 * 1024),
        name="assemble",
    )(place, *pieces)


def group_pieces(piece):
    rail = rail_gather(piece)
    stacked = ring(jnp.concatenate(rail), "core", 1)
    rows = piece.shape[0]
    return rail + [stacked[i * rows : (i + 1) * rows] for i in range(4)]


def rms_scale(values):
    return lax.rsqrt(jnp.mean(values * values, axis=-1, keepdims=True) + EPSILON)


def rotate_t(values, cosine, sine_table):
    half = HEAD_DIM // 2
    first, second = values[:, :half], values[:, half:]
    return jnp.concatenate(
        [first * cosine - second * sine_table, second * cosine + first * sine_table], axis=1
    )


def norm_back(grad_normed, values, scale_rows, gain_full):
    unit_rows = values * scale_rows
    grad_unit = grad_normed * gain_full
    return scale_rows * (
        grad_unit - unit_rows * jnp.mean(grad_unit * unit_rows, axis=-1, keepdims=True)
    )


def contract(form, left, right):
    return jnp.einsum(form, left, right, preferred_element_type=F32)


def shards(
    inputs,
    positions,
    cotangent,
    w_query,
    w_key,
    w_value,
    w_out,
    w_gate,
    w_up,
    w_down,
    gain_attn,
    gain_mlp,
):
    zl, y, zh, x, core = (lax.axis_index(axis) for axis in AXES)
    xc = x * 2 + core
    rail_rows = 4 * TOK

    index_here = (zh * GROUP + xc) * TOK + jnp.arange(TOK, dtype=jnp.int32)
    head_end = jnp.where(
        (zh == 0) & (xc == 0),
        jnp.sum((positions == index_here).astype(jnp.int32)),
        index_here[0] - positions[0],
    )
    order = [(s, r) for s in range(2) for r in range(4)]
    places = jnp.stack([((x + r) % 4) * 2 + (core ^ s) for s, r in order]).astype(jnp.int32)
    meta = jnp.concatenate([jnp.stack([zh, head_end]).astype(jnp.int32), places])

    def columns(weight, width):
        return lax.dynamic_slice_in_dim(weight, xc * width, width, axis=1)

    kv_here = jnp.where(core == 0, w_key, w_value)
    kv_here = lax.dynamic_slice_in_dim(kv_here, x * HEAD_DIM, HEAD_DIM, axis=1)
    early = jnp.concatenate(
        [
            columns(w_query, Q_OWN),
            kv_here,
            gain_attn[:, None],
            gain_mlp[:, None],
            jnp.zeros((CHUNK, 62), BF16),
        ],
        axis=1,
    )
    rows_inputs = to_relative(inputs, zl, y)
    rows_cotangent = to_relative(cotangent, zl, y)

    inputs_all = group_gather(rows_inputs)
    early_all = weight_gather(early, 0)
    turned = swap_roles(
        jnp.concatenate([columns(w_down, CHUNK), columns(w_out, CHUNK)], axis=0)
    )
    gate_up_all = weight_gather(
        jnp.concatenate([columns(w_gate, FF_OWN), columns(w_up, FF_OWN)], axis=1), 0
    )
    down_out_all = weight_gather(turned, 1)
    full_down, full_out = down_out_all[:FF_OWN], down_out_all[FF_OWN:]
    full_qkv = early_all[:, : Q_OWN + HEAD_DIM]
    full_gain_attn = early_all[:, Q_OWN + HEAD_DIM].astype(F32)
    full_gain_mlp = early_all[:, Q_OWN + HEAD_DIM + 1].astype(F32)

    index_all = (zh * HALF + places[:, None] * TOK + jnp.arange(TOK, dtype=jnp.int32)).reshape(HALF)
    doc_start = jnp.where(
        index_all < head_end,
        0,
        jnp.where(index_all < head_end + MIDDLE, head_end, head_end + MIDDLE),
    )
    frequency = THETA ** (-(jnp.arange(HEAD_DIM // 2, dtype=F32) * 2.0 / HEAD_DIM))
    angles = frequency[:, None] * (index_all - doc_start).astype(F32)[None, :]
    cosine, sine_table = jnp.cos(angles), jnp.sin(angles)
    is_key = core == 0
    cosine_kv = jnp.where(is_key, cosine, 1.0)
    sine_kv = jnp.where(is_key, sine_table, 0.0)

    tokens_all = inputs_all.astype(F32)
    scale_all = rms_scale(tokens_all)
    unit_all = tokens_all * scale_all
    normed = (unit_all * full_gain_attn).astype(BF16)
    raw_t = contract("dn,td->nt", full_qkv, normed)
    query_t = (
        rotate_t(raw_t[:Q_OWN].reshape(HEADS_OWN, HEAD_DIM, HALF), cosine, sine_table)
        .reshape(Q_OWN, HALF)
        .astype(BF16)
        * (1.0 / math.sqrt(HEAD_DIM))
    ).astype(BF16)
    kv_t = tokens_to_natural(
        rotate_t(raw_t[Q_OWN:][None], cosine_kv, sine_kv)[0].astype(BF16), x, core
    )
    kv_other = ring(kv_t, "core", 1)
    kv_prev = lax.ppermute(kv_t, "zh", [(0, 1)])
    kv_prev_other = lax.ppermute(kv_t, ("zh", "core"), [(0, 3), (1, 2)])
    mine = jnp.concatenate([kv_prev, kv_t], axis=1)
    other = jnp.concatenate([kv_prev_other, kv_other], axis=1)
    keys_t = jnp.where(is_key, mine, other)
    values_t = jnp.where(is_key, other, mine)
    keys, values = keys_t.T, values_t.T
    attn_t, lse = attend(meta, query_t, keys, values_t)
    mixed_t = attn_t.astype(BF16)

    def out_rows(part):
        return contract("kt,kd->td", part, full_out)

    other_part = out_rows(mixed_t[:, rail_rows:])
    own_part = out_rows(mixed_t[:, :rail_rows])
    tokens_here = rows_inputs.astype(F32)
    residual = tokens_here + group_scatter(own_part, other_part)
    scale_mlp = rms_scale(residual)
    normed_mlp = group_gather((residual * scale_mlp * full_gain_mlp).astype(BF16))
    cotangent_all = group_gather(rows_cotangent)

    gate_up = contract("td,df->tf", normed_mlp, gate_up_all)
    gate, upward = gate_up[:, :FF_OWN], gate_up[:, FF_OWN:]
    grad_hidden = contract("td,fd->tf", cotangent_all, full_down)
    sigmoid_gate = jax.nn.sigmoid(gate)
    silu_gate = gate * sigmoid_gate
    hidden = (silu_gate * upward).astype(BF16)
    grad_acts = jnp.concatenate(
        [
            (grad_hidden * upward * sigmoid_gate * (1.0 + gate * (1.0 - sigmoid_gate))).astype(BF16),
            (grad_hidden * silu_gate).astype(BF16),
        ],
        axis=1,
    )

    def back_rows(part):
        return contract("tf,df->td", part, gate_up_all)

    other_part = back_rows(grad_acts[rail_rows:])
    own_part = back_rows(grad_acts[:rail_rows])
    grad_normed_mlp = group_scatter(own_part, other_part)
    grad_residual = rows_cotangent.astype(F32) + norm_back(
        grad_normed_mlp, residual, scale_mlp, full_gain_mlp
    )
    gain_mlp_term = jnp.sum(grad_normed_mlp * (residual * scale_mlp), axis=0)
    grad_attn_out = group_gather(grad_residual.astype(BF16))

    def down_rows(part):
        return contract("tf,fd->td", part, full_down)

    other_part = down_rows(hidden[rail_rows:])
    own_part = down_rows(hidden[:rail_rows])
    output = (residual + group_scatter(own_part, other_part)).astype(BF16)

    part_gate_up = contract("td,tf->df", normed_mlp, grad_acts)
    shard_gate_up = weight_scatter(part_gate_up, 0)
    part_down = contract("tf,td->fd", hidden, cotangent_all)

    grad_mixed_t = contract("kd,td->kt", full_out, grad_attn_out).astype(BF16)
    part_out = contract("kt,td->kd", mixed_t, grad_attn_out)
    shard_down_out = swap_roles(
        weight_scatter(jnp.concatenate([part_down, part_out], axis=0), 1)
    )
    grad_query_t, grad_keys_t, grad_values_t = attend_back(
        meta, query_t, grad_mixed_t, attn_t, lse, keys, values, keys_t
    )
    kept = jnp.where(is_key, grad_keys_t, grad_values_t)
    given = jnp.where(is_key, grad_values_t, grad_keys_t)
    grad_kv = kept + ring(given.astype(BF16), "core", 1).astype(F32)
    grad_kv_t = grad_kv[:, HALF:] + lax.ppermute(
        grad_kv[:, :HALF].astype(BF16), "zh", [(1, 0)]
    ).astype(F32)
    grad_kv_t = tokens_to_relative(grad_kv_t, x, core)
    grad_qkv_t = jnp.concatenate(
        [
            rotate_t(
                grad_query_t.reshape(HEADS_OWN, HEAD_DIM, HALF), cosine, -sine_table
            ).reshape(Q_OWN, HALF),
            rotate_t(grad_kv_t[None], cosine_kv, -sine_kv)[0],
        ]
    ).astype(BF16)

    def normed_rows(part):
        return contract("nt,dn->td", part, full_qkv)

    other_part = normed_rows(grad_qkv_t[:, rail_rows:])
    own_part = normed_rows(grad_qkv_t[:, :rail_rows])
    gain_attn_term = jnp.sum(own_part * unit_all[:rail_rows], axis=0) + jnp.sum(
        other_part * unit_all[rail_rows:], axis=0
    )
    grad_normed = group_scatter(own_part, other_part)
    part_qkv = contract("td,nt->dn", normed, grad_qkv_t)
    shard_qkv = weight_scatter(
        jnp.concatenate(
            [
                part_qkv,
                gain_attn_term[:, None],
                gain_mlp_term[:, None],
                jnp.zeros((D, 62), F32),
            ],
            axis=1,
        ),
        0,
    )
    scale_here = rms_scale(tokens_here)
    grad_inputs = grad_residual + norm_back(grad_normed, tokens_here, scale_here, full_gain_attn)

    grad_gate, grad_up = assemble(
        places, group_pieces(shard_gate_up), (FF_OWN, FF_OWN), 64
    )
    pieces = group_pieces(shard_down_out)
    (grad_down_out,) = assemble(places, pieces, (CHUNK,), 192)
    grad_down, grad_out = grad_down_out[:FF_OWN], grad_down_out[FF_OWN:]
    (grad_qkv,) = assemble(places, group_pieces(shard_qkv), (384,), 256)
    grad_qkv = grad_qkv.reshape(CHUNK, GROUP, 384)
    grad_query = grad_qkv[:, :, :Q_OWN].reshape(CHUNK, HEADS * HEAD_DIM)
    grad_kv_w = grad_qkv[:, :, Q_OWN : Q_OWN + HEAD_DIM].reshape(CHUNK, 4, 2, HEAD_DIM)
    grad_key = grad_kv_w[:, :, 0].reshape(CHUNK, KV_HEADS * HEAD_DIM)
    grad_value = grad_kv_w[:, :, 1].reshape(CHUNK, KV_HEADS * HEAD_DIM)
    grad_gain_attn = jnp.sum(grad_qkv[:, :, Q_OWN + HEAD_DIM], axis=1)
    grad_gain_mlp = jnp.sum(grad_qkv[:, :, Q_OWN + HEAD_DIM + 1], axis=1)
    return (
        to_absolute(output, zl, y),
        to_absolute(grad_inputs, zl, y),
        grad_query,
        grad_key,
        grad_value,
        grad_out,
        grad_gate,
        grad_up,
        grad_down,
        grad_gain_attn,
        grad_gain_mlp,
    )


def solution(mesh):
    split = Mesh(mesh.devices.reshape(2, 4, 2, 4, 2), AXES)
    dp, tokens = ("zl", "y"), AXES
    matrix = P(dp, None)
    return jax.shard_map(
        shards,
        mesh=split,
        in_specs=(
            P(tokens, None),
            P(tokens),
            P(tokens, None),
            matrix,
            matrix,
            matrix,
            matrix,
            matrix,
            matrix,
            matrix,
            P(dp),
            P(dp),
        ),
        out_specs=(
            P(tokens, None),
            P(tokens, None),
            matrix,
            matrix,
            matrix,
            matrix,
            matrix,
            matrix,
            matrix,
            P(dp),
            P(dp),
        ),
        check_vma=False,
    )
```

```python
import functools
import math

import jax
import jax.numpy as jnp
from jax import lax
from jax.experimental import pallas as pl
from jax.experimental.pallas import tpu as pltpu
from jax.sharding import Mesh, PartitionSpec as P

D = 2048
HEADS = 32
KV_HEADS = 4
HEAD_DIM = 64
FF = 5632
LENGTH = 2048
MIDDLE = 1920
EPSILON = 1e-05
THETA = 10000.0
NEG_LARGE = -1e30

AXES = ("zl", "y", "zh", "x", "core")
Z_RING = ("zl", "zh")
GROUP = 8
TOK = 128
HALF = GROUP * TOK
CHUNK = D // GROUP
FF_OWN = FF // GROUP
Q_OWN = HEADS * HEAD_DIM // GROUP
HEADS_OWN = HEADS // GROUP
SUB = FF_OWN // GROUP
OUT_SUB = Q_OWN // GROUP
KEY_CHUNK = 256
ROWS_Q = HEADS_OWN * TOK

F32 = jnp.float32
BF16 = jnp.bfloat16


def ring(values, axis, step):
    if axis == Z_RING:
        spot = [(z % 2) * 2 + z // 2 for z in range(4)]
        return lax.ppermute(values, axis, [(spot[z], spot[(z + step) % 4]) for z in range(4)])
    count = lax.axis_size(axis)
    return lax.ppermute(values, axis, [(i, (i + step) % count) for i in range(count)])


def place_kernel(copies, places, *refs):
    pieces, out, sems = refs[:-2], refs[-2], refs[-1]
    running = [
        pltpu.make_async_copy(
            pieces[piece].at[pl.ds(start, count)], out.at[pl.ds(places[i], count)], sems.at[i]
        )
        for i, (piece, start, count) in enumerate(copies)
    ]
    for copy in running:
        copy.start()
    for copy in running:
        copy.wait()


def cost(microseconds):
    return pl.CostEstimate(
        flops=int(microseconds * 1e9), bytes_accessed=int(microseconds * 3e6), transcendentals=0
    )


def put_in_place(places, pieces, copies, total):
    return pl.pallas_call(
        functools.partial(place_kernel, copies),
        grid_spec=pltpu.PrefetchScalarGridSpec(
            num_scalar_prefetch=1,
            grid=(1,),
            in_specs=[pl.BlockSpec(piece.shape, lambda i, places: (0, 0, 0)) for piece in pieces],
            out_specs=pl.BlockSpec(memory_space=pl.ANY),
            scratch_shapes=[pltpu.SemaphoreType.DMA((len(copies),))],
        ),
        out_shape=jax.ShapeDtypeStruct((total, *pieces[0].shape[1:]), pieces[0].dtype),
        compiler_params=pltpu.CompilerParams(vmem_limit_bytes=32 * 1024 * 1024),
        cost_estimate=cost(1),
        name="put_in_place",
    )(places, *pieces)


def near(block, axis):
    return ring(block, axis, -1), ring(block, axis, 1)


def far(ahead, behind, axis):
    half = ahead.shape[0] // 2
    return ring(ahead[:half], axis, -1), ring(behind[half:], axis, 1)


def across_z(own, ahead, behind, far_low, far_high):
    return (
        ring(jnp.concatenate([own, ahead]), Z_RING, 1),
        ring(jnp.concatenate([behind, far_low, far_high]), Z_RING, -1),
    )


def put_weights(blocks, z_blocks, zl, y):
    rows, columns = blocks[0].shape
    unit = rows // 2
    pieces = [block.reshape(-1, unit, columns) for block in (*blocks, *z_blocks)]
    copies = [(0, 0, 2), (1, 0, 2), (2, 0, 2), (3, 0, 1), (4, 0, 1)]
    copies += [(5, 0, 2), (5, 2, 2), (6, 0, 2), (6, 2, 2)]
    step = [(y + q) % 4 * 2 for q in range(4)]
    mine, other = zl * 8, (1 - zl) * 8
    places = [mine + step[0], mine + step[1], mine + step[3], mine + step[2], mine + step[2] + 1]
    places += [other + step[0], other + step[1], other + step[3], other + step[2]]
    places = jnp.stack(places).astype(jnp.int32)
    return put_in_place(places, pieces, copies, 16).reshape(8 * rows, columns)


def halves_kernel(copies, places, *refs):
    pieces, out, sems = refs[:-2], refs[-2], refs[-1]
    width = pieces[0].shape[-1]
    running = [
        pltpu.make_async_copy(
            pieces[piece].at[unit],
            out.at[places[i], :, pl.ds(unit % 2 * width, width)],
            sems.at[i],
        )
        for i, (piece, unit) in enumerate(copies)
    ]
    for copy in running:
        copy.start()
    for copy in running:
        copy.wait()


def stack_halves(block):
    half = block.shape[1] // 2
    return jnp.concatenate([block[:, :half], block[:, half:]])


def both_parities(own):
    half = own.shape[0] // 2
    return ring(own[:half], Z_RING, 1), ring(own[half:], Z_RING, -1)


def pair_places(zl, y):
    steps = [(y + q) % 4 for q in (0, 1, 3, 2)]
    return [[zl * 4 + at, (1 - zl) * 4 + at] for at in steps]


def put_pairs(pair, near_pairs, far_pair, zl, y):
    rows, columns = far_pair[0].shape
    pieces = [block.reshape(-1, rows, columns) for block in (pair, *near_pairs, *far_pair)]
    copies = [(i, u, 1) for i in range(3) for u in range(2)] + [(3, 0, 1), (4, 0, 1)]
    places = jnp.stack(sum(pair_places(zl, y), [])).astype(jnp.int32)
    return put_in_place(places, pieces, copies, 8).reshape(8 * rows, columns)


def put_row_pairs(pair, near_pairs, far_pair, zl, y):
    rows, columns = far_pair[0].shape
    unit = rows // 2
    pieces = [block.reshape(-1, unit, columns) for block in (pair, *near_pairs, *far_pair)]
    copies = [(i, u) for i in range(3) for u in range(4)]
    copies += [(i, u) for i in (3, 4) for u in range(2)]
    places = sum([[at, at] for spots in pair_places(zl, y) for at in spots], [])
    places = jnp.stack(places).astype(jnp.int32)
    return pl.pallas_call(
        functools.partial(halves_kernel, copies),
        grid_spec=pltpu.PrefetchScalarGridSpec(
            num_scalar_prefetch=1,
            grid=(1,),
            in_specs=[pl.BlockSpec(piece.shape, lambda i, places: (0, 0, 0)) for piece in pieces],
            out_specs=pl.BlockSpec(memory_space=pl.ANY),
            scratch_shapes=[pltpu.SemaphoreType.DMA((len(copies),))],
        ),
        out_shape=jax.ShapeDtypeStruct((8, unit, 2 * columns), BF16),
        compiler_params=pltpu.CompilerParams(vmem_limit_bytes=32 * 1024 * 1024),
        cost_estimate=cost(1),
        name="put_rows",
    )(places, *pieces).reshape(8 * unit, 2 * columns)


def put_rows(blocks, blocks_two, group_places):
    rows, columns = blocks[0].shape
    unit = rows // 2
    pieces = [block.reshape(-1, unit, columns) for block in (*blocks, *blocks_two)]
    copies = [(0, 0, 2), (1, 0, 2), (2, 0, 2), (3, 0, 1), (4, 0, 1)]
    copies += [(5, 0, 2), (6, 0, 2), (6, 2, 2), (7, 0, 2)]
    spots = [2 * group_places[i] for i in (0, 1, 3, 2, 2, 4, 5, 7, 6)]
    spots[4] = spots[4] + 1
    return put_in_place(jnp.stack(spots), pieces, copies, 2 * GROUP).reshape(
        GROUP * rows, columns
    )


def swap_blocks(own, ahead, behind, far_low, far_high):
    return (
        ring(own, "core", 1),
        ring(jnp.concatenate([ahead, behind]), "core", 1),
        ring(jnp.concatenate([far_low, far_high]), "core", 1),
    )


def scatter_z(pairs):
    return ring(pairs[0], Z_RING, 1), ring(pairs[1], Z_RING, -1)


def chunk_for_y(own, arrived, y, step):
    at = (y + step) % 4
    more = jnp.where(
        at < 2,
        lax.dynamic_index_in_dim(arrived[0], at & 1, 0, keepdims=False),
        lax.dynamic_index_in_dim(arrived[1], at & 1, 0, keepdims=False),
    )
    here = lax.dynamic_index_in_dim(own, at, 0, keepdims=False)
    return here.astype(F32) + more.astype(F32)


def chunks_for_y(own, arrived, y):
    return [chunk_for_y(own, arrived, y, 0)] + [
        chunk_for_y(own, arrived, y, step).astype(BF16) for step in (1, 2, 3)
    ]


def far_along_y(own, arrived, y):
    block = chunk_for_y(own, arrived, y, 2).astype(BF16)
    half = block.shape[0] // 2
    return ring(block[:half], "y", 1), ring(block[half:], "y", -1)


def near_along_y(own, arrived, first, y):
    ahead, behind = chunk_for_y(own, arrived, y, 1), chunk_for_y(own, arrived, y, 3)
    half = ahead.shape[0] // 2
    ahead = jnp.concatenate([ahead[:half] + first[0].astype(F32), ahead[half:]])
    behind = jnp.concatenate([behind[:half], behind[half:] + first[1].astype(F32)])
    return (
        chunk_for_y(own, arrived, y, 0),
        ring(ahead.astype(BF16), "y", 1),
        ring(behind.astype(BF16), "y", -1),
    )


def send_along_y(chunks):
    return [chunks[0]] + [ring(chunks[step], "y", step) for step in (1, 2, 3)]


def scatter_y(own, arrived, y):
    return send_along_y(chunks_for_y(own, arrived, y))


def scatter_zh(parts):
    total = add_up(parts).astype(BF16)
    return total, ring(total, "zh", 1)


def both_halves(pair):
    return add_up(pair).astype(BF16)


def rows_to_core(partial, core):
    partial = partial.astype(BF16).reshape(4, 2, TOK, D)

    def of_core(at):
        return lax.dynamic_index_in_dim(partial, at, 1, keepdims=False)

    return of_core(core), ring(of_core(1 - core), "core", 1)


def rows_along_x(total, x):
    def chunk(step):
        return lax.dynamic_index_in_dim(total, (x + step) % 4, 0, keepdims=False)

    far = ring(chunk(2).astype(BF16), "x", 2)
    ahead = ring(chunk(1).astype(BF16), "x", 1)
    behind = ring(chunk(3).astype(BF16), "x", -1)
    return chunk(0), ahead, behind, far


def exchange_x(blocks, x):
    def chunk(step):
        return lax.dynamic_index_in_dim(blocks, (x + step) % 4, 0, keepdims=False)

    return [chunk(0)] + [ring(chunk(step), "x", step) for step in (1, 2, 3)]


def put_exchanged(parts, others, x, core):
    rows = parts[0].shape[1]
    pieces = [*parts, others]
    copies, places = [], []
    for r in range(4):
        at = (x - r) % 4 * 2
        for tokens in range(2):
            copies += [(r, tokens, 1), (4, 2 * r + tokens, 1)]
            places += [tokens * GROUP + at + core, tokens * GROUP + at + 1 - core]
    places = jnp.stack(places).astype(jnp.int32)
    return put_in_place(places, pieces, copies, 2 * GROUP).reshape(2, GROUP, rows, TOK)


def far_rows_along_x(total, x):
    block = lax.dynamic_index_in_dim(total, (x + 2) % 4, 0, keepdims=False).astype(BF16)
    half = block.shape[0] // 2
    return ring(block[:half], "x", 1), ring(block[half:], "x", -1)


def near_rows_along_x(total, first, x):
    def chunk(step):
        return lax.dynamic_index_in_dim(total, (x + step) % 4, 0, keepdims=False)

    ahead, behind = chunk(1), chunk(3)
    half = ahead.shape[0] // 2
    ahead = jnp.concatenate([ahead[:half] + first[0].astype(F32), ahead[half:]])
    behind = jnp.concatenate([behind[:half], behind[half:] + first[1].astype(F32)])
    return chunk(0), ring(ahead.astype(BF16), "x", 1), ring(behind.astype(BF16), "x", -1)


def add_up(parts):
    return sum(part.astype(F32) for part in parts)


def rail_of(block):
    return [block, ring(block, "x", -1), ring(block, "x", 2), ring(block, "x", 1)]


def with_other_core(rail):
    return rail + [ring(part, "core", 1) for part in rail]


def swap_roles(values):
    return lax.ppermute(
        values,
        ("zl", "y", "x", "core"),
        [(a * GROUP + b, b * GROUP + a) for a in range(GROUP) for b in range(GROUP)],
    )


def after(values, *others):
    return lax.optimization_barrier((values, *others))[0]


def join(*groups):
    return lax.optimization_barrier(groups)


def heads_side_by_side(block):
    return jnp.concatenate(
        [block[i * HEAD_DIM : (i + 1) * HEAD_DIM] for i in range(HEADS_OWN)], axis=1
    )


def heads_stacked(block):
    return jnp.concatenate(
        [block[:, i * TOK : (i + 1) * TOK] for i in range(HEADS_OWN)], axis=0
    )


def block_bounds(meta, j):
    half_at, place = meta[0], j
    first = jnp.where(half_at == 1, 0, HALF // KEY_CHUNK)
    last = HALF // KEY_CHUNK + place * TOK // KEY_CHUNK
    every = (half_at == 1) & (place == GROUP - 1)
    return first, last, every


def allowed_keys(meta, j, chunk):
    half_at, head_end, place = meta[0], meta[1], j
    shape = (KEY_CHUNK, ROWS_Q)
    column = lax.broadcasted_iota(jnp.int32, (1, ROWS_Q), 1)
    query = half_at * HALF + place * TOK + (column & (TOK - 1))
    start = jnp.where(
        query < head_end,
        0,
        jnp.where(query < head_end + MIDDLE, head_end, head_end + MIDDLE),
    )
    key = (
        lax.broadcasted_iota(jnp.int32, shape, 0)
        + chunk * KEY_CHUNK
        + (half_at - 1) * HALF
    )
    return (key <= query) & (key >= start)


def dot_kn(left, right):
    return jnp.dot(left, right, preferred_element_type=F32)


def dot_nt(left, right):
    return lax.dot_general(
        left, right, (((1,), (1,)), ((), ())), preferred_element_type=F32
    )


def forward_kernel(
    meta, q_ref, kt_ref, vt_ref, out_ref, mixed_ref, lse_ref, k_ref, v_ref, top_ref, acc_ref
):
    j = pl.program_id(0)

    @pl.when(j == 0)
    def _():
        k_ref[...] = kt_ref[...].astype(F32).T.astype(BF16)
        row = lax.broadcasted_iota(jnp.int32, (V_ROWS - HEAD_DIM, 2 * HALF), 0)
        v_ref[:HEAD_DIM, :] = vt_ref[...]
        v_ref[HEAD_DIM:, :] = jnp.where(row == 0, 1.0, 0.0).astype(BF16)

    query = heads_side_by_side(q_ref[...])
    first, last, every = block_bounds(meta, j)
    top_ref[...] = jnp.full_like(top_ref, NEG_LARGE)
    acc_ref[...] = jnp.zeros_like(acc_ref)

    def step(chunk, masked):
        at = pl.multiple_of(chunk * KEY_CHUNK, KEY_CHUNK)
        scores = dot_kn(k_ref[pl.ds(at, KEY_CHUNK), :], query)
        if masked:
            scores = jnp.where(allowed_keys(meta, j, chunk), scores, NEG_LARGE)
        old = top_ref[...]
        new = jnp.maximum(old, jnp.max(scores, axis=0, keepdims=True))
        weights = jnp.exp(scores - new).astype(BF16)
        acc_ref[...] = acc_ref[...] * jnp.exp(old - new) + dot_kn(
            v_ref[:, pl.ds(at, KEY_CHUNK)], weights
        )
        top_ref[...] = new

    def body(chunk, carry):
        masked = every | (chunk == first) | (chunk == last)

        @pl.when(masked)
        def _():
            step(chunk, True)

        @pl.when(jnp.logical_not(masked))
        def _():
            step(chunk, False)

        return carry

    lax.fori_loop(first, last + 1, body, 0)
    total = acc_ref[HEAD_DIM : HEAD_DIM + 1, :]
    attended = heads_stacked(acc_ref[:HEAD_DIM, :] / total)
    out_ref[0] = attended
    mixed_ref[0] = attended.astype(BF16)
    lse_ref[...] = jnp.broadcast_to(top_ref[...] + jnp.log(total), lse_ref.shape)


def backward_kernel(
    meta,
    q_ref,
    g_ref,
    o_ref,
    lse_ref,
    kt_ref,
    vt_ref,
    *rest,
    begin,
):
    dq_ref, dk_ref, dv_ref, k_ref, v_ref, acc_ref = rest[-6:]
    j = pl.program_id(0) + begin

    @pl.when(pl.program_id(0) == 0)
    def _():
        k_ref[...] = kt_ref[...].astype(F32).T.astype(BF16)
        v_ref[...] = vt_ref[...].astype(F32).T.astype(BF16)
        if begin:
            dk_ref[...] = rest[0][...]
            dv_ref[...] = rest[1][...]
        else:
            dk_ref[...] = jnp.zeros_like(dk_ref)
            dv_ref[...] = jnp.zeros_like(dv_ref)

    query = heads_side_by_side(q_ref[...])
    grad = heads_side_by_side(g_ref[0])
    mixed = heads_side_by_side(o_ref[0])
    delta = jnp.sum(grad.astype(F32) * mixed, axis=0, keepdims=True)
    lse = lse_ref[0:1, :]
    first, last, every = block_bounds(meta, j)
    acc_ref[...] = jnp.zeros_like(acc_ref)

    def step(chunk, masked):
        at = pl.multiple_of(chunk * KEY_CHUNK, KEY_CHUNK)
        rows = pl.ds(at, KEY_CHUNK)
        scores = dot_kn(k_ref[rows, :], query)
        grad_probs = dot_kn(v_ref[rows, :], grad)
        if masked:
            scores = jnp.where(allowed_keys(meta, j, chunk), scores, NEG_LARGE)
        probs = jnp.exp(scores - lse)
        grad_scores = (probs * (grad_probs - delta)).astype(BF16)
        acc_ref[...] += dot_kn(kt_ref[:, rows], grad_scores)
        dk_ref[:, rows] += dot_nt(query, grad_scores)
        dv_ref[:, rows] += dot_nt(grad, probs.astype(BF16))

    def body(chunk, carry):
        masked = every | (chunk == first) | (chunk == last)

        @pl.when(masked)
        def _():
            step(chunk, True)

        @pl.when(jnp.logical_not(masked))
        def _():
            step(chunk, False)

        return carry

    lax.fori_loop(first, last + 1, body, 0)
    dq_ref[0] = heads_stacked(acc_ref[...] * (1.0 / math.sqrt(HEAD_DIM)))


def whole(shape):
    return pl.BlockSpec(shape, lambda j, meta: (0,) * len(shape))


def token_block(rows):
    return pl.BlockSpec((rows, TOK), lambda j, meta: (0, j))


V_ROWS = 80
LSE_ROWS = 8


def attend(meta, query_t, keys_t, values_t):
    return pl.pallas_call(
        forward_kernel,
        grid_spec=pltpu.PrefetchScalarGridSpec(
            num_scalar_prefetch=1,
            grid=(GROUP,),
            in_specs=[
                token_block(Q_OWN),
                whole((HEAD_DIM, 2 * HALF)),
                whole((HEAD_DIM, 2 * HALF)),
            ],
            out_specs=[
                pl.BlockSpec((1, Q_OWN, TOK), lambda j, meta: (j, 0, 0)),
                pl.BlockSpec((1, Q_OWN, TOK), lambda j, meta: (j, 0, 0)),
                pl.BlockSpec((LSE_ROWS, ROWS_Q), lambda j, meta: (j, 0)),
            ],
            scratch_shapes=[
                pltpu.VMEM((2 * HALF, HEAD_DIM), BF16),
                pltpu.VMEM((V_ROWS, 2 * HALF), BF16),
                pltpu.VMEM((1, ROWS_Q), F32),
                pltpu.VMEM((V_ROWS, ROWS_Q), F32),
            ],
        ),
        out_shape=[
            jax.ShapeDtypeStruct((GROUP, Q_OWN, TOK), F32),
            jax.ShapeDtypeStruct((GROUP, Q_OWN, TOK), BF16),
            jax.ShapeDtypeStruct((GROUP * LSE_ROWS, ROWS_Q), F32),
        ],
        compiler_params=pltpu.CompilerParams(vmem_limit_bytes=32 * 1024 * 1024),
        cost_estimate=cost(1),
        name="attend",
    )(meta, query_t, keys_t, values_t)


def attend_back(meta, begin, end, query_t, grad_t, attn_t, lse, keys_t, values_t, *sums):
    block = pl.BlockSpec((1, Q_OWN, TOK), lambda j, meta: (j + begin, 0, 0))
    return pl.pallas_call(
        functools.partial(backward_kernel, begin=begin),
        grid_spec=pltpu.PrefetchScalarGridSpec(
            num_scalar_prefetch=1,
            grid=(end - begin,),
            in_specs=[
                pl.BlockSpec((Q_OWN, TOK), lambda j, meta: (0, j + begin)),
                block,
                block,
                pl.BlockSpec((LSE_ROWS, ROWS_Q), lambda j, meta: (j + begin, 0)),
            ]
            + [whole((HEAD_DIM, 2 * HALF))] * (2 + len(sums)),
            out_specs=[
                pl.BlockSpec((1, Q_OWN, TOK), lambda j, meta: (j, 0, 0)),
                whole((HEAD_DIM, 2 * HALF)),
                whole((HEAD_DIM, 2 * HALF)),
            ],
            scratch_shapes=[
                pltpu.VMEM((2 * HALF, HEAD_DIM), BF16),
                pltpu.VMEM((2 * HALF, HEAD_DIM), BF16),
                pltpu.VMEM((HEAD_DIM, ROWS_Q), F32),
            ],
        ),
        out_shape=[
            jax.ShapeDtypeStruct((end - begin, Q_OWN, TOK), F32),
            jax.ShapeDtypeStruct((HEAD_DIM, 2 * HALF), F32),
            jax.ShapeDtypeStruct((HEAD_DIM, 2 * HALF), F32),
        ],
        compiler_params=pltpu.CompilerParams(vmem_limit_bytes=32 * 1024 * 1024),
        cost_estimate=cost(1),
        name="attend_back",
    )(meta, query_t, grad_t, attn_t, lse, keys_t, values_t, *sums)


def norm_kernel(places, *refs):
    (own, ahead, behind, low, high, own_two, near_two, far_two, weights) = refs[:9]
    normed_out, gains_out, gains = refs[9:]
    i = pl.program_id(0)

    @pl.when(i == 0)
    def _():
        gains[...] = weights[...].astype(F32).T[HEAD_DIM : HEAD_DIM + 8, :]
        gains_out[...] = gains[...]

    def norm(block, start, size, to):
        values = block[start : start + size, :].astype(F32)
        scale = lax.rsqrt(jnp.mean(values * values, axis=-1, keepdims=True) + EPSILON)
        normed_out[to : to + size, :] = (values * scale * gains[0:1, :]).astype(BF16)

    sources = [
        [(own, 0)],
        [(ahead, 0)],
        [(low, 0), (high, 0)],
        [(behind, 0)],
        [(own_two, 0)],
        [(near_two, 0)],
        [(far_two, 0)],
        [(near_two, TOK)],
    ]
    for at, parts in enumerate(sources):

        @pl.when(i == at)
        def _(parts=parts):
            size = TOK // len(parts)
            for k, (block, start) in enumerate(parts):
                norm(block, start, size, k * size)


def gather_norm(places, pieces, early_all):
    rows = [pl.BlockSpec(piece.shape, lambda i, places: (0, 0)) for piece in pieces]
    placed = pl.BlockSpec((TOK, D), lambda i, places: (places[i], 0))
    return pl.pallas_call(
        norm_kernel,
        grid_spec=pltpu.PrefetchScalarGridSpec(
            num_scalar_prefetch=1,
            grid=(GROUP,),
            in_specs=rows + [pl.BlockSpec((D, 128), lambda i, places: (0, 2))],
            out_specs=[
                placed,
                pl.BlockSpec((8, D), lambda i, places: (0, 0)),
            ],
            scratch_shapes=[pltpu.VMEM((8, D), F32)],
        ),
        out_shape=[
            jax.ShapeDtypeStruct((HALF, D), BF16),
            jax.ShapeDtypeStruct((8, D), F32),
        ],
        compiler_params=pltpu.CompilerParams(vmem_limit_bytes=32 * 1024 * 1024),
        cost_estimate=cost(1),
        name="gather_norm",
    )(places, *pieces, early_all)


def take_kernel(own, gate, up, out):
    for at in range(GROUP):

        @pl.when(own[0] == at)
        def _():
            parts = []
            for ref in (gate, up):
                for block in range(GROUP):
                    start = block * FF_OWN + at * SUB
                    low = start // 128 * 128
                    window = ref[:, low : low + 256].astype(F32)
                    parts.append(window[:, start - low : start - low + SUB])
            out[...] = jnp.concatenate(parts, axis=1).astype(BF16)


def take_columns(own, gate, up):
    rows = 64
    return pl.pallas_call(
        take_kernel,
        grid_spec=pltpu.PrefetchScalarGridSpec(
            num_scalar_prefetch=1,
            grid=(CHUNK // rows,),
            in_specs=[pl.BlockSpec((rows, FF), lambda i, own: (i, 0))] * 2,
            out_specs=pl.BlockSpec((rows, 2 * FF_OWN), lambda i, own: (i, 0)),
        ),
        out_shape=jax.ShapeDtypeStruct((CHUNK, 2 * FF_OWN), BF16),
        compiler_params=pltpu.CompilerParams(vmem_limit_bytes=32 * 1024 * 1024),
        cost_estimate=cost(1),
        name="take_columns",
    )(own, gate, up)


def gate_up_kernel(pieces, w_gate, w_up, gate, up, products):
    total = 0.0
    for which, (weight, out) in enumerate(((w_gate, gate), (w_up, up))):
        parts = []
        for block in range(GROUP):
            start = which * FF_OWN + block * SUB
            low = start // 128 * 128
            size = min(256, 2 * FF_OWN - low)
            for at in range(GROUP):
                window = pieces[at, :, low : low + size].astype(F32)
                parts.append(window[:, start - low : start - low + SUB])
        values = jnp.concatenate(parts, axis=1)
        out[...] = values
        total = total + jnp.sum(values * weight[...].astype(F32), axis=1, keepdims=True)
    products[...] = jnp.broadcast_to(total, products.shape)


def put_gate_up(pieces, w_gate, w_up):
    rows = 64
    row_block = pl.BlockSpec((rows, FF), lambda i: (i, 0))
    return pl.pallas_call(
        gate_up_kernel,
        grid=(CHUNK // rows,),
        in_specs=[
            pl.BlockSpec((GROUP, rows, 2 * FF_OWN), lambda i: (0, i, 0)),
            row_block,
            row_block,
        ],
        out_specs=[row_block, row_block, pl.BlockSpec((rows, 128), lambda i: (i, 0))],
        out_shape=[
            jax.ShapeDtypeStruct((CHUNK, FF), F32),
            jax.ShapeDtypeStruct((CHUNK, FF), F32),
            jax.ShapeDtypeStruct((CHUNK, 128), F32),
        ],
        compiler_params=pltpu.CompilerParams(vmem_limit_bytes=48 * 1024 * 1024),
        cost_estimate=cost(1),
        name="gate_up",
    )(pieces.reshape(GROUP, CHUNK, 2 * FF_OWN), w_gate, w_up)


def down_out_kernel(rows, down, out):
    values = rows[...].astype(F32)
    down[...] = values[:SUB]
    out[...] = values[SUB:]


def split_down_out(rows):
    return pl.pallas_call(
        down_out_kernel,
        grid=(GROUP,),
        in_specs=[pl.BlockSpec((SUB + OUT_SUB, D), lambda i: (i, 0))],
        out_specs=[
            pl.BlockSpec((SUB, D), lambda i: (i, 0)),
            pl.BlockSpec((OUT_SUB, D), lambda i: (i, 0)),
        ],
        out_shape=[
            jax.ShapeDtypeStruct((FF_OWN, D), F32),
            jax.ShapeDtypeStruct((Q_OWN, D), F32),
        ],
        compiler_params=pltpu.CompilerParams(vmem_limit_bytes=32 * 1024 * 1024),
        cost_estimate=cost(1),
        name="down_out",
    )(rows)


def qkv_kernel(places, *refs):
    pieces, weights, outs, products, stack = refs[:8], refs[8:11], refs[11:14], *refs[14:]
    query, key, value = outs
    for i, piece in enumerate(pieces):
        stack[places[i]] = piece[...]
    for at in range(GROUP):
        values = stack[at].astype(F32)
        query[:, at * Q_OWN : (at + 1) * Q_OWN] = values[:, :Q_OWN]
        head = key if at % 2 == 0 else value
        place = (at // 2) * HEAD_DIM
        head[:, place : place + HEAD_DIM] = values[:, Q_OWN : Q_OWN + HEAD_DIM]
    total = sum(
        jnp.sum(out[...] * weight[...].astype(F32), axis=1, keepdims=True)
        for out, weight in zip(outs, weights, strict=True)
    )
    products[...] = jnp.broadcast_to(total, (CHUNK, 128)).T[:8]


def assemble(kernel, places, pieces, rows, weights, shapes):
    count, width = pieces[0].shape
    return pl.pallas_call(
        kernel,
        grid_spec=pltpu.PrefetchScalarGridSpec(
            num_scalar_prefetch=1,
            grid=(count // rows,),
            in_specs=[pl.BlockSpec((rows, width), lambda i, places: (i, 0))] * 8
            + [pl.BlockSpec((rows, w.shape[1]), lambda i, places: (i, 0)) for w in weights],
            out_specs=[
                pl.BlockSpec((block, columns), lambda i, places: (i, 0))
                for _, block, columns in shapes
            ],
            scratch_shapes=[pltpu.VMEM((GROUP, rows, width), BF16)],
        ),
        out_shape=[jax.ShapeDtypeStruct((whole, columns), F32) for whole, _, columns in shapes],
        compiler_params=pltpu.CompilerParams(vmem_limit_bytes=48 * 1024 * 1024),
        cost_estimate=cost(1),
        name=kernel.__name__.removesuffix("_kernel"),
    )(places, *pieces, *weights)


def rms_scale(values):
    return lax.rsqrt(jnp.mean(values * values, axis=-1, keepdims=True) + EPSILON)


def rotate_t(values, cosine, sine_table):
    half = HEAD_DIM // 2
    first, second = values[:, :half], values[:, half:]
    return jnp.concatenate(
        [first * cosine - second * sine_table, second * cosine + first * sine_table], axis=1
    )


def norm_back(grad_normed, values, scale_rows, gain_full):
    unit_rows = values * scale_rows
    grad_unit = grad_normed * gain_full
    return scale_rows * (
        grad_unit - unit_rows * jnp.mean(grad_unit * unit_rows, axis=-1, keepdims=True)
    )


def contract(form, left, right):
    return jnp.einsum(form, left, right, preferred_element_type=F32)


def shards(
    inputs,
    positions,
    cotangent,
    w_query,
    w_key,
    w_value,
    w_out,
    w_gate,
    w_up,
    w_down,
    gain_attn,
    gain_mlp,
):
    zl, y, zh, x, core = (lax.axis_index(axis) for axis in AXES)
    xc = x * 2 + core
    group = ("x", "core")

    def gather_rows(rows):
        return lax.all_gather(rows, group, axis=0, tiled=True)

    inputs_near = near(inputs, "x")
    inputs_two = ring(inputs, "core", 1)

    index_here = (zh * GROUP + xc) * TOK + jnp.arange(TOK, dtype=jnp.int32)
    head_end = jnp.where(
        (zh == 0) & (xc == 0),
        jnp.sum((positions == index_here).astype(jnp.int32)),
        index_here[0] - positions[0],
    )
    meta = jnp.stack([zh, head_end]).astype(jnp.int32)
    rail = [((x + r) % 4) * 2 for r in range(4)]
    group_places = jnp.stack(
        [at + core for at in rail] + [at + 1 - core for at in rail]
    ).astype(jnp.int32)
    def columns(weight, width):
        return lax.dynamic_slice_in_dim(weight, xc * width, width, axis=1)

    kv_here = jnp.where(core == 0, w_key, w_value)
    kv_here = lax.dynamic_slice_in_dim(kv_here, x * HEAD_DIM, HEAD_DIM, axis=1)
    early = jnp.concatenate(
        [
            columns(w_query, Q_OWN),
            kv_here,
            gain_attn[:, None],
            gain_mlp[:, None],
            jnp.zeros((CHUNK, 62), BF16),
        ],
        axis=1,
    )
    early_near = near(early, "y")
    gate_up_here = take_columns(xc[None].astype(jnp.int32), w_gate, w_up)
    half_width = D // 2
    out_here = lax.dynamic_slice_in_dim(w_out, core * half_width, half_width, axis=1)
    down_here = stack_halves(lax.dynamic_slice_in_dim(w_down, xc * SUB, SUB, axis=0))
    early_blocks = (early, *early_near, *far(*early_near, "y"))
    early_blocks, inputs_near, out_here = join(early_blocks, inputs_near, out_here)
    early_z = across_z(*early_blocks)
    inputs_far = far(*inputs_near, "x")
    out_near = near(out_here, "y")
    early_z, inputs_far, inputs_two, gate_up_here = join(
        early_z, inputs_far, inputs_two, gate_up_here
    )
    inputs_rest = (
        ring(jnp.concatenate(inputs_near), "core", 1),
        ring(jnp.concatenate(inputs_far), "core", 1),
    )
    full_qkv_gains = put_weights(early_blocks, early_z, zl, y)
    full_qkv_gains, inputs_rest, out_near = join(full_qkv_gains, inputs_rest, out_near)
    out_far = far(*out_near, "y")
    gate_up_other = both_parities(gate_up_here)
    normed, gains = gather_norm(
        group_places,
        [inputs, *inputs_near, *inputs_far, inputs_two, *inputs_rest],
        full_qkv_gains,
    )
    full_qkv = full_qkv_gains[:, : Q_OWN + HEAD_DIM]
    full_gain_attn, full_gain_mlp = gains[0], gains[1]

    index_all = zh * HALF + jnp.arange(HALF, dtype=jnp.int32)
    doc_start = jnp.where(
        index_all < head_end,
        0,
        jnp.where(index_all < head_end + MIDDLE, head_end, head_end + MIDDLE),
    )
    frequency = THETA ** (-(jnp.arange(HEAD_DIM // 2, dtype=F32) * 2.0 / HEAD_DIM))
    angles = frequency[:, None] * (index_all - doc_start).astype(F32)[None, :]
    cosine, sine_table = jnp.cos(angles), jnp.sin(angles)
    is_key = core == 0
    cosine_kv = jnp.where(is_key, cosine, 1.0)
    sine_kv = jnp.where(is_key, sine_table, 0.0)

    raw_t = contract("dn,td->nt", full_qkv, normed)
    query_t = (
        rotate_t(raw_t[:Q_OWN].reshape(HEADS_OWN, HEAD_DIM, HALF), cosine, sine_table)
        .reshape(Q_OWN, HALF)
        .astype(BF16)
        * (1.0 / math.sqrt(HEAD_DIM))
    ).astype(BF16)
    kv_t = rotate_t(raw_t[Q_OWN:][None], cosine_kv, sine_kv)[0].astype(BF16)
    kv_other = ring(kv_t, "core", 1)
    kv_prev = lax.ppermute(kv_t, "zh", [(0, 1)])
    kv_prev_other = lax.ppermute(kv_t, ("zh", "core"), [(0, 3), (1, 2)])
    kv_t, kv_other, kv_prev, kv_prev_other, query_t, gate_up_here, gate_up_other, out_far = join(
        kv_t, kv_other, kv_prev, kv_prev_other, query_t, gate_up_here, gate_up_other, out_far
    )
    mine = jnp.concatenate([kv_prev, kv_t], axis=1)
    theirs = jnp.concatenate([kv_prev_other, kv_other], axis=1)
    keys_t = jnp.where(is_key, mine, theirs)
    values_t = jnp.where(is_key, theirs, mine)
    out_blocks = (out_here, *out_near, *out_far)
    out_z = across_z(*out_blocks)
    gate_up_pair = jnp.concatenate([gate_up_here, *gate_up_other])
    gate_up_near = near(gate_up_pair, "y")
    attended = attend(meta, query_t, keys_t, values_t)
    (attn_t, mixed_t, lse), out_z, gate_up_near = join(attended, out_z, gate_up_near)
    mixed_parts = exchange_x(mixed_t.reshape(4, 2, Q_OWN, TOK), x)
    gate_up_far = far(*gate_up_near, "y")
    out_half = put_weights(out_blocks, out_z, zl, y)
    down_other = both_parities(down_here)
    mixed_parts, out_half, cotangent_here = join(mixed_parts, out_half, cotangent)
    mixed_others = ring(jnp.concatenate(mixed_parts), "core", 1)
    cotangent_near = near(cotangent_here, "x")
    mixed_others, mixed_parts = join(mixed_others, mixed_parts)
    mixed_both = put_exchanged(mixed_parts, mixed_others, x, core)

    def of_core(values, at):
        return lax.dynamic_index_in_dim(values, at, 0, keepdims=False)

    out_rows = contract("ckt,kd->ctd", mixed_both.reshape(2, D, TOK), out_half).astype(BF16)
    out_mine = of_core(out_rows, core)
    out_theirs = ring(of_core(out_rows, 1 - core), "core", 1)
    out_theirs, gate_up_far, down_other, cotangent_near = join(
        out_theirs, gate_up_far, down_other, cotangent_near
    )
    down_pair = jnp.concatenate([down_here, *down_other])
    down_near = near(down_pair, "y")
    tokens_here = inputs.astype(F32)
    residual = tokens_here + jnp.concatenate(
        [
            jnp.where(core == 0, out_mine, out_theirs),
            jnp.where(core == 0, out_theirs, out_mine),
        ],
        axis=1,
    ).astype(F32)
    scale_mlp = rms_scale(residual)
    normed_rows = (residual * scale_mlp * full_gain_mlp).astype(BF16)
    normed_mlp = gather_rows(normed_rows)
    gate_up_all = put_pairs(gate_up_pair, gate_up_near, gate_up_far, zl, y)
    cotangent_far = far(*cotangent_near, "x")
    cotangent_far, down_near, gate_up_all = join(cotangent_far, down_near, gate_up_all)
    cotangent_blocks = (cotangent_here, *cotangent_near, *cotangent_far)
    cotangent_two = swap_blocks(*cotangent_blocks)
    down_far = far(*down_near, "y")
    normed_mlp, cotangent_two = join(normed_mlp, cotangent_two)

    gate_up = contract("td,df->tf", normed_mlp, gate_up_all)
    cotangent_all = put_rows(cotangent_blocks, cotangent_two, group_places)
    gate_up, down_far, cotangent_all = join(gate_up, down_far, cotangent_all)
    full_down = put_row_pairs(down_pair, down_near, down_far, zl, y)
    grad_hidden = contract("td,fd->tf", cotangent_all, full_down)
    gate, upward = gate_up[:, :FF_OWN], gate_up[:, FF_OWN:]
    sigmoid_gate = jax.nn.sigmoid(gate)
    silu_gate = gate * sigmoid_gate
    hidden = (silu_gate * upward).astype(BF16)
    grad_acts = jnp.concatenate(
        [
            (grad_hidden * upward * sigmoid_gate * (1.0 + gate * (1.0 - sigmoid_gate))).astype(BF16),
            (grad_hidden * silu_gate).astype(BF16),
        ],
        axis=1,
    )
    part_output = contract("tf,fd->td", hidden, full_down).astype(BF16)
    grad_acts, part_output = join(grad_acts, part_output)
    output_rows = lax.psum_scatter(part_output, group, scatter_dimension=0, tiled=True)
    back_rows = rows_to_core(contract("tf,df->td", grad_acts, gate_up_all), core)

    def columns_at(values, start, count):
        return lax.dynamic_slice_in_dim(values, start * CHUNK, count * CHUNK, axis=1)

    other = (1 - zl) * 4

    def gate_up_product(start, count):
        rows = contract("td,tf->df", columns_at(normed_mlp, start, count), grad_acts)
        return rows.astype(BF16).reshape(count, CHUNK, 2 * FF_OWN)

    gate_up_theirs = gate_up_product(other, 4)
    back_total = back_rows[0].astype(F32) + back_rows[1].astype(F32)
    back_total, gate_up_pairs, hidden, normed_mlp, grad_acts = join(
        back_total, (gate_up_theirs[:2], gate_up_theirs[2:]), hidden, normed_mlp, grad_acts
    )
    back_rows = rows_along_x(back_total, x)
    gate_up_z = scatter_z(gate_up_pairs)
    gate_up_mine = gate_up_product(zl * 4, 4)
    part_down = contract("tf,td->fd", hidden, cotangent_all).astype(BF16)
    part_down = part_down.reshape(8, SUB, D)
    back_rows, gate_up_z, gate_up_mine, part_down, output_rows = join(
        back_rows, gate_up_z, gate_up_mine, part_down, output_rows
    )
    gate_up_far = far_along_y(gate_up_mine, gate_up_z, y)
    grad_normed_mlp = add_up(back_rows)
    grad_residual = cotangent.astype(F32) + norm_back(
        grad_normed_mlp, residual, scale_mlp, full_gain_mlp
    )
    grad_here = grad_residual.astype(BF16)
    grad_theirs = ring(grad_here, "core", 1)
    grad_theirs, grad_here = join(grad_theirs, grad_here)
    grad_both = jnp.stack(
        [jnp.where(core == 0, grad_here, grad_theirs), jnp.where(core == 0, grad_theirs, grad_here)]
    )
    grad_both = jnp.where(core == 0, grad_both[..., :half_width], grad_both[..., half_width:])
    grad_partial = contract("kd,ctd->kct", out_half, grad_both).reshape(4, 2, Q_OWN, 2, TOK)

    def heads_of(at):
        return lax.dynamic_index_in_dim(grad_partial, at, 1, keepdims=False)

    grad_arrived = ring(heads_of(1 - core).astype(BF16), "core", 1)
    grad_arrived, gate_up_far = join(grad_arrived, gate_up_far)
    grad_heads = (heads_of(core) + grad_arrived.astype(F32)).astype(BF16)
    grad_parts = exchange_x(grad_heads.transpose(0, 2, 1, 3), x)
    grad_attn_out = gather_rows(grad_here)
    (grad_parts,) = join(grad_parts)
    gate_up_y = near_along_y(gate_up_mine, gate_up_z, gate_up_far, y)
    places = jnp.stack([(x - r) % 4 * 2 for r in range(4)]).astype(jnp.int32)
    grad_mixed_t = put_in_place(places, grad_parts, [(r, 0, 2) for r in range(4)], GROUP)
    back_args = (query_t, grad_mixed_t, attn_t, lse, keys_t, values_t)
    attended = attend_back(meta, 0, 4, *back_args)
    (query_0, *key_sums), gate_up_y = join(attended, gate_up_y)
    gate_up_zh = scatter_zh(gate_up_y)
    attended = attend_back(meta, 4, 6, *back_args, *key_sums)
    (query_1, *key_sums), gate_up_zh, grad_attn_out = join(attended, gate_up_zh, grad_attn_out)
    gate_up_grads = gather_rows(both_halves(gate_up_zh))
    part_out = contract(
        "bkt,btd->kd", mixed_t, grad_attn_out.reshape(GROUP, TOK, D)
    ).astype(BF16)
    part_down_out = jnp.concatenate([part_down, part_out.reshape(8, OUT_SUB, D)], axis=1)

    def chunks(start, count):
        return lax.dynamic_slice_in_dim(part_down_out, start, count, axis=0)

    down_out_pairs = (chunks(other, 2), chunks(other + 2, 2))
    down_out_pairs, key_sums = join(down_out_pairs, key_sums)
    down_out_z = scatter_z(down_out_pairs)
    attended = attend_back(meta, 6, 8, *back_args, *key_sums)
    (query_2, grad_keys_t, grad_values_t), down_out_z = join(attended, down_out_z)
    grad_query_t = jnp.concatenate([query_0, query_1, query_2])

    kept = jnp.where(is_key, grad_keys_t, grad_values_t)
    given = jnp.where(is_key, grad_values_t, grad_keys_t)
    arrived = ring(given.astype(BF16), "core", 1)
    arrived, kept, grad_query_t = join(arrived, kept, grad_query_t)
    grad_kv = kept + arrived.astype(F32)
    from_next = lax.ppermute(grad_kv[:, :HALF].astype(BF16), "zh", [(1, 0)])
    from_next, grad_kv, grad_query_t = join(from_next, grad_kv, grad_query_t)
    down_out_y = scatter_y(chunks(zl * 4, 4), down_out_z, y)
    grad_kv_t = grad_kv[:, HALF:] + from_next.astype(F32)

    def by_block(table):
        return table.reshape(-1, GROUP, TOK).transpose(1, 0, 2)

    half_head = HEAD_DIM // 2
    cosine_b, sine_b = by_block(cosine)[:, None], by_block(sine_table)[:, None]
    first = grad_query_t.reshape(GROUP, HEADS_OWN, HEAD_DIM, TOK)[:, :, :half_head]
    second = grad_query_t.reshape(GROUP, HEADS_OWN, HEAD_DIM, TOK)[:, :, half_head:]
    turned = jnp.concatenate(
        [first * cosine_b + second * sine_b, second * cosine_b - first * sine_b], axis=2
    ).reshape(GROUP, Q_OWN, TOK)
    grad_qkv = jnp.concatenate(
        [turned, by_block(rotate_t(grad_kv_t[None], cosine_kv, -sine_kv)[0])], axis=1
    ).astype(BF16)
    grad_qkv_rows = grad_qkv.transpose(0, 2, 1).reshape(HALF, Q_OWN + HEAD_DIM)
    part_normed = contract("tn,dn->td", grad_qkv_rows, full_qkv).astype(BF16)

    def qkv_product(start, count):
        rows = contract("td,tn->dn", columns_at(normed, start, count), grad_qkv_rows)
        return rows.astype(BF16).reshape(count, CHUNK, Q_OWN + HEAD_DIM)

    qkv_pairs = [qkv_product(other, 2), qkv_product(other + 2, 2)]
    normed_pair = rows_to_core(part_normed, core)
    normed_pair, qkv_pairs, grad_qkv_rows = join(normed_pair, qkv_pairs, grad_qkv_rows)
    qkv_z = scatter_z(qkv_pairs)
    qkv_mine = qkv_product(zl * 4, 4)
    normed_total = normed_pair[0].astype(F32) + normed_pair[1].astype(F32)
    qkv_z, qkv_mine, down_out_y, normed_total = join(qkv_z, qkv_mine, down_out_y, normed_total)
    qkv_y = scatter_y(qkv_mine, qkv_z, y)
    normed_first = far_rows_along_x(normed_total, x)
    down_out_zh = scatter_zh(down_out_y)
    qkv_y, down_out_zh, normed_total, normed_first, gate_up_grads = join(
        qkv_y, down_out_zh, normed_total, normed_first, gate_up_grads
    )
    qkv_zh = scatter_zh(qkv_y)
    normed_parts = near_rows_along_x(normed_total, normed_first, x)
    shard_down_out = both_halves(down_out_zh)
    turned_out = swap_roles(shard_down_out[SUB:])
    qkv_zh, turned_out, normed_parts = join(qkv_zh, turned_out, normed_parts)
    down_out_all = gather_rows(jnp.concatenate([shard_down_out[:SUB], turned_out]))
    qkv_rail = rail_of(both_halves(qkv_zh))
    grad_normed = add_up(normed_parts)
    grad_gate, grad_up, mlp_products = put_gate_up(gate_up_grads, w_gate, w_up)
    qkv_rail, grad_gate, grad_up, mlp_products = join(qkv_rail, grad_gate, grad_up, mlp_products)
    output = (residual + output_rows.astype(F32)).astype(BF16)
    scale_here = rms_scale(tokens_here)
    grad_inputs = grad_residual + norm_back(grad_normed, tokens_here, scale_here, full_gain_attn)

    grad_down, grad_out = split_down_out(down_out_all)
    kv_columns = KV_HEADS * HEAD_DIM
    grad_query, grad_key, grad_value, attn_products = assemble(
        qkv_kernel,
        group_places,
        with_other_core(qkv_rail),
        CHUNK,
        [w_query, w_key, w_value],
        [
            (CHUNK, CHUNK, HEADS * HEAD_DIM),
            (CHUNK, CHUNK, kv_columns),
            (CHUNK, CHUNK, kv_columns),
            (8, 8, CHUNK),
        ],
    )
    return (
        output,
        grad_inputs,
        grad_query,
        grad_key,
        grad_value,
        grad_out,
        grad_gate,
        grad_up,
        grad_down,
        attn_products[0] / gain_attn.astype(F32),
        mlp_products[:, 0] / gain_mlp.astype(F32),
    )


def solution(mesh):
    split = Mesh(mesh.devices.reshape(2, 4, 2, 4, 2), AXES)
    dp, tokens = ("zl", "y"), AXES
    matrix = P(dp, None)
    return jax.shard_map(
        shards,
        mesh=split,
        in_specs=(
            P(tokens, None),
            P(tokens),
            P(tokens, None),
            matrix,
            matrix,
            matrix,
            matrix,
            matrix,
            matrix,
            matrix,
            P(dp),
            P(dp),
        ),
        out_specs=(
            P(tokens, None),
            P(tokens, None),
            matrix,
            matrix,
            matrix,
            matrix,
            matrix,
            matrix,
            matrix,
            P(dp),
            P(dp),
        ),
        check_vma=False,
    )
```

```python
import functools
import math

import jax
import jax.numpy as jnp
from jax import lax
from jax.experimental import pallas as pl
from jax.experimental.pallas import tpu as pltpu
from jax.sharding import Mesh, PartitionSpec as P

D = 2048
HEADS = 32
KV_HEADS = 4
HEAD_DIM = 64
FF = 5632
LENGTH = 2048
MIDDLE = 1920
EPSILON = 1e-05
THETA = 10000.0
NEG_LARGE = -1e30

AXES = ("zl", "y", "zh", "x", "core")
Z_RING = ("zl", "zh")
GROUP = 8
TOK = 128
HALF = GROUP * TOK
CHUNK = D // GROUP
FF_OWN = FF // GROUP
Q_OWN = HEADS * HEAD_DIM // GROUP
HEADS_OWN = HEADS // GROUP
SUB = FF_OWN // GROUP
OUT_SUB = Q_OWN // GROUP
KEY_CHUNK = 256
ROWS_Q = HEADS_OWN * TOK

F32 = jnp.float32
BF16 = jnp.bfloat16


def ring(values, axis, step):
    if axis == Z_RING:
        spot = [(z % 2) * 2 + z // 2 for z in range(4)]
        return lax.ppermute(values, axis, [(spot[z], spot[(z + step) % 4]) for z in range(4)])
    count = lax.axis_size(axis)
    return lax.ppermute(values, axis, [(i, (i + step) % count) for i in range(count)])


def place_kernel(copies, places, *refs):
    pieces, out, sems = refs[:-2], refs[-2], refs[-1]
    running = [
        pltpu.make_async_copy(
            pieces[piece].at[pl.ds(start, count)], out.at[pl.ds(places[i], count)], sems.at[i]
        )
        for i, (piece, start, count) in enumerate(copies)
    ]
    for copy in running:
        copy.start()
    for copy in running:
        copy.wait()


def cost(microseconds):
    return pl.CostEstimate(
        flops=int(microseconds * 1e9), bytes_accessed=int(microseconds * 3e6), transcendentals=0
    )


def put_in_place(places, pieces, copies, total):
    return pl.pallas_call(
        functools.partial(place_kernel, copies),
        grid_spec=pltpu.PrefetchScalarGridSpec(
            num_scalar_prefetch=1,
            grid=(1,),
            in_specs=[pl.BlockSpec(piece.shape, lambda i, places: (0, 0, 0)) for piece in pieces],
            out_specs=pl.BlockSpec(memory_space=pl.ANY),
            scratch_shapes=[pltpu.SemaphoreType.DMA((len(copies),))],
        ),
        out_shape=jax.ShapeDtypeStruct((total, *pieces[0].shape[1:]), pieces[0].dtype),
        compiler_params=pltpu.CompilerParams(vmem_limit_bytes=32 * 1024 * 1024),
        cost_estimate=cost(1),
        name="put_in_place",
    )(places, *pieces)


def near(block, axis):
    return ring(block, axis, -1), ring(block, axis, 1)


def far(ahead, behind, axis):
    half = ahead.shape[0] // 2
    return ring(ahead[:half], axis, -1), ring(behind[half:], axis, 1)


def across_z(own, ahead, behind, far_low, far_high):
    return (
        ring(jnp.concatenate([own, ahead]), Z_RING, 1),
        ring(jnp.concatenate([behind, far_low, far_high]), Z_RING, -1),
    )


def put_weights(blocks, z_blocks, zl, y):
    rows, columns = blocks[0].shape
    unit = rows // 2
    pieces = [block.reshape(-1, unit, columns) for block in (*blocks, *z_blocks)]
    copies = [(0, 0, 2), (1, 0, 2), (2, 0, 2), (3, 0, 1), (4, 0, 1)]
    copies += [(5, 0, 2), (5, 2, 2), (6, 0, 2), (6, 2, 2)]
    step = [(y + q) % 4 * 2 for q in range(4)]
    mine, other = zl * 8, (1 - zl) * 8
    places = [mine + step[0], mine + step[1], mine + step[3], mine + step[2], mine + step[2] + 1]
    places += [other + step[0], other + step[1], other + step[3], other + step[2]]
    places = jnp.stack(places).astype(jnp.int32)
    return put_in_place(places, pieces, copies, 16).reshape(8 * rows, columns)


def halves_kernel(copies, places, *refs):
    pieces, out, sems = refs[:-2], refs[-2], refs[-1]
    width = pieces[0].shape[-1]
    running = [
        pltpu.make_async_copy(
            pieces[piece].at[unit],
            out.at[places[i], :, pl.ds(unit % 2 * width, width)],
            sems.at[i],
        )
        for i, (piece, unit) in enumerate(copies)
    ]
    for copy in running:
        copy.start()
    for copy in running:
        copy.wait()


def stack_halves(block):
    half = block.shape[1] // 2
    return jnp.concatenate([block[:, :half], block[:, half:]])


def both_parities(own):
    half = own.shape[0] // 2
    return ring(own[:half], Z_RING, 1), ring(own[half:], Z_RING, -1)


def pair_places(zl, y):
    steps = [(y + q) % 4 for q in (0, 1, 3, 2)]
    return [[zl * 4 + at, (1 - zl) * 4 + at] for at in steps]


def put_pairs(pair, near_pairs, far_pair, zl, y):
    rows, columns = far_pair[0].shape
    pieces = [block.reshape(-1, rows, columns) for block in (pair, *near_pairs, *far_pair)]
    copies = [(i, u, 1) for i in range(3) for u in range(2)] + [(3, 0, 1), (4, 0, 1)]
    places = jnp.stack(sum(pair_places(zl, y), [])).astype(jnp.int32)
    return put_in_place(places, pieces, copies, 8).reshape(8 * rows, columns)


def put_row_pairs(pair, near_pairs, far_pair, zl, y):
    rows, columns = far_pair[0].shape
    unit = rows // 2
    pieces = [block.reshape(-1, unit, columns) for block in (pair, *near_pairs, *far_pair)]
    copies = [(i, u) for i in range(3) for u in range(4)]
    copies += [(i, u) for i in (3, 4) for u in range(2)]
    places = sum([[at, at] for spots in pair_places(zl, y) for at in spots], [])
    places = jnp.stack(places).astype(jnp.int32)
    return pl.pallas_call(
        functools.partial(halves_kernel, copies),
        grid_spec=pltpu.PrefetchScalarGridSpec(
            num_scalar_prefetch=1,
            grid=(1,),
            in_specs=[pl.BlockSpec(piece.shape, lambda i, places: (0, 0, 0)) for piece in pieces],
            out_specs=pl.BlockSpec(memory_space=pl.ANY),
            scratch_shapes=[pltpu.SemaphoreType.DMA((len(copies),))],
        ),
        out_shape=jax.ShapeDtypeStruct((8, unit, 2 * columns), BF16),
        compiler_params=pltpu.CompilerParams(vmem_limit_bytes=32 * 1024 * 1024),
        cost_estimate=cost(1),
        name="put_rows",
    )(places, *pieces).reshape(8 * unit, 2 * columns)


def put_rows(blocks, blocks_two, group_places):
    rows, columns = blocks[0].shape
    unit = rows // 2
    pieces = [block.reshape(-1, unit, columns) for block in (*blocks, *blocks_two)]
    copies = [(0, 0, 2), (1, 0, 2), (2, 0, 2), (3, 0, 1), (4, 0, 1)]
    copies += [(5, 0, 2), (6, 0, 2), (6, 2, 2), (7, 0, 2)]
    spots = [2 * group_places[i] for i in (0, 1, 3, 2, 2, 4, 5, 7, 6)]
    spots[4] = spots[4] + 1
    return put_in_place(jnp.stack(spots), pieces, copies, 2 * GROUP).reshape(
        GROUP * rows, columns
    )


def swap_blocks(own, ahead, behind, far_low, far_high):
    return (
        ring(own, "core", 1),
        ring(jnp.concatenate([ahead, behind]), "core", 1),
        ring(jnp.concatenate([far_low, far_high]), "core", 1),
    )


def scatter_z(pairs):
    return ring(pairs[0], Z_RING, 1), ring(pairs[1], Z_RING, -1)


def chunk_for_y(own, arrived, y, step):
    at = (y + step) % 4
    more = jnp.where(
        at < 2,
        lax.dynamic_index_in_dim(arrived[0], at & 1, 0, keepdims=False),
        lax.dynamic_index_in_dim(arrived[1], at & 1, 0, keepdims=False),
    )
    here = lax.dynamic_index_in_dim(own, at, 0, keepdims=False)
    return here.astype(F32) + more.astype(F32)


def chunks_for_y(own, arrived, y):
    return [chunk_for_y(own, arrived, y, 0)] + [
        chunk_for_y(own, arrived, y, step).astype(BF16) for step in (1, 2, 3)
    ]


def far_along_y(own, arrived, y):
    block = chunk_for_y(own, arrived, y, 2).astype(BF16)
    half = block.shape[0] // 2
    return ring(block[:half], "y", 1), ring(block[half:], "y", -1)


def near_along_y(own, arrived, first, y):
    ahead, behind = chunk_for_y(own, arrived, y, 1), chunk_for_y(own, arrived, y, 3)
    half = ahead.shape[0] // 2
    ahead = jnp.concatenate([ahead[:half] + first[0].astype(F32), ahead[half:]])
    behind = jnp.concatenate([behind[:half], behind[half:] + first[1].astype(F32)])
    return (
        chunk_for_y(own, arrived, y, 0),
        ring(ahead.astype(BF16), "y", 1),
        ring(behind.astype(BF16), "y", -1),
    )


def send_along_y(chunks):
    return [chunks[0]] + [ring(chunks[step], "y", step) for step in (1, 2, 3)]


def scatter_y(own, arrived, y):
    return send_along_y(chunks_for_y(own, arrived, y))


def scatter_zh(parts):
    total = add_up(parts).astype(BF16)
    return total, ring(total, "zh", 1)


def both_halves(pair):
    return add_up(pair).astype(BF16)


def rows_to_core(partial, core):
    partial = partial.astype(BF16).reshape(4, 2, TOK, D)

    def of_core(at):
        return lax.dynamic_index_in_dim(partial, at, 1, keepdims=False)

    return of_core(core), ring(of_core(1 - core), "core", 1)


def rows_along_x(total, x):
    def chunk(step):
        return lax.dynamic_index_in_dim(total, (x + step) % 4, 0, keepdims=False)

    far = ring(chunk(2).astype(BF16), "x", 2)
    ahead = ring(chunk(1).astype(BF16), "x", 1)
    behind = ring(chunk(3).astype(BF16), "x", -1)
    return chunk(0), ahead, behind, far


def exchange_x(blocks, x):
    def chunk(step):
        return lax.dynamic_index_in_dim(blocks, (x + step) % 4, 0, keepdims=False)

    return [chunk(0)] + [ring(chunk(step), "x", step) for step in (1, 2, 3)]


def put_exchanged(parts, others, x, core):
    rows = parts[0].shape[1]
    pieces = [*parts, others]
    copies, places = [], []
    for r in range(4):
        at = (x - r) % 4 * 2
        for tokens in range(2):
            copies += [(r, tokens, 1), (4, 2 * r + tokens, 1)]
            places += [tokens * GROUP + at + core, tokens * GROUP + at + 1 - core]
    places = jnp.stack(places).astype(jnp.int32)
    return put_in_place(places, pieces, copies, 2 * GROUP).reshape(2, GROUP, rows, TOK)


def far_rows_along_x(total, x):
    block = lax.dynamic_index_in_dim(total, (x + 2) % 4, 0, keepdims=False).astype(BF16)
    half = block.shape[0] // 2
    return ring(block[:half], "x", 1), ring(block[half:], "x", -1)


def near_rows_along_x(total, first, x):
    def chunk(step):
        return lax.dynamic_index_in_dim(total, (x + step) % 4, 0, keepdims=False)

    ahead, behind = chunk(1), chunk(3)
    half = ahead.shape[0] // 2
    ahead = jnp.concatenate([ahead[:half] + first[0].astype(F32), ahead[half:]])
    behind = jnp.concatenate([behind[:half], behind[half:] + first[1].astype(F32)])
    return chunk(0), ring(ahead.astype(BF16), "x", 1), ring(behind.astype(BF16), "x", -1)


def add_up(parts):
    return sum(part.astype(F32) for part in parts)


def rail_of(block):
    return [block, ring(block, "x", -1), ring(block, "x", 2), ring(block, "x", 1)]


def with_other_core(rail):
    return rail + [ring(part, "core", 1) for part in rail]


def swap_roles(values):
    return lax.ppermute(
        values,
        ("zl", "y", "x", "core"),
        [(a * GROUP + b, b * GROUP + a) for a in range(GROUP) for b in range(GROUP)],
    )


def after(values, *others):
    return lax.optimization_barrier((values, *others))[0]


def join(*groups):
    return lax.optimization_barrier(groups)


def heads_side_by_side(block):
    return jnp.concatenate(
        [block[i * HEAD_DIM : (i + 1) * HEAD_DIM] for i in range(HEADS_OWN)], axis=1
    )


def heads_stacked(block):
    return jnp.concatenate(
        [block[:, i * TOK : (i + 1) * TOK] for i in range(HEADS_OWN)], axis=0
    )


def allowed_keys(meta, j, start):
    half_at, head_end = meta[0], meta[1]
    shape = (KEY_CHUNK, ROWS_Q)
    column = lax.broadcasted_iota(jnp.int32, (1, ROWS_Q), 1)
    query = half_at * HALF + j * TOK + (column & (TOK - 1))
    first = jnp.where(
        query < head_end,
        0,
        jnp.where(query < head_end + MIDDLE, head_end, head_end + MIDDLE),
    )
    key = lax.broadcasted_iota(jnp.int32, shape, 0) + start + (half_at - 1) * HALF
    return (key <= query) & (key >= first)


def mask_scores(scores, meta, j, start, masked):
    parts = []
    for i in range(scores.shape[0] // KEY_CHUNK):
        part = scores[i * KEY_CHUNK : (i + 1) * KEY_CHUNK]
        if i in masked:
            part = jnp.where(allowed_keys(meta, j, start + i * KEY_CHUNK), part, NEG_LARGE)
        parts.append(part)
    return jnp.concatenate(parts) if len(parts) > 1 else parts[0]


def for_visible_keys(meta, j, step):
    chunks = HALF // KEY_CHUNK
    final = j == GROUP - 1

    @pl.when((meta[0] == 1) & jnp.logical_not(final))
    def _():
        step(0, HALF, (0,))

    @pl.when((meta[0] == 1) & final)
    def _():
        step(0, HALF, tuple(range(chunks)))

    for last in range(chunks):

        @pl.when((j * TOK // KEY_CHUNK == last) & jnp.logical_not(final))
        def _(last=last):
            step(HALF, (last + 1) * KEY_CHUNK, (0, last))

    @pl.when(final)
    def _():
        step(HALF, HALF, tuple(range(chunks)))


def dot_kn(left, right):
    return jnp.dot(left, right, preferred_element_type=F32)


def dot_nt(left, right):
    return lax.dot_general(
        left, right, (((1,), (1,)), ((), ())), preferred_element_type=F32
    )


def forward_kernel(
    meta, q_ref, kt_ref, vt_ref, out_ref, mixed_ref, lse_ref, k_ref, v_ref, top_ref, acc_ref
):
    j = pl.program_id(0)

    @pl.when(j == 0)
    def _():
        k_ref[...] = kt_ref[...].astype(F32).T.astype(BF16)
        row = lax.broadcasted_iota(jnp.int32, (V_ROWS - HEAD_DIM, 2 * HALF), 0)
        v_ref[:HEAD_DIM, :] = vt_ref[...]
        v_ref[HEAD_DIM:, :] = jnp.where(row == 0, 1.0, 0.0).astype(BF16)

    query = heads_side_by_side(q_ref[...])
    top_ref[...] = jnp.full_like(top_ref, NEG_LARGE)
    acc_ref[...] = jnp.zeros_like(acc_ref)

    def step(start, size, masked):
        rows = slice(start, start + size)
        scores = mask_scores(dot_kn(k_ref[rows, :], query), meta, j, start, masked)
        old = top_ref[...]
        new = jnp.maximum(old, jnp.max(scores, axis=0, keepdims=True))
        weights = jnp.exp(scores - new).astype(BF16)
        acc_ref[...] = acc_ref[...] * jnp.exp(old - new) + dot_kn(v_ref[:, rows], weights)
        top_ref[...] = new

    for_visible_keys(meta, j, step)
    total = acc_ref[HEAD_DIM : HEAD_DIM + 1, :]
    attended = heads_stacked(acc_ref[:HEAD_DIM, :] / total)
    out_ref[0] = attended
    mixed_ref[0] = attended.astype(BF16)
    lse_ref[...] = jnp.broadcast_to(top_ref[...] + jnp.log(total), lse_ref.shape)


def minus_rows(values):
    rows, rest = [], -values
    for _ in range(3):
        rows.append(rest.astype(BF16).astype(F32))
        rest = rest - rows[-1]
    zeros = jnp.zeros((EXTRA - 3, values.shape[1]), F32)
    return jnp.concatenate([*rows, zeros]).astype(BF16)


def backward_kernel(
    meta,
    q_ref,
    g_ref,
    o_ref,
    lse_ref,
    kt_ref,
    vt_ref,
    *rest,
    begin,
):
    dq_ref, dk_ref, dv_ref, k_ref, v_ref, acc_ref = rest[-6:]
    j = pl.program_id(0) + begin

    @pl.when(pl.program_id(0) == 0)
    def _():
        row = lax.broadcasted_iota(jnp.int32, (EXTRA, 2 * HALF), 0)
        ones = jnp.where(row < 3, 1.0, 0.0)
        k_ref[...] = jnp.concatenate([kt_ref[...].astype(F32), ones]).T.astype(BF16)
        v_ref[...] = jnp.concatenate([vt_ref[...].astype(F32), ones]).T.astype(BF16)
        if begin:
            dk_ref[...] = rest[0][...]
            dv_ref[...] = rest[1][...]
        else:
            dk_ref[...] = jnp.zeros_like(dk_ref)
            dv_ref[...] = jnp.zeros_like(dv_ref)

    query = heads_side_by_side(q_ref[...])
    grad = heads_side_by_side(g_ref[0])
    mixed = heads_side_by_side(o_ref[0])
    delta = jnp.sum(grad.astype(F32) * mixed, axis=0, keepdims=True)
    query_less = jnp.concatenate([query, minus_rows(lse_ref[0:1, :])])
    grad_less = jnp.concatenate([grad, minus_rows(delta)])
    acc_ref[...] = jnp.zeros_like(acc_ref)

    def step(start, size, masked):
        rows = slice(start, start + size)
        scores = mask_scores(dot_kn(k_ref[rows, :], query_less), meta, j, start, masked)
        probs = jnp.exp(scores)
        grad_scores = (probs * dot_kn(v_ref[rows, :], grad_less)).astype(BF16)
        acc_ref[...] += dot_kn(kt_ref[:, rows], grad_scores)
        dk_ref[:, rows] += dot_nt(query, grad_scores)
        dv_ref[:, rows] += dot_nt(grad, probs.astype(BF16))

    for_visible_keys(meta, j, step)
    dq_ref[0] = heads_stacked(acc_ref[...] * (1.0 / math.sqrt(HEAD_DIM)))


def whole(shape):
    return pl.BlockSpec(shape, lambda j, meta: (0,) * len(shape))


def token_block(rows):
    return pl.BlockSpec((rows, TOK), lambda j, meta: (0, j))


V_ROWS = 80
EXTRA = 16
LSE_ROWS = 8


def attend(meta, query_t, keys_t, values_t):
    return pl.pallas_call(
        forward_kernel,
        grid_spec=pltpu.PrefetchScalarGridSpec(
            num_scalar_prefetch=1,
            grid=(GROUP,),
            in_specs=[
                token_block(Q_OWN),
                whole((HEAD_DIM, 2 * HALF)),
                whole((HEAD_DIM, 2 * HALF)),
            ],
            out_specs=[
                pl.BlockSpec((1, Q_OWN, TOK), lambda j, meta: (j, 0, 0)),
                pl.BlockSpec((1, Q_OWN, TOK), lambda j, meta: (j, 0, 0)),
                pl.BlockSpec((LSE_ROWS, ROWS_Q), lambda j, meta: (j, 0)),
            ],
            scratch_shapes=[
                pltpu.VMEM((2 * HALF, HEAD_DIM), BF16),
                pltpu.VMEM((V_ROWS, 2 * HALF), BF16),
                pltpu.VMEM((1, ROWS_Q), F32),
                pltpu.VMEM((V_ROWS, ROWS_Q), F32),
            ],
        ),
        out_shape=[
            jax.ShapeDtypeStruct((GROUP, Q_OWN, TOK), F32),
            jax.ShapeDtypeStruct((GROUP, Q_OWN, TOK), BF16),
            jax.ShapeDtypeStruct((GROUP * LSE_ROWS, ROWS_Q), F32),
        ],
        compiler_params=pltpu.CompilerParams(vmem_limit_bytes=32 * 1024 * 1024),
        cost_estimate=cost(1),
        name="attend",
    )(meta, query_t, keys_t, values_t)


def attend_back(meta, begin, end, query_t, grad_t, attn_t, lse, keys_t, values_t, *sums):
    block = pl.BlockSpec((1, Q_OWN, TOK), lambda j, meta: (j + begin, 0, 0))
    return pl.pallas_call(
        functools.partial(backward_kernel, begin=begin),
        grid_spec=pltpu.PrefetchScalarGridSpec(
            num_scalar_prefetch=1,
            grid=(end - begin,),
            in_specs=[
                pl.BlockSpec((Q_OWN, TOK), lambda j, meta: (0, j + begin)),
                block,
                block,
                pl.BlockSpec((LSE_ROWS, ROWS_Q), lambda j, meta: (j + begin, 0)),
            ]
            + [whole((HEAD_DIM, 2 * HALF))] * (2 + len(sums)),
            out_specs=[
                pl.BlockSpec((1, Q_OWN, TOK), lambda j, meta: (j, 0, 0)),
                whole((HEAD_DIM, 2 * HALF)),
                whole((HEAD_DIM, 2 * HALF)),
            ],
            scratch_shapes=[
                pltpu.VMEM((2 * HALF, HEAD_DIM + EXTRA), BF16),
                pltpu.VMEM((2 * HALF, HEAD_DIM + EXTRA), BF16),
                pltpu.VMEM((HEAD_DIM, ROWS_Q), F32),
            ],
        ),
        out_shape=[
            jax.ShapeDtypeStruct((end - begin, Q_OWN, TOK), F32),
            jax.ShapeDtypeStruct((HEAD_DIM, 2 * HALF), F32),
            jax.ShapeDtypeStruct((HEAD_DIM, 2 * HALF), F32),
        ],
        compiler_params=pltpu.CompilerParams(vmem_limit_bytes=32 * 1024 * 1024),
        cost_estimate=cost(1),
        name="attend_back",
    )(meta, query_t, grad_t, attn_t, lse, keys_t, values_t, *sums)


def norm_kernel(places, *refs):
    (own, ahead, behind, low, high, own_two, near_two, far_two, weights) = refs[:9]
    normed_out, gains_out, gains = refs[9:]
    i = pl.program_id(0)

    @pl.when(i == 0)
    def _():
        gains[...] = weights[...].astype(F32).T[HEAD_DIM : HEAD_DIM + 8, :]
        gains_out[...] = gains[...]

    def norm(block, start, size, to):
        values = block[start : start + size, :].astype(F32)
        scale = lax.rsqrt(jnp.mean(values * values, axis=-1, keepdims=True) + EPSILON)
        normed_out[to : to + size, :] = (values * scale * gains[0:1, :]).astype(BF16)

    sources = [
        [(own, 0)],
        [(ahead, 0)],
        [(low, 0), (high, 0)],
        [(behind, 0)],
        [(own_two, 0)],
        [(near_two, 0)],
        [(far_two, 0)],
        [(near_two, TOK)],
    ]
    for at, parts in enumerate(sources):

        @pl.when(i == at)
        def _(parts=parts):
            size = TOK // len(parts)
            for k, (block, start) in enumerate(parts):
                norm(block, start, size, k * size)


def gather_norm(places, pieces, early_all):
    rows = [pl.BlockSpec(piece.shape, lambda i, places: (0, 0)) for piece in pieces]
    placed = pl.BlockSpec((TOK, D), lambda i, places: (places[i], 0))
    return pl.pallas_call(
        norm_kernel,
        grid_spec=pltpu.PrefetchScalarGridSpec(
            num_scalar_prefetch=1,
            grid=(GROUP,),
            in_specs=rows + [pl.BlockSpec((D, 128), lambda i, places: (0, 2))],
            out_specs=[
                placed,
                pl.BlockSpec((8, D), lambda i, places: (0, 0)),
            ],
            scratch_shapes=[pltpu.VMEM((8, D), F32)],
        ),
        out_shape=[
            jax.ShapeDtypeStruct((HALF, D), BF16),
            jax.ShapeDtypeStruct((8, D), F32),
        ],
        compiler_params=pltpu.CompilerParams(vmem_limit_bytes=32 * 1024 * 1024),
        cost_estimate=cost(1),
        name="gather_norm",
    )(places, *pieces, early_all)


def take_kernel(own, gate, up, out):
    for at in range(GROUP):

        @pl.when(own[0] == at)
        def _():
            parts = []
            for ref in (gate, up):
                for block in range(GROUP):
                    start = block * FF_OWN + at * SUB
                    low = start // 128 * 128
                    window = ref[:, low : low + 256].astype(F32)
                    parts.append(window[:, start - low : start - low + SUB])
            out[...] = jnp.concatenate(parts, axis=1).astype(BF16)


def take_columns(own, gate, up):
    rows = 64
    return pl.pallas_call(
        take_kernel,
        grid_spec=pltpu.PrefetchScalarGridSpec(
            num_scalar_prefetch=1,
            grid=(CHUNK // rows,),
            in_specs=[pl.BlockSpec((rows, FF), lambda i, own: (i, 0))] * 2,
            out_specs=pl.BlockSpec((rows, 2 * FF_OWN), lambda i, own: (i, 0)),
        ),
        out_shape=jax.ShapeDtypeStruct((CHUNK, 2 * FF_OWN), BF16),
        compiler_params=pltpu.CompilerParams(vmem_limit_bytes=32 * 1024 * 1024),
        cost_estimate=cost(1),
        name="take_columns",
    )(own, gate, up)


def gate_up_kernel(pieces, w_gate, w_up, gate, up, products):
    total = 0.0
    for which, (weight, out) in enumerate(((w_gate, gate), (w_up, up))):
        parts = []
        for block in range(GROUP):
            start = which * FF_OWN + block * SUB
            low = start // 128 * 128
            size = min(256, 2 * FF_OWN - low)
            for at in range(GROUP):
                window = pieces[at, :, low : low + size].astype(F32)
                parts.append(window[:, start - low : start - low + SUB])
        values = jnp.concatenate(parts, axis=1)
        out[...] = values
        total = total + jnp.sum(values * weight[...].astype(F32), axis=1, keepdims=True)
    products[...] = jnp.broadcast_to(total, products.shape)


def put_gate_up(pieces, w_gate, w_up):
    rows = 64
    row_block = pl.BlockSpec((rows, FF), lambda i: (i, 0))
    return pl.pallas_call(
        gate_up_kernel,
        grid=(CHUNK // rows,),
        in_specs=[
            pl.BlockSpec((GROUP, rows, 2 * FF_OWN), lambda i: (0, i, 0)),
            row_block,
            row_block,
        ],
        out_specs=[row_block, row_block, pl.BlockSpec((rows, 128), lambda i: (i, 0))],
        out_shape=[
            jax.ShapeDtypeStruct((CHUNK, FF), F32),
            jax.ShapeDtypeStruct((CHUNK, FF), F32),
            jax.ShapeDtypeStruct((CHUNK, 128), F32),
        ],
        compiler_params=pltpu.CompilerParams(vmem_limit_bytes=48 * 1024 * 1024),
        cost_estimate=cost(1),
        name="gate_up",
    )(pieces.reshape(GROUP, CHUNK, 2 * FF_OWN), w_gate, w_up)


def down_out_kernel(rows, down, out):
    values = rows[...].astype(F32)
    down[...] = values[:SUB]
    out[...] = values[SUB:]


def split_down_out(rows):
    return pl.pallas_call(
        down_out_kernel,
        grid=(GROUP,),
        in_specs=[pl.BlockSpec((SUB + OUT_SUB, D), lambda i: (i, 0))],
        out_specs=[
            pl.BlockSpec((SUB, D), lambda i: (i, 0)),
            pl.BlockSpec((OUT_SUB, D), lambda i: (i, 0)),
        ],
        out_shape=[
            jax.ShapeDtypeStruct((FF_OWN, D), F32),
            jax.ShapeDtypeStruct((Q_OWN, D), F32),
        ],
        compiler_params=pltpu.CompilerParams(vmem_limit_bytes=32 * 1024 * 1024),
        cost_estimate=cost(1),
        name="down_out",
    )(rows)


def qkv_kernel(places, *refs):
    pieces, weights, outs, products, stack = refs[:8], refs[8:11], refs[11:14], *refs[14:]
    query, key, value = outs
    for i, piece in enumerate(pieces):
        stack[places[i]] = piece[...]
    for at in range(GROUP):
        values = stack[at].astype(F32)
        query[:, at * Q_OWN : (at + 1) * Q_OWN] = values[:, :Q_OWN]
        head = key if at % 2 == 0 else value
        place = (at // 2) * HEAD_DIM
        head[:, place : place + HEAD_DIM] = values[:, Q_OWN : Q_OWN + HEAD_DIM]
    total = sum(
        jnp.sum(out[...] * weight[...].astype(F32), axis=1, keepdims=True)
        for out, weight in zip(outs, weights, strict=True)
    )
    products[...] = jnp.broadcast_to(total, (CHUNK, 128)).T[:8]


def assemble(kernel, places, pieces, rows, weights, shapes):
    count, width = pieces[0].shape
    return pl.pallas_call(
        kernel,
        grid_spec=pltpu.PrefetchScalarGridSpec(
            num_scalar_prefetch=1,
            grid=(count // rows,),
            in_specs=[pl.BlockSpec((rows, width), lambda i, places: (i, 0))] * 8
            + [pl.BlockSpec((rows, w.shape[1]), lambda i, places: (i, 0)) for w in weights],
            out_specs=[
                pl.BlockSpec((block, columns), lambda i, places: (i, 0))
                for _, block, columns in shapes
            ],
            scratch_shapes=[pltpu.VMEM((GROUP, rows, width), BF16)],
        ),
        out_shape=[jax.ShapeDtypeStruct((whole, columns), F32) for whole, _, columns in shapes],
        compiler_params=pltpu.CompilerParams(vmem_limit_bytes=48 * 1024 * 1024),
        cost_estimate=cost(1),
        name=kernel.__name__.removesuffix("_kernel"),
    )(places, *pieces, *weights)


def rms_scale(values):
    return lax.rsqrt(jnp.mean(values * values, axis=-1, keepdims=True) + EPSILON)


def rotate_t(values, cosine, sine_table):
    half = HEAD_DIM // 2
    first, second = values[:, :half], values[:, half:]
    return jnp.concatenate(
        [first * cosine - second * sine_table, second * cosine + first * sine_table], axis=1
    )


def norm_back(grad_normed, values, scale_rows, gain_full):
    unit_rows = values * scale_rows
    grad_unit = grad_normed * gain_full
    return scale_rows * (
        grad_unit - unit_rows * jnp.mean(grad_unit * unit_rows, axis=-1, keepdims=True)
    )


def contract(form, left, right):
    return jnp.einsum(form, left, right, preferred_element_type=F32)


def shards(
    inputs,
    positions,
    cotangent,
    w_query,
    w_key,
    w_value,
    w_out,
    w_gate,
    w_up,
    w_down,
    gain_attn,
    gain_mlp,
):
    zl, y, zh, x, core = (lax.axis_index(axis) for axis in AXES)
    xc = x * 2 + core
    group = ("x", "core")

    def gather_rows(rows):
        return lax.all_gather(rows, group, axis=0, tiled=True)

    inputs_near = near(inputs, "x")
    inputs_two = ring(inputs, "core", 1)

    index_here = (zh * GROUP + xc) * TOK + jnp.arange(TOK, dtype=jnp.int32)
    head_end = jnp.where(
        (zh == 0) & (xc == 0),
        jnp.sum((positions == index_here).astype(jnp.int32)),
        index_here[0] - positions[0],
    )
    meta = jnp.stack([zh, head_end]).astype(jnp.int32)
    rail = [((x + r) % 4) * 2 for r in range(4)]
    group_places = jnp.stack(
        [at + core for at in rail] + [at + 1 - core for at in rail]
    ).astype(jnp.int32)
    def columns(weight, width):
        return lax.dynamic_slice_in_dim(weight, xc * width, width, axis=1)

    kv_here = jnp.where(core == 0, w_key, w_value)
    kv_here = lax.dynamic_slice_in_dim(kv_here, x * HEAD_DIM, HEAD_DIM, axis=1)
    early = jnp.concatenate(
        [
            columns(w_query, Q_OWN),
            kv_here,
            gain_attn[:, None],
            gain_mlp[:, None],
            jnp.zeros((CHUNK, 62), BF16),
        ],
        axis=1,
    )
    early_near = near(early, "y")
    gate_up_here = take_columns(xc[None].astype(jnp.int32), w_gate, w_up)
    half_width = D // 2
    out_here = lax.dynamic_slice_in_dim(w_out, core * half_width, half_width, axis=1)
    down_here = stack_halves(lax.dynamic_slice_in_dim(w_down, xc * SUB, SUB, axis=0))
    early_blocks = (early, *early_near, *far(*early_near, "y"))
    early_blocks, inputs_near, out_here = join(early_blocks, inputs_near, out_here)
    early_z = across_z(*early_blocks)
    inputs_far = far(*inputs_near, "x")
    out_near = near(out_here, "y")
    early_z, inputs_far, inputs_two, gate_up_here = join(
        early_z, inputs_far, inputs_two, gate_up_here
    )
    inputs_rest = (
        ring(jnp.concatenate(inputs_near), "core", 1),
        ring(jnp.concatenate(inputs_far), "core", 1),
    )
    full_qkv_gains = put_weights(early_blocks, early_z, zl, y)
    full_qkv_gains, inputs_rest, out_near = join(full_qkv_gains, inputs_rest, out_near)
    out_far = far(*out_near, "y")
    gate_up_other = both_parities(gate_up_here)
    normed, gains = gather_norm(
        group_places,
        [inputs, *inputs_near, *inputs_far, inputs_two, *inputs_rest],
        full_qkv_gains,
    )
    full_qkv = full_qkv_gains[:, : Q_OWN + HEAD_DIM]
    full_gain_attn, full_gain_mlp = gains[0], gains[1]

    index_all = zh * HALF + jnp.arange(HALF, dtype=jnp.int32)
    doc_start = jnp.where(
        index_all < head_end,
        0,
        jnp.where(index_all < head_end + MIDDLE, head_end, head_end + MIDDLE),
    )
    frequency = THETA ** (-(jnp.arange(HEAD_DIM // 2, dtype=F32) * 2.0 / HEAD_DIM))
    angles = frequency[:, None] * (index_all - doc_start).astype(F32)[None, :]
    cosine, sine_table = jnp.cos(angles), jnp.sin(angles)
    is_key = core == 0
    cosine_kv = jnp.where(is_key, cosine, 1.0)
    sine_kv = jnp.where(is_key, sine_table, 0.0)

    raw_t = contract("dn,td->nt", full_qkv, normed)
    query_t = (
        rotate_t(raw_t[:Q_OWN].reshape(HEADS_OWN, HEAD_DIM, HALF), cosine, sine_table)
        .reshape(Q_OWN, HALF)
        .astype(BF16)
        * (1.0 / math.sqrt(HEAD_DIM))
    ).astype(BF16)
    kv_t = rotate_t(raw_t[Q_OWN:][None], cosine_kv, sine_kv)[0].astype(BF16)
    kv_other = ring(kv_t, "core", 1)
    kv_prev = lax.ppermute(kv_t, "zh", [(0, 1)])
    kv_prev_other = lax.ppermute(kv_t, ("zh", "core"), [(0, 3), (1, 2)])
    kv_t, kv_other, kv_prev, kv_prev_other, query_t, gate_up_here, gate_up_other, out_far = join(
        kv_t, kv_other, kv_prev, kv_prev_other, query_t, gate_up_here, gate_up_other, out_far
    )
    mine = jnp.concatenate([kv_prev, kv_t], axis=1)
    theirs = jnp.concatenate([kv_prev_other, kv_other], axis=1)
    keys_t = jnp.where(is_key, mine, theirs)
    values_t = jnp.where(is_key, theirs, mine)
    out_blocks = (out_here, *out_near, *out_far)
    out_z = across_z(*out_blocks)
    gate_up_pair = jnp.concatenate([gate_up_here, *gate_up_other])
    gate_up_near = near(gate_up_pair, "y")
    attended = attend(meta, query_t, keys_t, values_t)
    (attn_t, mixed_t, lse), out_z, gate_up_near = join(attended, out_z, gate_up_near)
    mixed_parts = exchange_x(mixed_t.reshape(4, 2, Q_OWN, TOK), x)
    gate_up_far = far(*gate_up_near, "y")
    out_half = put_weights(out_blocks, out_z, zl, y)
    mixed_parts, out_half = join(mixed_parts, out_half)
    mixed_others = ring(jnp.concatenate(mixed_parts), "core", 1)
    mixed_others, mixed_parts = join(mixed_others, mixed_parts)
    mixed_both = put_exchanged(mixed_parts, mixed_others, x, core)

    def of_core(values, at):
        return lax.dynamic_index_in_dim(values, at, 0, keepdims=False)

    out_rows = contract("ckt,kd->ctd", mixed_both.reshape(2, D, TOK), out_half).astype(BF16)
    out_mine = of_core(out_rows, core)
    out_theirs = ring(of_core(out_rows, 1 - core), "core", 1)
    out_theirs, down_here, cotangent_here = join(out_theirs, down_here, cotangent)
    tokens_here = inputs.astype(F32)
    residual = tokens_here + jnp.concatenate(
        [
            jnp.where(core == 0, out_mine, out_theirs),
            jnp.where(core == 0, out_theirs, out_mine),
        ],
        axis=1,
    ).astype(F32)
    scale_mlp = rms_scale(residual)
    normed_rows = (residual * scale_mlp * full_gain_mlp).astype(BF16)
    normed_mlp = gather_rows(normed_rows)
    down_other = both_parities(down_here)
    cotangent_near = near(cotangent_here, "x")
    down_other, cotangent_near, gate_up_far = join(down_other, cotangent_near, gate_up_far)
    down_pair = jnp.concatenate([down_here, *down_other])
    down_near = near(down_pair, "y")
    cotangent_far = far(*cotangent_near, "x")
    gate_up_all = put_pairs(gate_up_pair, gate_up_near, gate_up_far, zl, y)
    normed_mlp, gate_up_all, down_near, cotangent_far = join(
        normed_mlp, gate_up_all, down_near, cotangent_far
    )

    gate_up = contract("td,df->tf", normed_mlp, gate_up_all)
    down_far = far(*down_near, "y")
    cotangent_blocks = (cotangent_here, *cotangent_near, *cotangent_far)
    cotangent_two = swap_blocks(*cotangent_blocks)
    gate_up, down_far, cotangent_two = join(gate_up, down_far, cotangent_two)
    cotangent_all = put_rows(cotangent_blocks, cotangent_two, group_places)
    full_down = put_row_pairs(down_pair, down_near, down_far, zl, y)
    grad_hidden = contract("td,fd->tf", cotangent_all, full_down)
    gate, upward = gate_up[:, :FF_OWN], gate_up[:, FF_OWN:]
    sigmoid_gate = jax.nn.sigmoid(gate)
    silu_gate = gate * sigmoid_gate
    hidden = (silu_gate * upward).astype(BF16)
    grad_acts = jnp.concatenate(
        [
            (grad_hidden * upward * sigmoid_gate * (1.0 + gate * (1.0 - sigmoid_gate))).astype(BF16),
            (grad_hidden * silu_gate).astype(BF16),
        ],
        axis=1,
    )
    back_rows = rows_to_core(contract("tf,df->td", grad_acts, gate_up_all), core)

    def columns_at(values, start, count):
        return lax.dynamic_slice_in_dim(values, start * CHUNK, count * CHUNK, axis=1)

    other = (1 - zl) * 4

    def gate_up_product(start, count):
        rows = contract("td,tf->df", columns_at(normed_mlp, start, count), grad_acts)
        return rows.astype(BF16).reshape(count, CHUNK, 2 * FF_OWN)

    gate_up_theirs = gate_up_product(other, 4)
    back_total = back_rows[0].astype(F32) + back_rows[1].astype(F32)
    back_total, gate_up_pairs, hidden, normed_mlp, grad_acts = join(
        back_total, (gate_up_theirs[:2], gate_up_theirs[2:]), hidden, normed_mlp, grad_acts
    )
    back_rows = rows_along_x(back_total, x)
    gate_up_z = scatter_z(gate_up_pairs)
    gate_up_mine = gate_up_product(zl * 4, 4)
    part_down = contract("tf,td->fd", hidden, cotangent_all).astype(BF16)
    part_down = part_down.reshape(8, SUB, D)
    part_output = contract("tf,fd->td", hidden, full_down).astype(BF16)
    back_rows, gate_up_z, gate_up_mine, part_down, part_output = join(
        back_rows, gate_up_z, gate_up_mine, part_down, part_output
    )
    gate_up_far = far_along_y(gate_up_mine, gate_up_z, y)
    grad_normed_mlp = add_up(back_rows)
    grad_residual = cotangent.astype(F32) + norm_back(
        grad_normed_mlp, residual, scale_mlp, full_gain_mlp
    )
    grad_here = grad_residual.astype(BF16)
    grad_theirs = ring(grad_here, "core", 1)
    grad_theirs, grad_here = join(grad_theirs, grad_here)
    grad_both = jnp.stack(
        [jnp.where(core == 0, grad_here, grad_theirs), jnp.where(core == 0, grad_theirs, grad_here)]
    )
    grad_both = jnp.where(core == 0, grad_both[..., :half_width], grad_both[..., half_width:])
    grad_partial = contract("kd,ctd->kct", out_half, grad_both).reshape(4, 2, Q_OWN, 2, TOK)

    def heads_of(at):
        return lax.dynamic_index_in_dim(grad_partial, at, 1, keepdims=False)

    grad_arrived = ring(heads_of(1 - core).astype(BF16), "core", 1)
    grad_arrived, gate_up_far = join(grad_arrived, gate_up_far)
    grad_heads = (heads_of(core) + grad_arrived.astype(F32)).astype(BF16)
    grad_parts = exchange_x(grad_heads.transpose(0, 2, 1, 3), x)
    grad_attn_out = gather_rows(grad_here)
    gate_up_y = near_along_y(gate_up_mine, gate_up_z, gate_up_far, y)
    grad_parts, gate_up_y, part_output = join(grad_parts, gate_up_y, part_output)
    output_rows = lax.psum_scatter(part_output, group, scatter_dimension=0, tiled=True)
    gate_up_zh = scatter_zh(gate_up_y)
    places = jnp.stack([(x - r) % 4 * 2 for r in range(4)]).astype(jnp.int32)
    grad_mixed_t = put_in_place(places, grad_parts, [(r, 0, 2) for r in range(4)], GROUP)
    back_args = (query_t, grad_mixed_t, attn_t, lse, keys_t, values_t)
    attended = attend_back(meta, 0, 4, *back_args)
    (query_0, *key_sums), gate_up_zh, grad_attn_out = join(attended, gate_up_zh, grad_attn_out)
    shard_gate_up = both_halves(gate_up_zh)
    part_out = contract(
        "bkt,btd->kd", mixed_t, grad_attn_out.reshape(GROUP, TOK, D)
    ).astype(BF16)
    part_down_out = jnp.concatenate([part_down, part_out.reshape(8, OUT_SUB, D)], axis=1)

    def chunks(start, count):
        return lax.dynamic_slice_in_dim(part_down_out, start, count, axis=0)

    down_out_pairs = (chunks(other, 2), chunks(other + 2, 2))
    down_out_pairs, key_sums = join(down_out_pairs, key_sums)
    down_out_z = scatter_z(down_out_pairs)
    attended = attend_back(meta, 4, 8, *back_args, *key_sums)
    (query_1, grad_keys_t, grad_values_t), down_out_z, output_rows, shard_gate_up = join(
        attended, down_out_z, output_rows, shard_gate_up
    )
    gate_up_grads = gather_rows(shard_gate_up)
    grad_query_t = jnp.concatenate([query_0, query_1])

    kept = jnp.where(is_key, grad_keys_t, grad_values_t)
    given = jnp.where(is_key, grad_values_t, grad_keys_t)
    arrived = ring(given.astype(BF16), "core", 1)
    arrived, kept, grad_query_t = join(arrived, kept, grad_query_t)
    grad_kv = kept + arrived.astype(F32)
    from_next = lax.ppermute(grad_kv[:, :HALF].astype(BF16), "zh", [(1, 0)])
    from_next, grad_kv, grad_query_t = join(from_next, grad_kv, grad_query_t)
    down_out_y = scatter_y(chunks(zl * 4, 4), down_out_z, y)
    grad_kv_t = grad_kv[:, HALF:] + from_next.astype(F32)

    def by_block(table):
        return table.reshape(-1, GROUP, TOK).transpose(1, 0, 2)

    half_head = HEAD_DIM // 2
    cosine_b, sine_b = by_block(cosine)[:, None], by_block(sine_table)[:, None]
    first = grad_query_t.reshape(GROUP, HEADS_OWN, HEAD_DIM, TOK)[:, :, :half_head]
    second = grad_query_t.reshape(GROUP, HEADS_OWN, HEAD_DIM, TOK)[:, :, half_head:]
    turned = jnp.concatenate(
        [first * cosine_b + second * sine_b, second * cosine_b - first * sine_b], axis=2
    ).reshape(GROUP, Q_OWN, TOK)
    grad_qkv = jnp.concatenate(
        [turned, by_block(rotate_t(grad_kv_t[None], cosine_kv, -sine_kv)[0])], axis=1
    ).astype(BF16)
    grad_qkv_rows = grad_qkv.transpose(0, 2, 1).reshape(HALF, Q_OWN + HEAD_DIM)
    part_normed = contract("tn,dn->td", grad_qkv_rows, full_qkv).astype(BF16)

    def qkv_product(start, count):
        rows = contract("td,tn->dn", columns_at(normed, start, count), grad_qkv_rows)
        return rows.astype(BF16).reshape(count, CHUNK, Q_OWN + HEAD_DIM)

    qkv_pairs = [qkv_product(other, 2), qkv_product(other + 2, 2)]
    normed_pair = rows_to_core(part_normed, core)
    normed_pair, qkv_pairs, grad_qkv_rows = join(normed_pair, qkv_pairs, grad_qkv_rows)
    qkv_z = scatter_z(qkv_pairs)
    qkv_mine = qkv_product(zl * 4, 4)
    normed_total = normed_pair[0].astype(F32) + normed_pair[1].astype(F32)
    qkv_z, qkv_mine, down_out_y, normed_total = join(qkv_z, qkv_mine, down_out_y, normed_total)
    qkv_y = scatter_y(qkv_mine, qkv_z, y)
    normed_first = far_rows_along_x(normed_total, x)
    down_out_zh = scatter_zh(down_out_y)
    qkv_y, down_out_zh, normed_total, normed_first, gate_up_grads = join(
        qkv_y, down_out_zh, normed_total, normed_first, gate_up_grads
    )
    qkv_zh = scatter_zh(qkv_y)
    normed_parts = near_rows_along_x(normed_total, normed_first, x)
    shard_down_out = both_halves(down_out_zh)
    turned_out = swap_roles(shard_down_out[SUB:])
    qkv_zh, turned_out, normed_parts, gate_up_grads = join(
        qkv_zh, turned_out, normed_parts, gate_up_grads
    )
    grad_gate, grad_up, mlp_products = put_gate_up(gate_up_grads, w_gate, w_up)
    down_out_all = gather_rows(jnp.concatenate([shard_down_out[:SUB], turned_out]))
    qkv_rail = rail_of(both_halves(qkv_zh))
    grad_normed = add_up(normed_parts)
    output = (residual + output_rows.astype(F32)).astype(BF16)
    scale_here = rms_scale(tokens_here)
    grad_inputs = grad_residual + norm_back(grad_normed, tokens_here, scale_here, full_gain_attn)

    grad_down, grad_out = split_down_out(down_out_all)
    kv_columns = KV_HEADS * HEAD_DIM
    grad_query, grad_key, grad_value, attn_products = assemble(
        qkv_kernel,
        group_places,
        with_other_core(qkv_rail),
        CHUNK,
        [w_query, w_key, w_value],
        [
            (CHUNK, CHUNK, HEADS * HEAD_DIM),
            (CHUNK, CHUNK, kv_columns),
            (CHUNK, CHUNK, kv_columns),
            (8, 8, CHUNK),
        ],
    )
    return (
        output,
        grad_inputs,
        grad_query,
        grad_key,
        grad_value,
        grad_out,
        grad_gate,
        grad_up,
        grad_down,
        attn_products[0] / gain_attn.astype(F32),
        mlp_products[:, 0] / gain_mlp.astype(F32),
    )


def solution(mesh):
    split = Mesh(mesh.devices.reshape(2, 4, 2, 4, 2), AXES)
    dp, tokens = ("zl", "y"), AXES
    matrix = P(dp, None)
    return jax.shard_map(
        shards,
        mesh=split,
        in_specs=(
            P(tokens, None),
            P(tokens),
            P(tokens, None),
            matrix,
            matrix,
            matrix,
            matrix,
            matrix,
            matrix,
            matrix,
            P(dp),
            P(dp),
        ),
        out_specs=(
            P(tokens, None),
            P(tokens, None),
            matrix,
            matrix,
            matrix,
            matrix,
            matrix,
            matrix,
            matrix,
            P(dp),
            P(dp),
        ),
        check_vma=False,
    )
```

```python
import functools
import math

import jax
import jax.numpy as jnp
from jax import lax
from jax.experimental import pallas as pl
from jax.experimental.pallas import tpu as pltpu
from jax.sharding import Mesh, PartitionSpec as P

D = 2048
HEADS = 32
KV_HEADS = 4
HEAD_DIM = 64
FF = 5632
LENGTH = 2048
MIDDLE = 1920
EPSILON = 1e-05
THETA = 10000.0
NEG_LARGE = -1e30

AXES = ("zl", "y", "zh", "x", "core")
Z_RING = ("zl", "zh")
GROUP = 8
TOK = 128
HALF = GROUP * TOK
CHUNK = D // GROUP
FF_OWN = FF // GROUP
Q_OWN = HEADS * HEAD_DIM // GROUP
HEADS_OWN = HEADS // GROUP
SUB = FF_OWN // GROUP
OUT_SUB = Q_OWN // GROUP
KEY_CHUNK = 256
ROWS_Q = HEADS_OWN * TOK

F32 = jnp.float32
BF16 = jnp.bfloat16


def ring(values, axis, step):
    if axis == Z_RING:
        spot = [(z % 2) * 2 + z // 2 for z in range(4)]
        return lax.ppermute(values, axis, [(spot[z], spot[(z + step) % 4]) for z in range(4)])
    count = lax.axis_size(axis)
    return lax.ppermute(values, axis, [(i, (i + step) % count) for i in range(count)])


def place_kernel(copies, places, *refs):
    pieces, out, sems = refs[:-2], refs[-2], refs[-1]
    running = [
        pltpu.make_async_copy(
            pieces[piece].at[pl.ds(start, count)], out.at[pl.ds(places[i], count)], sems.at[i]
        )
        for i, (piece, start, count) in enumerate(copies)
    ]
    for copy in running:
        copy.start()
    for copy in running:
        copy.wait()


def cost(microseconds):
    return pl.CostEstimate(
        flops=int(microseconds * 1e9), bytes_accessed=int(microseconds * 3e6), transcendentals=0
    )


def put_in_place(places, pieces, copies, total):
    return pl.pallas_call(
        functools.partial(place_kernel, copies),
        grid_spec=pltpu.PrefetchScalarGridSpec(
            num_scalar_prefetch=1,
            grid=(1,),
            in_specs=[pl.BlockSpec(piece.shape, lambda i, places: (0, 0, 0)) for piece in pieces],
            out_specs=pl.BlockSpec(memory_space=pl.ANY),
            scratch_shapes=[pltpu.SemaphoreType.DMA((len(copies),))],
        ),
        out_shape=jax.ShapeDtypeStruct((total, *pieces[0].shape[1:]), pieces[0].dtype),
        compiler_params=pltpu.CompilerParams(vmem_limit_bytes=32 * 1024 * 1024),
        cost_estimate=cost(1),
        name="put_in_place",
    )(places, *pieces)


def near(block, axis):
    return ring(block, axis, -1), ring(block, axis, 1)


def far(ahead, behind, axis):
    half = ahead.shape[0] // 2
    return ring(ahead[:half], axis, -1), ring(behind[half:], axis, 1)


def across_z(own, ahead, behind, far_low, far_high):
    return (
        ring(jnp.concatenate([own, ahead]), Z_RING, 1),
        ring(jnp.concatenate([behind, far_low, far_high]), Z_RING, -1),
    )


def put_weights(blocks, z_blocks, zl, y):
    rows, columns = blocks[0].shape
    unit = rows // 2
    pieces = [block.reshape(-1, unit, columns) for block in (*blocks, *z_blocks)]
    copies = [(0, 0, 2), (1, 0, 2), (2, 0, 2), (3, 0, 1), (4, 0, 1)]
    copies += [(5, 0, 2), (5, 2, 2), (6, 0, 2), (6, 2, 2)]
    step = [(y + q) % 4 * 2 for q in range(4)]
    mine, other = zl * 8, (1 - zl) * 8
    places = [mine + step[0], mine + step[1], mine + step[3], mine + step[2], mine + step[2] + 1]
    places += [other + step[0], other + step[1], other + step[3], other + step[2]]
    places = jnp.stack(places).astype(jnp.int32)
    return put_in_place(places, pieces, copies, 16).reshape(8 * rows, columns)


def halves_kernel(copies, places, *refs):
    pieces, out, sems = refs[:-2], refs[-2], refs[-1]
    width = pieces[0].shape[-1]
    running = [
        pltpu.make_async_copy(
            pieces[piece].at[unit],
            out.at[places[i], :, pl.ds(unit % 2 * width, width)],
            sems.at[i],
        )
        for i, (piece, unit) in enumerate(copies)
    ]
    for copy in running:
        copy.start()
    for copy in running:
        copy.wait()


def stack_halves(block):
    half = block.shape[1] // 2
    return jnp.concatenate([block[:, :half], block[:, half:]])


def both_parities(own):
    half = own.shape[0] // 2
    return ring(own[:half], Z_RING, 1), ring(own[half:], Z_RING, -1)


def pair_places(zl, y):
    steps = [(y + q) % 4 for q in (0, 1, 3, 2)]
    return [[zl * 4 + at, (1 - zl) * 4 + at] for at in steps]


def put_pairs(pair, near_pairs, far_pair, zl, y):
    rows, columns = far_pair[0].shape
    pieces = [block.reshape(-1, rows, columns) for block in (pair, *near_pairs, *far_pair)]
    copies = [(i, u, 1) for i in range(3) for u in range(2)] + [(3, 0, 1), (4, 0, 1)]
    places = jnp.stack(sum(pair_places(zl, y), [])).astype(jnp.int32)
    return put_in_place(places, pieces, copies, 8).reshape(8 * rows, columns)


def put_row_pairs(pair, near_pairs, far_pair, zl, y):
    rows, columns = far_pair[0].shape
    unit = rows // 2
    pieces = [block.reshape(-1, unit, columns) for block in (pair, *near_pairs, *far_pair)]
    copies = [(i, u) for i in range(3) for u in range(4)]
    copies += [(i, u) for i in (3, 4) for u in range(2)]
    places = sum([[at, at] for spots in pair_places(zl, y) for at in spots], [])
    places = jnp.stack(places).astype(jnp.int32)
    return pl.pallas_call(
        functools.partial(halves_kernel, copies),
        grid_spec=pltpu.PrefetchScalarGridSpec(
            num_scalar_prefetch=1,
            grid=(1,),
            in_specs=[pl.BlockSpec(piece.shape, lambda i, places: (0, 0, 0)) for piece in pieces],
            out_specs=pl.BlockSpec(memory_space=pl.ANY),
            scratch_shapes=[pltpu.SemaphoreType.DMA((len(copies),))],
        ),
        out_shape=jax.ShapeDtypeStruct((8, unit, 2 * columns), BF16),
        compiler_params=pltpu.CompilerParams(vmem_limit_bytes=32 * 1024 * 1024),
        cost_estimate=cost(1),
        name="put_rows",
    )(places, *pieces).reshape(8 * unit, 2 * columns)


def put_rows(blocks, blocks_two, group_places):
    rows, columns = blocks[0].shape
    unit = rows // 2
    pieces = [block.reshape(-1, unit, columns) for block in (*blocks, *blocks_two)]
    copies = [(0, 0, 2), (1, 0, 2), (2, 0, 2), (3, 0, 1), (4, 0, 1)]
    copies += [(5, 0, 2), (6, 0, 2), (6, 2, 2), (7, 0, 2)]
    spots = [2 * group_places[i] for i in (0, 1, 3, 2, 2, 4, 5, 7, 6)]
    spots[4] = spots[4] + 1
    return put_in_place(jnp.stack(spots), pieces, copies, 2 * GROUP).reshape(
        GROUP * rows, columns
    )


def swap_blocks(own, ahead, behind, far_low, far_high):
    return (
        ring(own, "core", 1),
        ring(jnp.concatenate([ahead, behind]), "core", 1),
        ring(jnp.concatenate([far_low, far_high]), "core", 1),
    )


def scatter_z(pairs):
    return ring(pairs[0], Z_RING, 1), ring(pairs[1], Z_RING, -1)


def chunk_for_y(own, arrived, y, step):
    at = (y + step) % 4
    more = jnp.where(
        at < 2,
        lax.dynamic_index_in_dim(arrived[0], at & 1, 0, keepdims=False),
        lax.dynamic_index_in_dim(arrived[1], at & 1, 0, keepdims=False),
    )
    here = lax.dynamic_index_in_dim(own, at, 0, keepdims=False)
    return here.astype(F32) + more.astype(F32)


def chunks_for_y(own, arrived, y):
    return [chunk_for_y(own, arrived, y, 0)] + [
        chunk_for_y(own, arrived, y, step).astype(BF16) for step in (1, 2, 3)
    ]


def far_along_y(own, arrived, y):
    block = chunk_for_y(own, arrived, y, 2).astype(BF16)
    half = block.shape[0] // 2
    return ring(block[:half], "y", 1), ring(block[half:], "y", -1)


def near_along_y(own, arrived, first, y):
    ahead, behind = chunk_for_y(own, arrived, y, 1), chunk_for_y(own, arrived, y, 3)
    half = ahead.shape[0] // 2
    ahead = jnp.concatenate([ahead[:half] + first[0].astype(F32), ahead[half:]])
    behind = jnp.concatenate([behind[:half], behind[half:] + first[1].astype(F32)])
    return (
        chunk_for_y(own, arrived, y, 0),
        ring(ahead.astype(BF16), "y", 1),
        ring(behind.astype(BF16), "y", -1),
    )


def send_along_y(chunks):
    return [chunks[0]] + [ring(chunks[step], "y", step) for step in (1, 2, 3)]


def scatter_y(own, arrived, y):
    return send_along_y(chunks_for_y(own, arrived, y))


def scatter_zh(parts):
    total = add_up(parts).astype(BF16)
    return total, ring(total, "zh", 1)


def both_halves(pair):
    return add_up(pair).astype(BF16)


def rows_to_core(partial, core):
    partial = partial.astype(BF16).reshape(4, 2, TOK, D)

    def of_core(at):
        return lax.dynamic_index_in_dim(partial, at, 1, keepdims=False)

    return of_core(core), ring(of_core(1 - core), "core", 1)


def rows_along_x(total, x):
    def chunk(step):
        return lax.dynamic_index_in_dim(total, (x + step) % 4, 0, keepdims=False)

    far = ring(chunk(2).astype(BF16), "x", 2)
    ahead = ring(chunk(1).astype(BF16), "x", 1)
    behind = ring(chunk(3).astype(BF16), "x", -1)
    return chunk(0), ahead, behind, far


def exchange_x(blocks, x):
    def chunk(step):
        return lax.dynamic_index_in_dim(blocks, (x + step) % 4, 0, keepdims=False)

    return [chunk(0)] + [ring(chunk(step), "x", step) for step in (1, 2, 3)]


def put_exchanged(parts, others, x, core):
    rows = parts[0].shape[1]
    pieces = [*parts, others]
    copies, places = [], []
    for r in range(4):
        at = (x - r) % 4 * 2
        for tokens in range(2):
            copies += [(r, tokens, 1), (4, 2 * r + tokens, 1)]
            places += [tokens * GROUP + at + core, tokens * GROUP + at + 1 - core]
    places = jnp.stack(places).astype(jnp.int32)
    return put_in_place(places, pieces, copies, 2 * GROUP).reshape(2, GROUP, rows, TOK)


def far_rows_along_x(total, x):
    block = lax.dynamic_index_in_dim(total, (x + 2) % 4, 0, keepdims=False).astype(BF16)
    half = block.shape[0] // 2
    return ring(block[:half], "x", 1), ring(block[half:], "x", -1)


def near_rows_along_x(total, first, x):
    def chunk(step):
        return lax.dynamic_index_in_dim(total, (x + step) % 4, 0, keepdims=False)

    ahead, behind = chunk(1), chunk(3)
    half = ahead.shape[0] // 2
    ahead = jnp.concatenate([ahead[:half] + first[0].astype(F32), ahead[half:]])
    behind = jnp.concatenate([behind[:half], behind[half:] + first[1].astype(F32)])
    return chunk(0), ring(ahead.astype(BF16), "x", 1), ring(behind.astype(BF16), "x", -1)


def add_up(parts):
    return sum(part.astype(F32) for part in parts)


def rail_of(block):
    return [block, ring(block, "x", -1), ring(block, "x", 2), ring(block, "x", 1)]


def with_other_core(rail):
    return rail + [ring(part, "core", 1) for part in rail]


def swap_roles(values):
    return lax.ppermute(
        values,
        ("zl", "y", "x", "core"),
        [(a * GROUP + b, b * GROUP + a) for a in range(GROUP) for b in range(GROUP)],
    )


def after(values, *others):
    return lax.optimization_barrier((values, *others))[0]


def join(*groups):
    return lax.optimization_barrier(groups)


def heads_side_by_side(block):
    return jnp.concatenate(
        [block[i * HEAD_DIM : (i + 1) * HEAD_DIM] for i in range(HEADS_OWN)], axis=1
    )


def heads_stacked(block):
    return jnp.concatenate(
        [block[:, i * TOK : (i + 1) * TOK] for i in range(HEADS_OWN)], axis=0
    )


def allowed_keys(meta, j, start):
    half_at, head_end = meta[0], meta[1]
    shape = (KEY_CHUNK, ROWS_Q)
    column = lax.broadcasted_iota(jnp.int32, (1, ROWS_Q), 1)
    query = half_at * HALF + j * TOK + (column & (TOK - 1))
    first = jnp.where(
        query < head_end,
        0,
        jnp.where(query < head_end + MIDDLE, head_end, head_end + MIDDLE),
    )
    key = lax.broadcasted_iota(jnp.int32, shape, 0) + start + (half_at - 1) * HALF
    return (key <= query) & (key >= first)


def mask_scores(scores, meta, j, start, masked):
    parts = []
    for i in range(scores.shape[0] // KEY_CHUNK):
        part = scores[i * KEY_CHUNK : (i + 1) * KEY_CHUNK]
        if i in masked:
            part = jnp.where(allowed_keys(meta, j, start + i * KEY_CHUNK), part, NEG_LARGE)
        parts.append(part)
    return jnp.concatenate(parts) if len(parts) > 1 else parts[0]


def for_visible_keys(meta, j, step):
    chunks = HALF // KEY_CHUNK
    final = j == GROUP - 1

    @pl.when((meta[0] == 1) & jnp.logical_not(final))
    def _():
        step(0, HALF, (0,))

    @pl.when((meta[0] == 1) & final)
    def _():
        step(0, HALF, tuple(range(chunks)))

    for last in range(chunks):

        @pl.when((j * TOK // KEY_CHUNK == last) & jnp.logical_not(final))
        def _(last=last):
            step(HALF, (last + 1) * KEY_CHUNK, (0, last))

    @pl.when(final)
    def _():
        step(HALF, HALF, tuple(range(chunks)))


def dot_kn(left, right):
    return jnp.dot(left, right, preferred_element_type=F32)


def dot_nt(left, right):
    return lax.dot_general(
        left, right, (((1,), (1,)), ((), ())), preferred_element_type=F32
    )


def forward_kernel(
    meta, q_ref, kt_ref, vt_ref, out_ref, mixed_ref, lse_ref, k_ref, v_ref, top_ref, acc_ref
):
    j = pl.program_id(0)

    @pl.when(j == 0)
    def _():
        k_ref[...] = kt_ref[...].astype(F32).T.astype(BF16)
        row = lax.broadcasted_iota(jnp.int32, (V_ROWS - HEAD_DIM, 2 * HALF), 0)
        v_ref[:HEAD_DIM, :] = vt_ref[...]
        v_ref[HEAD_DIM:, :] = jnp.where(row == 0, 1.0, 0.0).astype(BF16)

    query = heads_side_by_side(q_ref[...])
    top_ref[...] = jnp.full_like(top_ref, NEG_LARGE)
    acc_ref[...] = jnp.zeros_like(acc_ref)

    def step(start, size, masked):
        rows = slice(start, start + size)
        scores = mask_scores(dot_kn(k_ref[rows, :], query), meta, j, start, masked)
        old = top_ref[...]
        new = jnp.maximum(old, jnp.max(scores, axis=0, keepdims=True))
        weights = jnp.exp(scores - new).astype(BF16)
        acc_ref[...] = acc_ref[...] * jnp.exp(old - new) + dot_kn(v_ref[:, rows], weights)
        top_ref[...] = new

    for_visible_keys(meta, j, step)
    total = acc_ref[HEAD_DIM : HEAD_DIM + 1, :]
    attended = heads_stacked(acc_ref[:HEAD_DIM, :] / total)
    out_ref[0] = attended
    mixed_ref[0] = attended.astype(BF16)
    lse_ref[...] = jnp.broadcast_to(top_ref[...] + jnp.log(total), lse_ref.shape)


def minus_rows(values):
    rows, rest = [], -values
    for _ in range(3):
        rows.append(rest.astype(BF16).astype(F32))
        rest = rest - rows[-1]
    zeros = jnp.zeros((EXTRA - 3, values.shape[1]), F32)
    return jnp.concatenate([*rows, zeros]).astype(BF16)


def backward_kernel(
    meta,
    q_ref,
    g_ref,
    o_ref,
    lse_ref,
    kt_ref,
    vt_ref,
    *rest,
    begin,
):
    dq_ref, dk_ref, dv_ref, k_ref, v_ref, acc_ref = rest[-6:]
    j = pl.program_id(0) + begin

    @pl.when(pl.program_id(0) == 0)
    def _():
        row = lax.broadcasted_iota(jnp.int32, (EXTRA, 2 * HALF), 0)
        ones = jnp.where(row < 3, 1.0, 0.0)
        k_ref[...] = jnp.concatenate([kt_ref[...].astype(F32), ones]).T.astype(BF16)
        v_ref[...] = jnp.concatenate([vt_ref[...].astype(F32), ones]).T.astype(BF16)
        if begin:
            dk_ref[...] = rest[0][...]
            dv_ref[...] = rest[1][...]
        else:
            dk_ref[...] = jnp.zeros_like(dk_ref)
            dv_ref[...] = jnp.zeros_like(dv_ref)

    query = heads_side_by_side(q_ref[...])
    grad = heads_side_by_side(g_ref[0])
    mixed = heads_side_by_side(o_ref[0])
    delta = jnp.sum(grad.astype(F32) * mixed, axis=0, keepdims=True)
    query_less = jnp.concatenate([query, minus_rows(lse_ref[0:1, :])])
    grad_less = jnp.concatenate([grad, minus_rows(delta)])
    acc_ref[...] = jnp.zeros_like(acc_ref)

    def step(start, size, masked):
        rows = slice(start, start + size)
        scores = mask_scores(dot_kn(k_ref[rows, :], query_less), meta, j, start, masked)
        probs = jnp.exp(scores)
        grad_scores = (probs * dot_kn(v_ref[rows, :], grad_less)).astype(BF16)
        acc_ref[...] += dot_kn(kt_ref[:, rows], grad_scores)
        dk_ref[:, rows] += dot_nt(query, grad_scores)
        dv_ref[:, rows] += dot_nt(grad, probs.astype(BF16))

    for_visible_keys(meta, j, step)
    dq_ref[0] = heads_stacked(acc_ref[...] * (1.0 / math.sqrt(HEAD_DIM)))


def whole(shape):
    return pl.BlockSpec(shape, lambda j, meta: (0,) * len(shape))


def token_block(rows):
    return pl.BlockSpec((rows, TOK), lambda j, meta: (0, j))


V_ROWS = 80
EXTRA = 16
LSE_ROWS = 8


def attend(meta, query_t, keys_t, values_t):
    return pl.pallas_call(
        forward_kernel,
        grid_spec=pltpu.PrefetchScalarGridSpec(
            num_scalar_prefetch=1,
            grid=(GROUP,),
            in_specs=[
                token_block(Q_OWN),
                whole((HEAD_DIM, 2 * HALF)),
                whole((HEAD_DIM, 2 * HALF)),
            ],
            out_specs=[
                pl.BlockSpec((1, Q_OWN, TOK), lambda j, meta: (j, 0, 0)),
                pl.BlockSpec((1, Q_OWN, TOK), lambda j, meta: (j, 0, 0)),
                pl.BlockSpec((LSE_ROWS, ROWS_Q), lambda j, meta: (j, 0)),
            ],
            scratch_shapes=[
                pltpu.VMEM((2 * HALF, HEAD_DIM), BF16),
                pltpu.VMEM((V_ROWS, 2 * HALF), BF16),
                pltpu.VMEM((1, ROWS_Q), F32),
                pltpu.VMEM((V_ROWS, ROWS_Q), F32),
            ],
        ),
        out_shape=[
            jax.ShapeDtypeStruct((GROUP, Q_OWN, TOK), F32),
            jax.ShapeDtypeStruct((GROUP, Q_OWN, TOK), BF16),
            jax.ShapeDtypeStruct((GROUP * LSE_ROWS, ROWS_Q), F32),
        ],
        compiler_params=pltpu.CompilerParams(vmem_limit_bytes=32 * 1024 * 1024),
        cost_estimate=cost(1),
        name="attend",
    )(meta, query_t, keys_t, values_t)


def attend_back(meta, begin, end, query_t, grad_t, attn_t, lse, keys_t, values_t, *sums):
    block = pl.BlockSpec((1, Q_OWN, TOK), lambda j, meta: (j + begin, 0, 0))
    return pl.pallas_call(
        functools.partial(backward_kernel, begin=begin),
        grid_spec=pltpu.PrefetchScalarGridSpec(
            num_scalar_prefetch=1,
            grid=(end - begin,),
            in_specs=[
                pl.BlockSpec((Q_OWN, TOK), lambda j, meta: (0, j + begin)),
                block,
                block,
                pl.BlockSpec((LSE_ROWS, ROWS_Q), lambda j, meta: (j + begin, 0)),
            ]
            + [whole((HEAD_DIM, 2 * HALF))] * (2 + len(sums)),
            out_specs=[
                pl.BlockSpec((1, Q_OWN, TOK), lambda j, meta: (j, 0, 0)),
                whole((HEAD_DIM, 2 * HALF)),
                whole((HEAD_DIM, 2 * HALF)),
            ],
            scratch_shapes=[
                pltpu.VMEM((2 * HALF, HEAD_DIM + EXTRA), BF16),
                pltpu.VMEM((2 * HALF, HEAD_DIM + EXTRA), BF16),
                pltpu.VMEM((HEAD_DIM, ROWS_Q), F32),
            ],
        ),
        out_shape=[
            jax.ShapeDtypeStruct((end - begin, Q_OWN, TOK), F32),
            jax.ShapeDtypeStruct((HEAD_DIM, 2 * HALF), F32),
            jax.ShapeDtypeStruct((HEAD_DIM, 2 * HALF), F32),
        ],
        compiler_params=pltpu.CompilerParams(vmem_limit_bytes=32 * 1024 * 1024),
        cost_estimate=cost(1),
        name="attend_back",
    )(meta, query_t, grad_t, attn_t, lse, keys_t, values_t, *sums)


def norm_kernel(places, *refs):
    (own, ahead, behind, low, high, own_two, near_two, far_two, weights) = refs[:9]
    normed_out, gains_out, gains = refs[9:]
    i = pl.program_id(0)

    @pl.when(i == 0)
    def _():
        gains[...] = weights[...].astype(F32).T[HEAD_DIM : HEAD_DIM + 8, :]
        gains_out[...] = gains[...]

    def norm(block, start, size, to):
        values = block[start : start + size, :].astype(F32)
        scale = lax.rsqrt(jnp.mean(values * values, axis=-1, keepdims=True) + EPSILON)
        normed_out[to : to + size, :] = (values * scale * gains[0:1, :]).astype(BF16)

    sources = [
        [(own, 0)],
        [(ahead, 0)],
        [(low, 0), (high, 0)],
        [(behind, 0)],
        [(own_two, 0)],
        [(near_two, 0)],
        [(far_two, 0)],
        [(near_two, TOK)],
    ]
    for at, parts in enumerate(sources):

        @pl.when(i == at)
        def _(parts=parts):
            size = TOK // len(parts)
            for k, (block, start) in enumerate(parts):
                norm(block, start, size, k * size)


def gather_norm(places, pieces, early_all):
    rows = [pl.BlockSpec(piece.shape, lambda i, places: (0, 0)) for piece in pieces]
    placed = pl.BlockSpec((TOK, D), lambda i, places: (places[i], 0))
    return pl.pallas_call(
        norm_kernel,
        grid_spec=pltpu.PrefetchScalarGridSpec(
            num_scalar_prefetch=1,
            grid=(GROUP,),
            in_specs=rows + [pl.BlockSpec((D, 128), lambda i, places: (0, 2))],
            out_specs=[
                placed,
                pl.BlockSpec((8, D), lambda i, places: (0, 0)),
            ],
            scratch_shapes=[pltpu.VMEM((8, D), F32)],
        ),
        out_shape=[
            jax.ShapeDtypeStruct((HALF, D), BF16),
            jax.ShapeDtypeStruct((8, D), F32),
        ],
        compiler_params=pltpu.CompilerParams(vmem_limit_bytes=32 * 1024 * 1024),
        cost_estimate=cost(1),
        name="gather_norm",
    )(places, *pieces, early_all)


def take_kernel(own, gate, up, out):
    for at in range(GROUP):

        @pl.when(own[0] == at)
        def _():
            parts = []
            for ref in (gate, up):
                for block in range(GROUP):
                    start = block * FF_OWN + at * SUB
                    low = start // 128 * 128
                    window = ref[:, low : low + 256].astype(F32)
                    parts.append(window[:, start - low : start - low + SUB])
            out[...] = jnp.concatenate(parts, axis=1).astype(BF16)


def take_columns(own, gate, up):
    rows = 64
    return pl.pallas_call(
        take_kernel,
        grid_spec=pltpu.PrefetchScalarGridSpec(
            num_scalar_prefetch=1,
            grid=(CHUNK // rows,),
            in_specs=[pl.BlockSpec((rows, FF), lambda i, own: (i, 0))] * 2,
            out_specs=pl.BlockSpec((rows, 2 * FF_OWN), lambda i, own: (i, 0)),
        ),
        out_shape=jax.ShapeDtypeStruct((CHUNK, 2 * FF_OWN), BF16),
        compiler_params=pltpu.CompilerParams(vmem_limit_bytes=32 * 1024 * 1024),
        cost_estimate=cost(1),
        name="take_columns",
    )(own, gate, up)


def gate_up_kernel(pieces, w_gate, w_up, gate, up, products):
    total = 0.0
    for which, (weight, out) in enumerate(((w_gate, gate), (w_up, up))):
        parts = []
        for block in range(GROUP):
            start = which * FF_OWN + block * SUB
            low = start // 128 * 128
            size = min(256, 2 * FF_OWN - low)
            for at in range(GROUP):
                window = pieces[at, :, low : low + size].astype(F32)
                parts.append(window[:, start - low : start - low + SUB])
        values = jnp.concatenate(parts, axis=1)
        out[...] = values
        total = total + jnp.sum(values * weight[...].astype(F32), axis=1, keepdims=True)
    products[...] = jnp.broadcast_to(total, products.shape)


def put_gate_up(pieces, w_gate, w_up):
    rows = 64
    row_block = pl.BlockSpec((rows, FF), lambda i: (i, 0))
    return pl.pallas_call(
        gate_up_kernel,
        grid=(CHUNK // rows,),
        in_specs=[
            pl.BlockSpec((GROUP, rows, 2 * FF_OWN), lambda i: (0, i, 0)),
            row_block,
            row_block,
        ],
        out_specs=[row_block, row_block, pl.BlockSpec((rows, 128), lambda i: (i, 0))],
        out_shape=[
            jax.ShapeDtypeStruct((CHUNK, FF), F32),
            jax.ShapeDtypeStruct((CHUNK, FF), F32),
            jax.ShapeDtypeStruct((CHUNK, 128), F32),
        ],
        compiler_params=pltpu.CompilerParams(vmem_limit_bytes=48 * 1024 * 1024),
        cost_estimate=cost(1),
        name="gate_up",
    )(pieces.reshape(GROUP, CHUNK, 2 * FF_OWN), w_gate, w_up)


def down_out_kernel(rows, down, out):
    values = rows[...].astype(F32)
    down[...] = values[:SUB]
    out[...] = values[SUB:]


def split_down_out(rows):
    return pl.pallas_call(
        down_out_kernel,
        grid=(GROUP,),
        in_specs=[pl.BlockSpec((SUB + OUT_SUB, D), lambda i: (i, 0))],
        out_specs=[
            pl.BlockSpec((SUB, D), lambda i: (i, 0)),
            pl.BlockSpec((OUT_SUB, D), lambda i: (i, 0)),
        ],
        out_shape=[
            jax.ShapeDtypeStruct((FF_OWN, D), F32),
            jax.ShapeDtypeStruct((Q_OWN, D), F32),
        ],
        compiler_params=pltpu.CompilerParams(vmem_limit_bytes=32 * 1024 * 1024),
        cost_estimate=cost(1),
        name="down_out",
    )(rows)


def qkv_kernel(places, *refs):
    pieces, weights, outs, products, stack = refs[:8], refs[8:11], refs[11:14], *refs[14:]
    query, key, value = outs
    for i, piece in enumerate(pieces):
        stack[places[i]] = piece[...]
    for at in range(GROUP):
        values = stack[at].astype(F32)
        query[:, at * Q_OWN : (at + 1) * Q_OWN] = values[:, :Q_OWN]
        head = key if at % 2 == 0 else value
        place = (at // 2) * HEAD_DIM
        head[:, place : place + HEAD_DIM] = values[:, Q_OWN : Q_OWN + HEAD_DIM]
    total = sum(
        jnp.sum(out[...] * weight[...].astype(F32), axis=1, keepdims=True)
        for out, weight in zip(outs, weights, strict=True)
    )
    products[...] = jnp.broadcast_to(total, (CHUNK, 128)).T[:8]


def assemble(kernel, places, pieces, rows, weights, shapes):
    count, width = pieces[0].shape
    return pl.pallas_call(
        kernel,
        grid_spec=pltpu.PrefetchScalarGridSpec(
            num_scalar_prefetch=1,
            grid=(count // rows,),
            in_specs=[pl.BlockSpec((rows, width), lambda i, places: (i, 0))] * 8
            + [pl.BlockSpec((rows, w.shape[1]), lambda i, places: (i, 0)) for w in weights],
            out_specs=[
                pl.BlockSpec((block, columns), lambda i, places: (i, 0))
                for _, block, columns in shapes
            ],
            scratch_shapes=[pltpu.VMEM((GROUP, rows, width), BF16)],
        ),
        out_shape=[jax.ShapeDtypeStruct((whole, columns), F32) for whole, _, columns in shapes],
        compiler_params=pltpu.CompilerParams(vmem_limit_bytes=48 * 1024 * 1024),
        cost_estimate=cost(1),
        name=kernel.__name__.removesuffix("_kernel"),
    )(places, *pieces, *weights)


def rms_scale(values):
    return lax.rsqrt(jnp.mean(values * values, axis=-1, keepdims=True) + EPSILON)


def rotate_t(values, cosine, sine_table):
    half = HEAD_DIM // 2
    first, second = values[:, :half], values[:, half:]
    return jnp.concatenate(
        [first * cosine - second * sine_table, second * cosine + first * sine_table], axis=1
    )


def norm_back(grad_normed, values, scale_rows, gain_full):
    unit_rows = values * scale_rows
    grad_unit = grad_normed * gain_full
    return scale_rows * (
        grad_unit - unit_rows * jnp.mean(grad_unit * unit_rows, axis=-1, keepdims=True)
    )


def contract(form, left, right):
    return jnp.einsum(form, left, right, preferred_element_type=F32)


def shards(
    inputs,
    positions,
    cotangent,
    w_query,
    w_key,
    w_value,
    w_out,
    w_gate,
    w_up,
    w_down,
    gain_attn,
    gain_mlp,
):
    zl, y, zh, x, core = (lax.axis_index(axis) for axis in AXES)
    xc = x * 2 + core
    group = ("x", "core")

    def gather_rows(rows):
        return lax.all_gather(rows, group, axis=0, tiled=True)

    inputs_near = near(inputs, "x")
    inputs_two = ring(inputs, "core", 1)

    index_here = (zh * GROUP + xc) * TOK + jnp.arange(TOK, dtype=jnp.int32)
    head_end = jnp.where(
        (zh == 0) & (xc == 0),
        jnp.sum((positions == index_here).astype(jnp.int32)),
        index_here[0] - positions[0],
    )
    meta = jnp.stack([zh, head_end]).astype(jnp.int32)
    rail = [((x + r) % 4) * 2 for r in range(4)]
    group_places = jnp.stack(
        [at + core for at in rail] + [at + 1 - core for at in rail]
    ).astype(jnp.int32)
    def columns(weight, width):
        return lax.dynamic_slice_in_dim(weight, xc * width, width, axis=1)

    kv_here = jnp.where(core == 0, w_key, w_value)
    kv_here = lax.dynamic_slice_in_dim(kv_here, x * HEAD_DIM, HEAD_DIM, axis=1)
    early = jnp.concatenate(
        [
            columns(w_query, Q_OWN),
            kv_here,
            gain_attn[:, None],
            gain_mlp[:, None],
            jnp.zeros((CHUNK, 62), BF16),
        ],
        axis=1,
    )
    early_near = near(early, "y")
    gate_up_here = take_columns(xc[None].astype(jnp.int32), w_gate, w_up)
    half_width = D // 2
    out_here = lax.dynamic_slice_in_dim(w_out, core * half_width, half_width, axis=1)
    down_here = stack_halves(lax.dynamic_slice_in_dim(w_down, xc * SUB, SUB, axis=0))
    early_blocks = (early, *early_near, *far(*early_near, "y"))
    early_blocks, inputs_near, out_here = join(early_blocks, inputs_near, out_here)
    early_z = across_z(*early_blocks)
    inputs_far = far(*inputs_near, "x")
    out_near = near(out_here, "y")
    early_z, inputs_far, inputs_two, gate_up_here = join(
        early_z, inputs_far, inputs_two, gate_up_here
    )
    inputs_rest = (
        ring(jnp.concatenate(inputs_near), "core", 1),
        ring(jnp.concatenate(inputs_far), "core", 1),
    )
    full_qkv_gains = put_weights(early_blocks, early_z, zl, y)
    full_qkv_gains, inputs_rest, out_near = join(full_qkv_gains, inputs_rest, out_near)
    out_far = far(*out_near, "y")
    gate_up_other = both_parities(gate_up_here)
    normed, gains = gather_norm(
        group_places,
        [inputs, *inputs_near, *inputs_far, inputs_two, *inputs_rest],
        full_qkv_gains,
    )
    full_qkv = full_qkv_gains[:, : Q_OWN + HEAD_DIM]
    full_gain_attn, full_gain_mlp = gains[0], gains[1]

    index_all = zh * HALF + jnp.arange(HALF, dtype=jnp.int32)
    doc_start = jnp.where(
        index_all < head_end,
        0,
        jnp.where(index_all < head_end + MIDDLE, head_end, head_end + MIDDLE),
    )
    frequency = THETA ** (-(jnp.arange(HEAD_DIM // 2, dtype=F32) * 2.0 / HEAD_DIM))
    angles = frequency[:, None] * (index_all - doc_start).astype(F32)[None, :]
    cosine, sine_table = jnp.cos(angles), jnp.sin(angles)
    is_key = core == 0
    cosine_kv = jnp.where(is_key, cosine, 1.0)
    sine_kv = jnp.where(is_key, sine_table, 0.0)

    raw_t = contract("dn,td->nt", full_qkv, normed)
    query_t = (
        rotate_t(raw_t[:Q_OWN].reshape(HEADS_OWN, HEAD_DIM, HALF), cosine, sine_table)
        .reshape(Q_OWN, HALF)
        .astype(BF16)
        * (1.0 / math.sqrt(HEAD_DIM))
    ).astype(BF16)
    kv_t = rotate_t(raw_t[Q_OWN:][None], cosine_kv, sine_kv)[0].astype(BF16)
    kv_other = ring(kv_t, "core", 1)
    kv_prev = lax.ppermute(kv_t, "zh", [(0, 1)])
    kv_prev_other = lax.ppermute(kv_t, ("zh", "core"), [(0, 3), (1, 2)])
    kv_t, kv_other, kv_prev, kv_prev_other, query_t, gate_up_here, gate_up_other, out_far = join(
        kv_t, kv_other, kv_prev, kv_prev_other, query_t, gate_up_here, gate_up_other, out_far
    )
    mine = jnp.concatenate([kv_prev, kv_t], axis=1)
    theirs = jnp.concatenate([kv_prev_other, kv_other], axis=1)
    keys_t = jnp.where(is_key, mine, theirs)
    values_t = jnp.where(is_key, theirs, mine)
    out_blocks = (out_here, *out_near, *out_far)
    gate_up_pair = jnp.concatenate([gate_up_here, *gate_up_other])
    gate_up_near = near(gate_up_pair, "y")
    out_z = across_z(*out_blocks)
    attended = attend(meta, query_t, keys_t, values_t)
    (attn_t, mixed_t, lse), out_z, gate_up_near = join(attended, out_z, gate_up_near)
    mixed_parts = exchange_x(mixed_t.reshape(4, 2, Q_OWN, TOK), x)
    gate_up_far = far(*gate_up_near, "y")
    out_half = put_weights(out_blocks, out_z, zl, y)
    mixed_parts, out_half = join(mixed_parts, out_half)
    mixed_others = ring(jnp.concatenate(mixed_parts), "core", 1)
    mixed_others, mixed_parts = join(mixed_others, mixed_parts)
    mixed_both = put_exchanged(mixed_parts, mixed_others, x, core)

    def of_core(values, at):
        return lax.dynamic_index_in_dim(values, at, 0, keepdims=False)

    out_rows = contract("ckt,kd->ctd", mixed_both.reshape(2, D, TOK), out_half).astype(BF16)
    out_mine = of_core(out_rows, core)
    out_theirs = ring(of_core(out_rows, 1 - core), "core", 1)
    out_theirs, down_here, cotangent_here = join(out_theirs, down_here, cotangent)
    tokens_here = inputs.astype(F32)
    residual = tokens_here + jnp.concatenate(
        [
            jnp.where(core == 0, out_mine, out_theirs),
            jnp.where(core == 0, out_theirs, out_mine),
        ],
        axis=1,
    ).astype(F32)
    scale_mlp = rms_scale(residual)
    normed_rows = (residual * scale_mlp * full_gain_mlp).astype(BF16)
    normed_mlp = gather_rows(normed_rows)
    down_other = both_parities(down_here)
    cotangent_near = near(cotangent_here, "x")
    down_other, cotangent_near, gate_up_far = join(down_other, cotangent_near, gate_up_far)
    down_pair = jnp.concatenate([down_here, *down_other])
    down_near = near(down_pair, "y")
    cotangent_far = far(*cotangent_near, "x")
    gate_up_all = put_pairs(gate_up_pair, gate_up_near, gate_up_far, zl, y)
    normed_mlp, gate_up_all, down_near, cotangent_far = join(
        normed_mlp, gate_up_all, down_near, cotangent_far
    )

    gate_up = contract("td,df->tf", normed_mlp, gate_up_all)
    down_far = far(*down_near, "y")
    cotangent_blocks = (cotangent_here, *cotangent_near, *cotangent_far)
    cotangent_two = swap_blocks(*cotangent_blocks)
    gate_up, down_far, cotangent_two = join(gate_up, down_far, cotangent_two)
    cotangent_all = put_rows(cotangent_blocks, cotangent_two, group_places)
    full_down = put_row_pairs(down_pair, down_near, down_far, zl, y)
    grad_hidden = contract("td,fd->tf", cotangent_all, full_down)
    gate, upward = gate_up[:, :FF_OWN], gate_up[:, FF_OWN:]
    sigmoid_gate = jax.nn.sigmoid(gate)
    silu_gate = gate * sigmoid_gate
    hidden = (silu_gate * upward).astype(BF16)
    grad_acts = jnp.concatenate(
        [
            (grad_hidden * upward * sigmoid_gate * (1.0 + gate * (1.0 - sigmoid_gate))).astype(BF16),
            (grad_hidden * silu_gate).astype(BF16),
        ],
        axis=1,
    )
    back_rows = rows_to_core(contract("tf,df->td", grad_acts, gate_up_all), core)

    def columns_at(values, start, count):
        return lax.dynamic_slice_in_dim(values, start * CHUNK, count * CHUNK, axis=1)

    other = (1 - zl) * 4

    def gate_up_product(start, count):
        rows = contract("td,tf->df", columns_at(normed_mlp, start, count), grad_acts)
        return rows.astype(BF16).reshape(count, CHUNK, 2 * FF_OWN)

    gate_up_theirs = gate_up_product(other, 4)
    back_total = back_rows[0].astype(F32) + back_rows[1].astype(F32)
    back_total, gate_up_pairs, hidden, normed_mlp, grad_acts = join(
        back_total, (gate_up_theirs[:2], gate_up_theirs[2:]), hidden, normed_mlp, grad_acts
    )
    back_rows = rows_along_x(back_total, x)
    gate_up_z = scatter_z(gate_up_pairs)
    gate_up_mine = gate_up_product(zl * 4, 4)
    part_down = contract("tf,td->fd", hidden, cotangent_all).astype(BF16)
    part_down = part_down.reshape(8, SUB, D)
    part_output = contract("tf,fd->td", hidden, full_down).astype(BF16)
    back_rows, gate_up_z, gate_up_mine, part_down, part_output = join(
        back_rows, gate_up_z, gate_up_mine, part_down, part_output
    )
    gate_up_far = far_along_y(gate_up_mine, gate_up_z, y)
    grad_normed_mlp = add_up(back_rows)
    grad_residual = cotangent.astype(F32) + norm_back(
        grad_normed_mlp, residual, scale_mlp, full_gain_mlp
    )
    grad_here = grad_residual.astype(BF16)
    grad_theirs = ring(grad_here, "core", 1)
    grad_theirs, grad_here, gate_up_mine, gate_up_z = join(
        grad_theirs, grad_here, gate_up_mine, gate_up_z
    )
    grad_both = jnp.stack(
        [jnp.where(core == 0, grad_here, grad_theirs), jnp.where(core == 0, grad_theirs, grad_here)]
    )
    grad_both = jnp.where(core == 0, grad_both[..., :half_width], grad_both[..., half_width:])
    grad_partial = contract("kd,ctd->kct", out_half, grad_both).reshape(4, 2, Q_OWN, 2, TOK)

    def heads_of(at):
        return lax.dynamic_index_in_dim(grad_partial, at, 1, keepdims=False)

    grad_arrived = ring(heads_of(1 - core).astype(BF16), "core", 1)
    grad_arrived, gate_up_far = join(grad_arrived, gate_up_far)
    grad_heads = (heads_of(core) + grad_arrived.astype(F32)).astype(BF16)
    grad_parts = exchange_x(grad_heads.transpose(0, 2, 1, 3), x)
    grad_attn_out = gather_rows(grad_here)
    gate_up_y = near_along_y(gate_up_mine, gate_up_z, gate_up_far, y)
    grad_parts, gate_up_y, part_output = join(grad_parts, gate_up_y, part_output)
    output_rows = lax.psum_scatter(part_output, group, scatter_dimension=0, tiled=True)
    gate_up_zh = scatter_zh(gate_up_y)
    places = jnp.stack([(x - r) % 4 * 2 for r in range(4)]).astype(jnp.int32)
    grad_mixed_t = put_in_place(places, grad_parts, [(r, 0, 2) for r in range(4)], GROUP)
    back_args = (query_t, grad_mixed_t, attn_t, lse, keys_t, values_t)
    attended = attend_back(meta, 0, 4, *back_args)
    (query_0, *key_sums), gate_up_zh, grad_attn_out = join(attended, gate_up_zh, grad_attn_out)
    shard_gate_up = both_halves(gate_up_zh)
    part_out = contract(
        "bkt,btd->kd", mixed_t, grad_attn_out.reshape(GROUP, TOK, D)
    ).astype(BF16)
    part_down_out = jnp.concatenate([part_down, part_out.reshape(8, OUT_SUB, D)], axis=1)

    def chunks(start, count):
        return lax.dynamic_slice_in_dim(part_down_out, start, count, axis=0)

    down_out_pairs = (chunks(other, 2), chunks(other + 2, 2))
    down_out_pairs, key_sums = join(down_out_pairs, key_sums)
    down_out_z = scatter_z(down_out_pairs)
    attended = attend_back(meta, 4, 8, *back_args, *key_sums)
    (query_1, grad_keys_t, grad_values_t), down_out_z, output_rows, shard_gate_up = join(
        attended, down_out_z, output_rows, shard_gate_up
    )
    gate_up_grads = gather_rows(shard_gate_up)
    grad_query_t = jnp.concatenate([query_0, query_1])

    kept = jnp.where(is_key, grad_keys_t, grad_values_t)
    given = jnp.where(is_key, grad_values_t, grad_keys_t)
    arrived = ring(given.astype(BF16), "core", 1)
    arrived, kept, grad_query_t = join(arrived, kept, grad_query_t)
    grad_kv = kept + arrived.astype(F32)
    from_next = lax.ppermute(grad_kv[:, :HALF].astype(BF16), "zh", [(1, 0)])
    from_next, grad_kv, grad_query_t = join(from_next, grad_kv, grad_query_t)
    down_out_y = scatter_y(chunks(zl * 4, 4), down_out_z, y)
    grad_kv_t = grad_kv[:, HALF:] + from_next.astype(F32)

    def by_block(table):
        return table.reshape(-1, GROUP, TOK).transpose(1, 0, 2)

    half_head = HEAD_DIM // 2
    cosine_b, sine_b = by_block(cosine)[:, None], by_block(sine_table)[:, None]
    first = grad_query_t.reshape(GROUP, HEADS_OWN, HEAD_DIM, TOK)[:, :, :half_head]
    second = grad_query_t.reshape(GROUP, HEADS_OWN, HEAD_DIM, TOK)[:, :, half_head:]
    turned = jnp.concatenate(
        [first * cosine_b + second * sine_b, second * cosine_b - first * sine_b], axis=2
    ).reshape(GROUP, Q_OWN, TOK)
    grad_qkv = jnp.concatenate(
        [turned, by_block(rotate_t(grad_kv_t[None], cosine_kv, -sine_kv)[0])], axis=1
    ).astype(BF16)
    grad_qkv_rows = grad_qkv.transpose(0, 2, 1).reshape(HALF, Q_OWN + HEAD_DIM)
    part_normed = contract("tn,dn->td", grad_qkv_rows, full_qkv).astype(BF16)

    def qkv_product(start, count):
        rows = contract("td,tn->dn", columns_at(normed, start, count), grad_qkv_rows)
        return rows.astype(BF16).reshape(count, CHUNK, Q_OWN + HEAD_DIM)

    qkv_pairs = [qkv_product(other, 2), qkv_product(other + 2, 2)]
    normed_pair = rows_to_core(part_normed, core)
    normed_pair, qkv_pairs, grad_qkv_rows = join(normed_pair, qkv_pairs, grad_qkv_rows)
    qkv_z = scatter_z(qkv_pairs)
    qkv_mine = qkv_product(zl * 4, 4)
    normed_total = normed_pair[0].astype(F32) + normed_pair[1].astype(F32)
    qkv_z, qkv_mine, down_out_y, normed_total = join(qkv_z, qkv_mine, down_out_y, normed_total)
    qkv_y = scatter_y(qkv_mine, qkv_z, y)
    normed_first = far_rows_along_x(normed_total, x)
    down_out_zh = scatter_zh(down_out_y)
    qkv_y, down_out_zh, normed_total, normed_first, gate_up_grads = join(
        qkv_y, down_out_zh, normed_total, normed_first, gate_up_grads
    )
    qkv_zh = scatter_zh(qkv_y)
    normed_parts = near_rows_along_x(normed_total, normed_first, x)
    shard_down_out = both_halves(down_out_zh)
    turned_out = swap_roles(shard_down_out[SUB:])
    qkv_zh, turned_out, normed_parts, gate_up_grads = join(
        qkv_zh, turned_out, normed_parts, gate_up_grads
    )
    grad_gate, grad_up, mlp_products = put_gate_up(gate_up_grads, w_gate, w_up)
    down_out_all = gather_rows(jnp.concatenate([shard_down_out[:SUB], turned_out]))
    qkv_rail = rail_of(both_halves(qkv_zh))
    grad_normed = add_up(normed_parts)
    output = (residual + output_rows.astype(F32)).astype(BF16)
    scale_here = rms_scale(tokens_here)
    grad_inputs = grad_residual + norm_back(grad_normed, tokens_here, scale_here, full_gain_attn)

    grad_down, grad_out = split_down_out(down_out_all)
    kv_columns = KV_HEADS * HEAD_DIM
    grad_query, grad_key, grad_value, attn_products = assemble(
        qkv_kernel,
        group_places,
        with_other_core(qkv_rail),
        CHUNK,
        [w_query, w_key, w_value],
        [
            (CHUNK, CHUNK, HEADS * HEAD_DIM),
            (CHUNK, CHUNK, kv_columns),
            (CHUNK, CHUNK, kv_columns),
            (8, 8, CHUNK),
        ],
    )
    return (
        output,
        grad_inputs,
        grad_query,
        grad_key,
        grad_value,
        grad_out,
        grad_gate,
        grad_up,
        grad_down,
        attn_products[0] / gain_attn.astype(F32),
        mlp_products[:, 0] / gain_mlp.astype(F32),
    )


def solution(mesh):
    split = Mesh(mesh.devices.reshape(2, 4, 2, 4, 2), AXES)
    dp, tokens = ("zl", "y"), AXES
    matrix = P(dp, None)
    return jax.shard_map(
        shards,
        mesh=split,
        in_specs=(
            P(tokens, None),
            P(tokens),
            P(tokens, None),
            matrix,
            matrix,
            matrix,
            matrix,
            matrix,
            matrix,
            matrix,
            P(dp),
            P(dp),
        ),
        out_specs=(
            P(tokens, None),
            P(tokens, None),
            matrix,
            matrix,
            matrix,
            matrix,
            matrix,
            matrix,
            matrix,
            P(dp),
            P(dp),
        ),
        check_vma=False,
    )
```

```python
import functools
import math

import jax
import jax.numpy as jnp
from jax import lax
from jax.experimental import pallas as pl
from jax.experimental.pallas import tpu as pltpu
from jax.sharding import Mesh, PartitionSpec as P

D = 2048
HEADS = 32
KV_HEADS = 4
HEAD_DIM = 64
FF = 5632
LENGTH = 2048
MIDDLE = 1920
EPSILON = 1e-05
THETA = 10000.0
NEG_LARGE = -1e30

AXES = ("zl", "y", "zh", "x", "core")
Z_RING = ("zl", "zh")
GROUP = 8
TOK = 128
HALF = GROUP * TOK
CHUNK = D // GROUP
FF_OWN = FF // GROUP
Q_OWN = HEADS * HEAD_DIM // GROUP
HEADS_OWN = HEADS // GROUP
SUB = FF_OWN // GROUP
OUT_SUB = Q_OWN // GROUP
KEY_CHUNK = 256
ROWS_Q = HEADS_OWN * TOK

F32 = jnp.float32
BF16 = jnp.bfloat16


def ring(values, axis, step):
    if axis == Z_RING:
        spot = [(z % 2) * 2 + z // 2 for z in range(4)]
        return lax.ppermute(values, axis, [(spot[z], spot[(z + step) % 4]) for z in range(4)])
    count = lax.axis_size(axis)
    return lax.ppermute(values, axis, [(i, (i + step) % count) for i in range(count)])


def place_kernel(copies, places, *refs):
    pieces, out, sems = refs[:-2], refs[-2], refs[-1]
    running = [
        pltpu.make_async_copy(
            pieces[piece].at[pl.ds(start, count)], out.at[pl.ds(places[i], count)], sems.at[i]
        )
        for i, (piece, start, count) in enumerate(copies)
    ]
    for copy in running:
        copy.start()
    for copy in running:
        copy.wait()


def cost(microseconds):
    return pl.CostEstimate(
        flops=int(microseconds * 1e9), bytes_accessed=int(microseconds * 3e6), transcendentals=0
    )


def put_in_place(places, pieces, copies, total):
    return pl.pallas_call(
        functools.partial(place_kernel, copies),
        grid_spec=pltpu.PrefetchScalarGridSpec(
            num_scalar_prefetch=1,
            grid=(1,),
            in_specs=[pl.BlockSpec(piece.shape, lambda i, places: (0, 0, 0)) for piece in pieces],
            out_specs=pl.BlockSpec(memory_space=pl.ANY),
            scratch_shapes=[pltpu.SemaphoreType.DMA((len(copies),))],
        ),
        out_shape=jax.ShapeDtypeStruct((total, *pieces[0].shape[1:]), pieces[0].dtype),
        compiler_params=pltpu.CompilerParams(vmem_limit_bytes=32 * 1024 * 1024),
        cost_estimate=cost(1),
        name="put_in_place",
    )(places, *pieces)


def near(block, axis):
    return ring(block, axis, -1), ring(block, axis, 1)


def far(ahead, behind, axis):
    half = ahead.shape[0] // 2
    return ring(ahead[:half], axis, -1), ring(behind[half:], axis, 1)


def across_z(own, ahead, behind, far_low, far_high):
    return (
        ring(jnp.concatenate([own, ahead]), Z_RING, 1),
        ring(jnp.concatenate([behind, far_low, far_high]), Z_RING, -1),
    )


def put_weights(blocks, z_blocks, zl, y):
    rows, columns = blocks[0].shape
    unit = rows // 2
    pieces = [block.reshape(-1, unit, columns) for block in (*blocks, *z_blocks)]
    copies = [(0, 0, 2), (1, 0, 2), (2, 0, 2), (3, 0, 1), (4, 0, 1)]
    copies += [(5, 0, 2), (5, 2, 2), (6, 0, 2), (6, 2, 2)]
    step = [(y + q) % 4 * 2 for q in range(4)]
    mine, other = zl * 8, (1 - zl) * 8
    places = [mine + step[0], mine + step[1], mine + step[3], mine + step[2], mine + step[2] + 1]
    places += [other + step[0], other + step[1], other + step[3], other + step[2]]
    places = jnp.stack(places).astype(jnp.int32)
    return put_in_place(places, pieces, copies, 16).reshape(8 * rows, columns)


def halves_kernel(copies, places, *refs):
    pieces, out, sems = refs[:-2], refs[-2], refs[-1]
    width = pieces[0].shape[-1]
    running = [
        pltpu.make_async_copy(
            pieces[piece].at[unit],
            out.at[places[i], :, pl.ds(unit % 2 * width, width)],
            sems.at[i],
        )
        for i, (piece, unit) in enumerate(copies)
    ]
    for copy in running:
        copy.start()
    for copy in running:
        copy.wait()


def stack_halves(block):
    half = block.shape[1] // 2
    return jnp.concatenate([block[:, :half], block[:, half:]])


def both_parities(own):
    half = own.shape[0] // 2
    return ring(own[:half], Z_RING, 1), ring(own[half:], Z_RING, -1)


def pair_places(zl, y):
    steps = [(y + q) % 4 for q in (0, 1, 3, 2)]
    return [[zl * 4 + at, (1 - zl) * 4 + at] for at in steps]


def put_pairs(pair, near_pairs, far_pair, zl, y):
    rows, columns = far_pair[0].shape
    pieces = [block.reshape(-1, rows, columns) for block in (pair, *near_pairs, *far_pair)]
    copies = [(i, u, 1) for i in range(3) for u in range(2)] + [(3, 0, 1), (4, 0, 1)]
    places = jnp.stack(sum(pair_places(zl, y), [])).astype(jnp.int32)
    return put_in_place(places, pieces, copies, 8).reshape(8 * rows, columns)


def put_row_pairs(pair, near_pairs, far_pair, zl, y):
    rows, columns = far_pair[0].shape
    unit = rows // 2
    pieces = [block.reshape(-1, unit, columns) for block in (pair, *near_pairs, *far_pair)]
    copies = [(i, u) for i in range(3) for u in range(4)]
    copies += [(i, u) for i in (3, 4) for u in range(2)]
    places = sum([[at, at] for spots in pair_places(zl, y) for at in spots], [])
    places = jnp.stack(places).astype(jnp.int32)
    return pl.pallas_call(
        functools.partial(halves_kernel, copies),
        grid_spec=pltpu.PrefetchScalarGridSpec(
            num_scalar_prefetch=1,
            grid=(1,),
            in_specs=[pl.BlockSpec(piece.shape, lambda i, places: (0, 0, 0)) for piece in pieces],
            out_specs=pl.BlockSpec(memory_space=pl.ANY),
            scratch_shapes=[pltpu.SemaphoreType.DMA((len(copies),))],
        ),
        out_shape=jax.ShapeDtypeStruct((8, unit, 2 * columns), BF16),
        compiler_params=pltpu.CompilerParams(vmem_limit_bytes=32 * 1024 * 1024),
        cost_estimate=cost(1),
        name="put_rows",
    )(places, *pieces).reshape(8 * unit, 2 * columns)


def put_rows(blocks, blocks_two, group_places):
    rows, columns = blocks[0].shape
    unit = rows // 2
    pieces = [block.reshape(-1, unit, columns) for block in (*blocks, *blocks_two)]
    copies = [(0, 0, 2), (1, 0, 2), (2, 0, 2), (3, 0, 1), (4, 0, 1)]
    copies += [(5, 0, 2), (6, 0, 2), (6, 2, 2), (7, 0, 2)]
    spots = [2 * group_places[i] for i in (0, 1, 3, 2, 2, 4, 5, 7, 6)]
    spots[4] = spots[4] + 1
    return put_in_place(jnp.stack(spots), pieces, copies, 2 * GROUP).reshape(
        GROUP * rows, columns
    )


def swap_blocks(own, ahead, behind, far_low, far_high):
    return (
        ring(own, "core", 1),
        ring(jnp.concatenate([ahead, behind]), "core", 1),
        ring(jnp.concatenate([far_low, far_high]), "core", 1),
    )


def scatter_z(pairs):
    return ring(pairs[0], Z_RING, 1), ring(pairs[1], Z_RING, -1)


def chunk_for_y(own, arrived, y, step):
    at = (y + step) % 4
    more = jnp.where(
        at < 2,
        lax.dynamic_index_in_dim(arrived[0], at & 1, 0, keepdims=False),
        lax.dynamic_index_in_dim(arrived[1], at & 1, 0, keepdims=False),
    )
    here = lax.dynamic_index_in_dim(own, at, 0, keepdims=False)
    return here.astype(F32) + more.astype(F32)


def chunks_for_y(own, arrived, y):
    return [chunk_for_y(own, arrived, y, 0)] + [
        chunk_for_y(own, arrived, y, step).astype(BF16) for step in (1, 2, 3)
    ]


def far_along_y(own, arrived, y):
    block = chunk_for_y(own, arrived, y, 2).astype(BF16)
    half = block.shape[0] // 2
    return ring(block[:half], "y", 1), ring(block[half:], "y", -1)


def near_along_y(own, arrived, first, y):
    ahead, behind = chunk_for_y(own, arrived, y, 1), chunk_for_y(own, arrived, y, 3)
    half = ahead.shape[0] // 2
    ahead = jnp.concatenate([ahead[:half] + first[0].astype(F32), ahead[half:]])
    behind = jnp.concatenate([behind[:half], behind[half:] + first[1].astype(F32)])
    return (
        chunk_for_y(own, arrived, y, 0),
        ring(ahead.astype(BF16), "y", 1),
        ring(behind.astype(BF16), "y", -1),
    )


def send_along_y(chunks):
    return [chunks[0]] + [ring(chunks[step], "y", step) for step in (1, 2, 3)]


def scatter_y(own, arrived, y):
    return send_along_y(chunks_for_y(own, arrived, y))


def scatter_zh(parts):
    total = add_up(parts).astype(BF16)
    return total, ring(total, "zh", 1)


def both_halves(pair):
    return add_up(pair).astype(BF16)


def rows_to_core(partial, core):
    partial = partial.astype(BF16).reshape(4, 2, TOK, D)

    def of_core(at):
        return lax.dynamic_index_in_dim(partial, at, 1, keepdims=False)

    return of_core(core), ring(of_core(1 - core), "core", 1)


def rows_along_x(total, x):
    def chunk(step):
        return lax.dynamic_index_in_dim(total, (x + step) % 4, 0, keepdims=False)

    far = ring(chunk(2).astype(BF16), "x", 2)
    ahead = ring(chunk(1).astype(BF16), "x", 1)
    behind = ring(chunk(3).astype(BF16), "x", -1)
    return chunk(0), ahead, behind, far


def exchange_x(blocks, x):
    def chunk(step):
        return lax.dynamic_index_in_dim(blocks, (x + step) % 4, 0, keepdims=False)

    return [chunk(0)] + [ring(chunk(step), "x", step) for step in (1, 2, 3)]


def put_exchanged(parts, others, x, core):
    rows = parts[0].shape[1]
    pieces = [*parts, others]
    copies, places = [], []
    for r in range(4):
        at = (x - r) % 4 * 2
        for tokens in range(2):
            copies += [(r, tokens, 1), (4, 2 * r + tokens, 1)]
            places += [tokens * GROUP + at + core, tokens * GROUP + at + 1 - core]
    places = jnp.stack(places).astype(jnp.int32)
    return put_in_place(places, pieces, copies, 2 * GROUP).reshape(2, GROUP, rows, TOK)


def far_rows_along_x(total, x):
    block = lax.dynamic_index_in_dim(total, (x + 2) % 4, 0, keepdims=False).astype(BF16)
    half = block.shape[0] // 2
    return ring(block[:half], "x", 1), ring(block[half:], "x", -1)


def near_rows_along_x(total, first, x):
    def chunk(step):
        return lax.dynamic_index_in_dim(total, (x + step) % 4, 0, keepdims=False)

    ahead, behind = chunk(1), chunk(3)
    half = ahead.shape[0] // 2
    ahead = jnp.concatenate([ahead[:half] + first[0].astype(F32), ahead[half:]])
    behind = jnp.concatenate([behind[:half], behind[half:] + first[1].astype(F32)])
    return chunk(0), ring(ahead.astype(BF16), "x", 1), ring(behind.astype(BF16), "x", -1)


def add_up(parts):
    return sum(part.astype(F32) for part in parts)


def rail_of(block):
    return [block, ring(block, "x", -1), ring(block, "x", 2), ring(block, "x", 1)]


def with_other_core(rail):
    return rail + [ring(part, "core", 1) for part in rail]


def swap_roles(values):
    return lax.ppermute(
        values,
        ("zl", "y", "x", "core"),
        [(a * GROUP + b, b * GROUP + a) for a in range(GROUP) for b in range(GROUP)],
    )


def after(values, *others):
    return lax.optimization_barrier((values, *others))[0]


def join(*groups):
    return lax.optimization_barrier(groups)


def heads_side_by_side(block):
    return jnp.concatenate(
        [block[i * HEAD_DIM : (i + 1) * HEAD_DIM] for i in range(HEADS_OWN)], axis=1
    )


def heads_stacked(block):
    return jnp.concatenate(
        [block[:, i * TOK : (i + 1) * TOK] for i in range(HEADS_OWN)], axis=0
    )


def allowed_keys(meta, j, start):
    half_at, head_end = meta[0], meta[1]
    shape = (KEY_CHUNK, ROWS_Q)
    column = lax.broadcasted_iota(jnp.int32, (1, ROWS_Q), 1)
    query = half_at * HALF + j * TOK + (column & (TOK - 1))
    first = jnp.where(
        query < head_end,
        0,
        jnp.where(query < head_end + MIDDLE, head_end, head_end + MIDDLE),
    )
    key = lax.broadcasted_iota(jnp.int32, shape, 0) + start + (half_at - 1) * HALF
    return (key <= query) & (key >= first)


def mask_scores(scores, meta, j, start, masked):
    parts = []
    for i in range(scores.shape[0] // KEY_CHUNK):
        part = scores[i * KEY_CHUNK : (i + 1) * KEY_CHUNK]
        if i in masked:
            part = jnp.where(allowed_keys(meta, j, start + i * KEY_CHUNK), part, NEG_LARGE)
        parts.append(part)
    return jnp.concatenate(parts) if len(parts) > 1 else parts[0]


def for_visible_keys(meta, j, step):
    chunks = HALF // KEY_CHUNK
    final = j == GROUP - 1

    @pl.when((meta[0] == 1) & jnp.logical_not(final))
    def _():
        step(0, HALF, (0,))

    @pl.when((meta[0] == 1) & final)
    def _():
        step(0, HALF, tuple(range(chunks)))

    for last in range(chunks):

        @pl.when((j * TOK // KEY_CHUNK == last) & jnp.logical_not(final))
        def _(last=last):
            step(HALF, (last + 1) * KEY_CHUNK, (0, last))

    @pl.when(final)
    def _():
        step(HALF, HALF, tuple(range(chunks)))


def dot_kn(left, right):
    return jnp.dot(left, right, preferred_element_type=F32)


def dot_nt(left, right):
    return lax.dot_general(
        left, right, (((1,), (1,)), ((), ())), preferred_element_type=F32
    )


def forward_kernel(
    meta, q_ref, kt_ref, vt_ref, out_ref, mixed_ref, lse_ref, k_ref, v_ref, top_ref, acc_ref
):
    j = pl.program_id(0)

    @pl.when(j == 0)
    def _():
        k_ref[...] = kt_ref[...].astype(F32).T.astype(BF16)
        row = lax.broadcasted_iota(jnp.int32, (V_ROWS - HEAD_DIM, 2 * HALF), 0)
        v_ref[:HEAD_DIM, :] = vt_ref[...]
        v_ref[HEAD_DIM:, :] = jnp.where(row == 0, 1.0, 0.0).astype(BF16)

    query = heads_side_by_side(q_ref[...])
    chunks = HALF // KEY_CHUNK
    final = j == GROUP - 1
    every = tuple(range(chunks))

    def scores_of(start, size, masked):
        rows = slice(start, start + size)
        return mask_scores(dot_kn(k_ref[rows, :], query), meta, j, start, masked)

    def finish(parts):
        top = functools.reduce(
            jnp.maximum, [jnp.max(scores, axis=0, keepdims=True) for _, scores in parts]
        )
        acc = 0.0
        for start, scores in parts:
            rows = slice(start, start + scores.shape[0])
            acc = acc + dot_kn(v_ref[:, rows], jnp.exp(scores - top).astype(BF16))
        acc_ref[...] = acc
        top_ref[...] = top

    for last in range(chunks + 1):
        size = min(last + 1, chunks) * KEY_CHUNK
        whole_mask = last == chunks
        here = final if whole_mask else (j * TOK // KEY_CHUNK == last) & jnp.logical_not(final)
        masked = every if whole_mask else (0, last)

        @pl.when(here & (meta[0] == 1))
        def _(size=size, masked=masked, whole_mask=whole_mask):
            earlier = scores_of(0, HALF, every if whole_mask else (0,))
            finish([(0, earlier), (HALF, scores_of(HALF, size, masked))])

        @pl.when(here & (meta[0] == 0))
        def _(size=size, masked=masked):
            finish([(HALF, scores_of(HALF, size, masked))])

    total = acc_ref[HEAD_DIM : HEAD_DIM + 1, :]
    attended = heads_stacked(acc_ref[:HEAD_DIM, :] / total)
    out_ref[0] = attended
    mixed_ref[0] = attended.astype(BF16)
    lse_ref[...] = jnp.broadcast_to(top_ref[...] + jnp.log(total), lse_ref.shape)


def minus_rows(values):
    rows, rest = [], -values
    for _ in range(3):
        rows.append(rest.astype(BF16).astype(F32))
        rest = rest - rows[-1]
    zeros = jnp.zeros((EXTRA - 3, values.shape[1]), F32)
    return jnp.concatenate([*rows, zeros]).astype(BF16)


def backward_kernel(
    meta,
    q_ref,
    g_ref,
    o_ref,
    lse_ref,
    kt_ref,
    vt_ref,
    *rest,
    begin,
):
    dq_ref, dk_ref, dv_ref, k_ref, v_ref, acc_ref = rest[-6:]
    j = pl.program_id(0) + begin

    @pl.when(pl.program_id(0) == 0)
    def _():
        row = lax.broadcasted_iota(jnp.int32, (EXTRA, 2 * HALF), 0)
        ones = jnp.where(row < 3, 1.0, 0.0)
        k_ref[...] = jnp.concatenate([kt_ref[...].astype(F32), ones]).T.astype(BF16)
        v_ref[...] = jnp.concatenate([vt_ref[...].astype(F32), ones]).T.astype(BF16)
        if begin:
            dk_ref[...] = rest[0][...]
            dv_ref[...] = rest[1][...]
        else:
            dk_ref[...] = jnp.zeros_like(dk_ref)
            dv_ref[...] = jnp.zeros_like(dv_ref)

    query = heads_side_by_side(q_ref[...])
    grad = heads_side_by_side(g_ref[0])
    mixed = heads_side_by_side(o_ref[0])
    delta = jnp.sum(grad.astype(F32) * mixed, axis=0, keepdims=True)
    query_less = jnp.concatenate([query, minus_rows(lse_ref[0:1, :])])
    grad_less = jnp.concatenate([grad, minus_rows(delta)])
    acc_ref[...] = jnp.zeros_like(acc_ref)

    def step(start, size, masked):
        rows = slice(start, start + size)
        scores = mask_scores(dot_kn(k_ref[rows, :], query_less), meta, j, start, masked)
        probs = jnp.exp(scores)
        grad_scores = (probs * dot_kn(v_ref[rows, :], grad_less)).astype(BF16)
        acc_ref[...] += dot_kn(kt_ref[:, rows], grad_scores)
        dk_ref[:, rows] += dot_nt(query, grad_scores)
        dv_ref[:, rows] += dot_nt(grad, probs.astype(BF16))

    for_visible_keys(meta, j, step)
    dq_ref[0] = heads_stacked(acc_ref[...] * (1.0 / math.sqrt(HEAD_DIM)))


def whole(shape):
    return pl.BlockSpec(shape, lambda j, meta: (0,) * len(shape))


def token_block(rows):
    return pl.BlockSpec((rows, TOK), lambda j, meta: (0, j))


V_ROWS = 80
EXTRA = 16
LSE_ROWS = 8


def attend(meta, query_t, keys_t, values_t):
    return pl.pallas_call(
        forward_kernel,
        grid_spec=pltpu.PrefetchScalarGridSpec(
            num_scalar_prefetch=1,
            grid=(GROUP,),
            in_specs=[
                token_block(Q_OWN),
                whole((HEAD_DIM, 2 * HALF)),
                whole((HEAD_DIM, 2 * HALF)),
            ],
            out_specs=[
                pl.BlockSpec((1, Q_OWN, TOK), lambda j, meta: (j, 0, 0)),
                pl.BlockSpec((1, Q_OWN, TOK), lambda j, meta: (j, 0, 0)),
                pl.BlockSpec((LSE_ROWS, ROWS_Q), lambda j, meta: (j, 0)),
            ],
            scratch_shapes=[
                pltpu.VMEM((2 * HALF, HEAD_DIM), BF16),
                pltpu.VMEM((V_ROWS, 2 * HALF), BF16),
                pltpu.VMEM((1, ROWS_Q), F32),
                pltpu.VMEM((V_ROWS, ROWS_Q), F32),
            ],
        ),
        out_shape=[
            jax.ShapeDtypeStruct((GROUP, Q_OWN, TOK), F32),
            jax.ShapeDtypeStruct((GROUP, Q_OWN, TOK), BF16),
            jax.ShapeDtypeStruct((GROUP * LSE_ROWS, ROWS_Q), F32),
        ],
        compiler_params=pltpu.CompilerParams(vmem_limit_bytes=32 * 1024 * 1024),
        cost_estimate=cost(1),
        name="attend",
    )(meta, query_t, keys_t, values_t)


def attend_back(meta, begin, end, query_t, grad_t, attn_t, lse, keys_t, values_t, *sums):
    block = pl.BlockSpec((1, Q_OWN, TOK), lambda j, meta: (j + begin, 0, 0))
    return pl.pallas_call(
        functools.partial(backward_kernel, begin=begin),
        grid_spec=pltpu.PrefetchScalarGridSpec(
            num_scalar_prefetch=1,
            grid=(end - begin,),
            in_specs=[
                pl.BlockSpec((Q_OWN, TOK), lambda j, meta: (0, j + begin)),
                block,
                block,
                pl.BlockSpec((LSE_ROWS, ROWS_Q), lambda j, meta: (j + begin, 0)),
            ]
            + [whole((HEAD_DIM, 2 * HALF))] * (2 + len(sums)),
            out_specs=[
                pl.BlockSpec((1, Q_OWN, TOK), lambda j, meta: (j, 0, 0)),
                whole((HEAD_DIM, 2 * HALF)),
                whole((HEAD_DIM, 2 * HALF)),
            ],
            scratch_shapes=[
                pltpu.VMEM((2 * HALF, HEAD_DIM + EXTRA), BF16),
                pltpu.VMEM((2 * HALF, HEAD_DIM + EXTRA), BF16),
                pltpu.VMEM((HEAD_DIM, ROWS_Q), F32),
            ],
        ),
        out_shape=[
            jax.ShapeDtypeStruct((end - begin, Q_OWN, TOK), F32),
            jax.ShapeDtypeStruct((HEAD_DIM, 2 * HALF), F32),
            jax.ShapeDtypeStruct((HEAD_DIM, 2 * HALF), F32),
        ],
        compiler_params=pltpu.CompilerParams(vmem_limit_bytes=32 * 1024 * 1024),
        cost_estimate=cost(1),
        name="attend_back",
    )(meta, query_t, grad_t, attn_t, lse, keys_t, values_t, *sums)


def norm_kernel(places, *refs):
    (own, ahead, behind, low, high, own_two, near_two, far_two, weights) = refs[:9]
    normed_out, gains_out, gains = refs[9:]
    i = pl.program_id(0)

    @pl.when(i == 0)
    def _():
        gains[...] = weights[...].astype(F32).T[HEAD_DIM : HEAD_DIM + 8, :]
        gains_out[...] = gains[...]

    def norm(block, start, size, to):
        values = block[start : start + size, :].astype(F32)
        scale = lax.rsqrt(jnp.mean(values * values, axis=-1, keepdims=True) + EPSILON)
        normed_out[to : to + size, :] = (values * scale * gains[0:1, :]).astype(BF16)

    sources = [
        [(own, 0)],
        [(ahead, 0)],
        [(low, 0), (high, 0)],
        [(behind, 0)],
        [(own_two, 0)],
        [(near_two, 0)],
        [(far_two, 0)],
        [(near_two, TOK)],
    ]
    for at, parts in enumerate(sources):

        @pl.when(i == at)
        def _(parts=parts):
            size = TOK // len(parts)
            for k, (block, start) in enumerate(parts):
                norm(block, start, size, k * size)


def gather_norm(places, pieces, early_all):
    rows = [pl.BlockSpec(piece.shape, lambda i, places: (0, 0)) for piece in pieces]
    placed = pl.BlockSpec((TOK, D), lambda i, places: (places[i], 0))
    return pl.pallas_call(
        norm_kernel,
        grid_spec=pltpu.PrefetchScalarGridSpec(
            num_scalar_prefetch=1,
            grid=(GROUP,),
            in_specs=rows + [pl.BlockSpec((D, 128), lambda i, places: (0, 2))],
            out_specs=[
                placed,
                pl.BlockSpec((8, D), lambda i, places: (0, 0)),
            ],
            scratch_shapes=[pltpu.VMEM((8, D), F32)],
        ),
        out_shape=[
            jax.ShapeDtypeStruct((HALF, D), BF16),
            jax.ShapeDtypeStruct((8, D), F32),
        ],
        compiler_params=pltpu.CompilerParams(vmem_limit_bytes=32 * 1024 * 1024),
        cost_estimate=cost(1),
        name="gather_norm",
    )(places, *pieces, early_all)


def take_kernel(own, gate, up, out):
    for at in range(GROUP):

        @pl.when(own[0] == at)
        def _():
            parts = []
            for ref in (gate, up):
                for block in range(GROUP):
                    start = block * FF_OWN + at * SUB
                    low = start // 128 * 128
                    window = ref[:, low : low + 256].astype(F32)
                    parts.append(window[:, start - low : start - low + SUB])
            out[...] = jnp.concatenate(parts, axis=1).astype(BF16)


def take_columns(own, gate, up):
    rows = 64
    return pl.pallas_call(
        take_kernel,
        grid_spec=pltpu.PrefetchScalarGridSpec(
            num_scalar_prefetch=1,
            grid=(CHUNK // rows,),
            in_specs=[pl.BlockSpec((rows, FF), lambda i, own: (i, 0))] * 2,
            out_specs=pl.BlockSpec((rows, 2 * FF_OWN), lambda i, own: (i, 0)),
        ),
        out_shape=jax.ShapeDtypeStruct((CHUNK, 2 * FF_OWN), BF16),
        compiler_params=pltpu.CompilerParams(vmem_limit_bytes=32 * 1024 * 1024),
        cost_estimate=cost(1),
        name="take_columns",
    )(own, gate, up)


def gate_up_kernel(pieces, w_gate, w_up, gate, up, products):
    total = 0.0
    for which, (weight, out) in enumerate(((w_gate, gate), (w_up, up))):
        parts = []
        for block in range(GROUP):
            start = which * FF_OWN + block * SUB
            low = start // 128 * 128
            size = min(256, 2 * FF_OWN - low)
            for at in range(GROUP):
                window = pieces[at, :, low : low + size].astype(F32)
                parts.append(window[:, start - low : start - low + SUB])
        values = jnp.concatenate(parts, axis=1)
        out[...] = values
        total = total + jnp.sum(values * weight[...].astype(F32), axis=1, keepdims=True)
    products[...] = jnp.broadcast_to(total, products.shape)


def put_gate_up(pieces, w_gate, w_up):
    rows = 64
    row_block = pl.BlockSpec((rows, FF), lambda i: (i, 0))
    return pl.pallas_call(
        gate_up_kernel,
        grid=(CHUNK // rows,),
        in_specs=[
            pl.BlockSpec((GROUP, rows, 2 * FF_OWN), lambda i: (0, i, 0)),
            row_block,
            row_block,
        ],
        out_specs=[row_block, row_block, pl.BlockSpec((rows, 128), lambda i: (i, 0))],
        out_shape=[
            jax.ShapeDtypeStruct((CHUNK, FF), F32),
            jax.ShapeDtypeStruct((CHUNK, FF), F32),
            jax.ShapeDtypeStruct((CHUNK, 128), F32),
        ],
        compiler_params=pltpu.CompilerParams(vmem_limit_bytes=48 * 1024 * 1024),
        cost_estimate=cost(1),
        name="gate_up",
    )(pieces.reshape(GROUP, CHUNK, 2 * FF_OWN), w_gate, w_up)


def down_out_kernel(rows, down, out):
    values = rows[...].astype(F32)
    down[...] = values[:SUB]
    out[...] = values[SUB:]


def split_down_out(rows):
    return pl.pallas_call(
        down_out_kernel,
        grid=(GROUP,),
        in_specs=[pl.BlockSpec((SUB + OUT_SUB, D), lambda i: (i, 0))],
        out_specs=[
            pl.BlockSpec((SUB, D), lambda i: (i, 0)),
            pl.BlockSpec((OUT_SUB, D), lambda i: (i, 0)),
        ],
        out_shape=[
            jax.ShapeDtypeStruct((FF_OWN, D), F32),
            jax.ShapeDtypeStruct((Q_OWN, D), F32),
        ],
        compiler_params=pltpu.CompilerParams(vmem_limit_bytes=32 * 1024 * 1024),
        cost_estimate=cost(1),
        name="down_out",
    )(rows)


def qkv_kernel(places, *refs):
    pieces, weights, outs, products, stack = refs[:8], refs[8:11], refs[11:14], *refs[14:]
    query, key, value = outs
    for i, piece in enumerate(pieces):
        stack[places[i]] = piece[...]
    for at in range(GROUP):
        values = stack[at].astype(F32)
        query[:, at * Q_OWN : (at + 1) * Q_OWN] = values[:, :Q_OWN]
        head = key if at % 2 == 0 else value
        place = (at // 2) * HEAD_DIM
        head[:, place : place + HEAD_DIM] = values[:, Q_OWN : Q_OWN + HEAD_DIM]
    total = sum(
        jnp.sum(out[...] * weight[...].astype(F32), axis=1, keepdims=True)
        for out, weight in zip(outs, weights, strict=True)
    )
    products[...] = jnp.broadcast_to(total, (CHUNK, 128)).T[:8]


def assemble(kernel, places, pieces, rows, weights, shapes):
    count, width = pieces[0].shape
    return pl.pallas_call(
        kernel,
        grid_spec=pltpu.PrefetchScalarGridSpec(
            num_scalar_prefetch=1,
            grid=(count // rows,),
            in_specs=[pl.BlockSpec((rows, width), lambda i, places: (i, 0))] * 8
            + [pl.BlockSpec((rows, w.shape[1]), lambda i, places: (i, 0)) for w in weights],
            out_specs=[
                pl.BlockSpec((block, columns), lambda i, places: (i, 0))
                for _, block, columns in shapes
            ],
            scratch_shapes=[pltpu.VMEM((GROUP, rows, width), BF16)],
        ),
        out_shape=[jax.ShapeDtypeStruct((whole, columns), F32) for whole, _, columns in shapes],
        compiler_params=pltpu.CompilerParams(vmem_limit_bytes=48 * 1024 * 1024),
        cost_estimate=cost(1),
        name=kernel.__name__.removesuffix("_kernel"),
    )(places, *pieces, *weights)


def rms_scale(values):
    return lax.rsqrt(jnp.mean(values * values, axis=-1, keepdims=True) + EPSILON)


def rotate_t(values, cosine, sine_table):
    half = HEAD_DIM // 2
    first, second = values[:, :half], values[:, half:]
    return jnp.concatenate(
        [first * cosine - second * sine_table, second * cosine + first * sine_table], axis=1
    )


def norm_back(grad_normed, values, scale_rows, gain_full):
    unit_rows = values * scale_rows
    grad_unit = grad_normed * gain_full
    return scale_rows * (
        grad_unit - unit_rows * jnp.mean(grad_unit * unit_rows, axis=-1, keepdims=True)
    )


def contract(form, left, right):
    return jnp.einsum(form, left, right, preferred_element_type=F32)


def shards(
    inputs,
    positions,
    cotangent,
    w_query,
    w_key,
    w_value,
    w_out,
    w_gate,
    w_up,
    w_down,
    gain_attn,
    gain_mlp,
):
    zl, y, zh, x, core = (lax.axis_index(axis) for axis in AXES)
    xc = x * 2 + core
    group = ("x", "core")

    def gather_rows(rows):
        return lax.all_gather(rows, group, axis=0, tiled=True)

    inputs_near = near(inputs, "x")
    inputs_two = ring(inputs, "core", 1)

    index_here = (zh * GROUP + xc) * TOK + jnp.arange(TOK, dtype=jnp.int32)
    head_end = jnp.where(
        (zh == 0) & (xc == 0),
        jnp.sum((positions == index_here).astype(jnp.int32)),
        index_here[0] - positions[0],
    )
    meta = jnp.stack([zh, head_end]).astype(jnp.int32)
    rail = [((x + r) % 4) * 2 for r in range(4)]
    group_places = jnp.stack(
        [at + core for at in rail] + [at + 1 - core for at in rail]
    ).astype(jnp.int32)
    def columns(weight, width):
        return lax.dynamic_slice_in_dim(weight, xc * width, width, axis=1)

    kv_here = jnp.where(core == 0, w_key, w_value)
    kv_here = lax.dynamic_slice_in_dim(kv_here, x * HEAD_DIM, HEAD_DIM, axis=1)
    early = jnp.concatenate(
        [
            columns(w_query, Q_OWN),
            kv_here,
            gain_attn[:, None],
            gain_mlp[:, None],
            jnp.zeros((CHUNK, 62), BF16),
        ],
        axis=1,
    )
    early_near = near(early, "y")
    gate_up_here = take_columns(xc[None].astype(jnp.int32), w_gate, w_up)
    half_width = D // 2
    out_here = lax.dynamic_slice_in_dim(w_out, core * half_width, half_width, axis=1)
    down_here = stack_halves(lax.dynamic_slice_in_dim(w_down, xc * SUB, SUB, axis=0))
    early_blocks = (early, *early_near, *far(*early_near, "y"))
    early_blocks, inputs_near, out_here = join(early_blocks, inputs_near, out_here)
    early_z = across_z(*early_blocks)
    inputs_far = far(*inputs_near, "x")
    out_near = near(out_here, "y")
    early_z, inputs_far, inputs_two, gate_up_here = join(
        early_z, inputs_far, inputs_two, gate_up_here
    )
    inputs_rest = (
        ring(jnp.concatenate(inputs_near), "core", 1),
        ring(jnp.concatenate(inputs_far), "core", 1),
    )
    full_qkv_gains = put_weights(early_blocks, early_z, zl, y)
    full_qkv_gains, inputs_rest, out_near = join(full_qkv_gains, inputs_rest, out_near)
    out_far = far(*out_near, "y")
    gate_up_other = both_parities(gate_up_here)
    normed, gains = gather_norm(
        group_places,
        [inputs, *inputs_near, *inputs_far, inputs_two, *inputs_rest],
        full_qkv_gains,
    )
    full_qkv = full_qkv_gains[:, : Q_OWN + HEAD_DIM]
    full_gain_attn, full_gain_mlp = gains[0], gains[1]

    index_all = zh * HALF + jnp.arange(HALF, dtype=jnp.int32)
    doc_start = jnp.where(
        index_all < head_end,
        0,
        jnp.where(index_all < head_end + MIDDLE, head_end, head_end + MIDDLE),
    )
    frequency = THETA ** (-(jnp.arange(HEAD_DIM // 2, dtype=F32) * 2.0 / HEAD_DIM))
    angles = frequency[:, None] * (index_all - doc_start).astype(F32)[None, :]
    cosine, sine_table = jnp.cos(angles), jnp.sin(angles)
    is_key = core == 0
    cosine_kv = jnp.where(is_key, cosine, 1.0)
    sine_kv = jnp.where(is_key, sine_table, 0.0)

    raw_t = contract("dn,td->nt", full_qkv, normed)
    query_t = (
        rotate_t(raw_t[:Q_OWN].reshape(HEADS_OWN, HEAD_DIM, HALF), cosine, sine_table)
        .reshape(Q_OWN, HALF)
        .astype(BF16)
        * (1.0 / math.sqrt(HEAD_DIM))
    ).astype(BF16)
    kv_t = rotate_t(raw_t[Q_OWN:][None], cosine_kv, sine_kv)[0].astype(BF16)
    kv_other = ring(kv_t, "core", 1)
    kv_prev = lax.ppermute(kv_t, "zh", [(0, 1)])
    kv_prev_other = lax.ppermute(kv_t, ("zh", "core"), [(0, 3), (1, 2)])
    kv_t, kv_other, kv_prev, kv_prev_other, query_t, gate_up_here, gate_up_other, out_far = join(
        kv_t, kv_other, kv_prev, kv_prev_other, query_t, gate_up_here, gate_up_other, out_far
    )
    mine = jnp.concatenate([kv_prev, kv_t], axis=1)
    theirs = jnp.concatenate([kv_prev_other, kv_other], axis=1)
    keys_t = jnp.where(is_key, mine, theirs)
    values_t = jnp.where(is_key, theirs, mine)
    out_blocks = (out_here, *out_near, *out_far)
    gate_up_pair = jnp.concatenate([gate_up_here, *gate_up_other])
    gate_up_near = near(gate_up_pair, "y")
    out_z = across_z(*out_blocks)
    attended = attend(meta, query_t, keys_t, values_t)
    (attn_t, mixed_t, lse), out_z, gate_up_near = join(attended, out_z, gate_up_near)
    mixed_parts = exchange_x(mixed_t.reshape(4, 2, Q_OWN, TOK), x)
    gate_up_far = far(*gate_up_near, "y")
    out_half = put_weights(out_blocks, out_z, zl, y)
    mixed_parts, out_half = join(mixed_parts, out_half)
    mixed_others = ring(jnp.concatenate(mixed_parts), "core", 1)
    mixed_others, mixed_parts = join(mixed_others, mixed_parts)
    mixed_both = put_exchanged(mixed_parts, mixed_others, x, core)

    def of_core(values, at):
        return lax.dynamic_index_in_dim(values, at, 0, keepdims=False)

    out_rows = contract("ckt,kd->ctd", mixed_both.reshape(2, D, TOK), out_half).astype(BF16)
    out_mine = of_core(out_rows, core)
    out_theirs = ring(of_core(out_rows, 1 - core), "core", 1)
    out_theirs, down_here, cotangent_here = join(out_theirs, down_here, cotangent)
    tokens_here = inputs.astype(F32)
    residual = tokens_here + jnp.concatenate(
        [
            jnp.where(core == 0, out_mine, out_theirs),
            jnp.where(core == 0, out_theirs, out_mine),
        ],
        axis=1,
    ).astype(F32)
    scale_mlp = rms_scale(residual)
    normed_rows = (residual * scale_mlp * full_gain_mlp).astype(BF16)
    normed_mlp = gather_rows(normed_rows)
    down_other = both_parities(down_here)
    cotangent_near = near(cotangent_here, "x")
    down_other, cotangent_near, gate_up_far = join(down_other, cotangent_near, gate_up_far)
    down_pair = jnp.concatenate([down_here, *down_other])
    down_near = near(down_pair, "y")
    cotangent_far = far(*cotangent_near, "x")
    gate_up_all = put_pairs(gate_up_pair, gate_up_near, gate_up_far, zl, y)
    normed_mlp, gate_up_all, down_near, cotangent_far = join(
        normed_mlp, gate_up_all, down_near, cotangent_far
    )

    gate_up = contract("td,df->tf", normed_mlp, gate_up_all)
    down_far = far(*down_near, "y")
    cotangent_blocks = (cotangent_here, *cotangent_near, *cotangent_far)
    cotangent_two = swap_blocks(*cotangent_blocks)
    gate_up, down_far, cotangent_two = join(gate_up, down_far, cotangent_two)
    cotangent_all = put_rows(cotangent_blocks, cotangent_two, group_places)
    full_down = put_row_pairs(down_pair, down_near, down_far, zl, y)
    grad_hidden = contract("td,fd->tf", cotangent_all, full_down)
    gate, upward = gate_up[:, :FF_OWN], gate_up[:, FF_OWN:]
    sigmoid_gate = jax.nn.sigmoid(gate)
    silu_gate = gate * sigmoid_gate
    hidden = (silu_gate * upward).astype(BF16)
    grad_acts = jnp.concatenate(
        [
            (grad_hidden * upward * sigmoid_gate * (1.0 + gate * (1.0 - sigmoid_gate))).astype(BF16),
            (grad_hidden * silu_gate).astype(BF16),
        ],
        axis=1,
    )
    back_rows = rows_to_core(contract("tf,df->td", grad_acts, gate_up_all), core)

    def columns_at(values, start, count):
        return lax.dynamic_slice_in_dim(values, start * CHUNK, count * CHUNK, axis=1)

    other = (1 - zl) * 4

    def gate_up_product(start, count):
        rows = contract("td,tf->df", columns_at(normed_mlp, start, count), grad_acts)
        return rows.astype(BF16).reshape(count, CHUNK, 2 * FF_OWN)

    gate_up_theirs = gate_up_product(other, 4)
    back_total = back_rows[0].astype(F32) + back_rows[1].astype(F32)
    back_total, gate_up_pairs, hidden, normed_mlp, grad_acts = join(
        back_total, (gate_up_theirs[:2], gate_up_theirs[2:]), hidden, normed_mlp, grad_acts
    )
    gate_up_z = scatter_z(gate_up_pairs)
    back_rows = rows_along_x(back_total, x)
    gate_up_mine = gate_up_product(zl * 4, 4)
    part_down = contract("tf,td->fd", hidden, cotangent_all).astype(BF16)
    part_down = part_down.reshape(8, SUB, D)
    part_output = contract("tf,fd->td", hidden, full_down).astype(BF16)
    back_rows, gate_up_z, gate_up_mine, part_down, part_output = join(
        back_rows, gate_up_z, gate_up_mine, part_down, part_output
    )
    gate_up_far = far_along_y(gate_up_mine, gate_up_z, y)
    grad_normed_mlp = add_up(back_rows)
    grad_residual = cotangent.astype(F32) + norm_back(
        grad_normed_mlp, residual, scale_mlp, full_gain_mlp
    )
    grad_here = grad_residual.astype(BF16)
    grad_theirs = ring(grad_here, "core", 1)
    grad_theirs, grad_here, gate_up_mine, gate_up_z = join(
        grad_theirs, grad_here, gate_up_mine, gate_up_z
    )
    grad_both = jnp.stack(
        [jnp.where(core == 0, grad_here, grad_theirs), jnp.where(core == 0, grad_theirs, grad_here)]
    )
    grad_both = jnp.where(core == 0, grad_both[..., :half_width], grad_both[..., half_width:])
    grad_partial = contract("kd,ctd->kct", out_half, grad_both).reshape(4, 2, Q_OWN, 2, TOK)

    def heads_of(at):
        return lax.dynamic_index_in_dim(grad_partial, at, 1, keepdims=False)

    grad_arrived = ring(heads_of(1 - core).astype(BF16), "core", 1)
    grad_arrived, gate_up_far = join(grad_arrived, gate_up_far)
    grad_heads = (heads_of(core) + grad_arrived.astype(F32)).astype(BF16)
    grad_parts = exchange_x(grad_heads.transpose(0, 2, 1, 3), x)
    grad_attn_out = gather_rows(grad_here)
    gate_up_y = near_along_y(gate_up_mine, gate_up_z, gate_up_far, y)
    grad_parts, gate_up_y, part_output = join(grad_parts, gate_up_y, part_output)
    output_rows = lax.psum_scatter(part_output, group, scatter_dimension=0, tiled=True)
    gate_up_zh = scatter_zh(gate_up_y)
    places = jnp.stack([(x - r) % 4 * 2 for r in range(4)]).astype(jnp.int32)
    grad_mixed_t = put_in_place(places, grad_parts, [(r, 0, 2) for r in range(4)], GROUP)
    back_args = (query_t, grad_mixed_t, attn_t, lse, keys_t, values_t)
    attended = attend_back(meta, 0, 4, *back_args)
    (query_0, *key_sums), gate_up_zh, grad_attn_out = join(attended, gate_up_zh, grad_attn_out)
    shard_gate_up = both_halves(gate_up_zh)
    part_out = contract(
        "bkt,btd->kd", mixed_t, grad_attn_out.reshape(GROUP, TOK, D)
    ).astype(BF16)
    part_down_out = jnp.concatenate([part_down, part_out.reshape(8, OUT_SUB, D)], axis=1)

    def chunks(start, count):
        return lax.dynamic_slice_in_dim(part_down_out, start, count, axis=0)

    down_out_pairs = (chunks(other, 2), chunks(other + 2, 2))
    down_out_pairs, key_sums = join(down_out_pairs, key_sums)
    down_out_z = scatter_z(down_out_pairs)
    attended = attend_back(meta, 4, 8, *back_args, *key_sums)
    (query_1, grad_keys_t, grad_values_t), down_out_z, output_rows, shard_gate_up = join(
        attended, down_out_z, output_rows, shard_gate_up
    )
    gate_up_grads = gather_rows(shard_gate_up)
    grad_query_t = jnp.concatenate([query_0, query_1])

    kept = jnp.where(is_key, grad_keys_t, grad_values_t)
    given = jnp.where(is_key, grad_values_t, grad_keys_t)
    arrived = ring(given.astype(BF16), "core", 1)
    arrived, kept, grad_query_t = join(arrived, kept, grad_query_t)
    grad_kv = kept + arrived.astype(F32)
    from_next = lax.ppermute(grad_kv[:, :HALF].astype(BF16), "zh", [(1, 0)])
    from_next, grad_kv, grad_query_t = join(from_next, grad_kv, grad_query_t)
    down_out_y = scatter_y(chunks(zl * 4, 4), down_out_z, y)
    grad_kv_t = grad_kv[:, HALF:] + from_next.astype(F32)

    def by_block(table):
        return table.reshape(-1, GROUP, TOK).transpose(1, 0, 2)

    half_head = HEAD_DIM // 2
    cosine_b, sine_b = by_block(cosine)[:, None], by_block(sine_table)[:, None]
    first = grad_query_t.reshape(GROUP, HEADS_OWN, HEAD_DIM, TOK)[:, :, :half_head]
    second = grad_query_t.reshape(GROUP, HEADS_OWN, HEAD_DIM, TOK)[:, :, half_head:]
    turned = jnp.concatenate(
        [first * cosine_b + second * sine_b, second * cosine_b - first * sine_b], axis=2
    ).reshape(GROUP, Q_OWN, TOK)
    grad_qkv = jnp.concatenate(
        [turned, by_block(rotate_t(grad_kv_t[None], cosine_kv, -sine_kv)[0])], axis=1
    ).astype(BF16)
    grad_qkv_rows = grad_qkv.transpose(0, 2, 1).reshape(HALF, Q_OWN + HEAD_DIM)
    part_normed = contract("tn,dn->td", grad_qkv_rows, full_qkv).astype(BF16)

    def qkv_product(start, count):
        rows = contract("td,tn->dn", columns_at(normed, start, count), grad_qkv_rows)
        return rows.astype(BF16).reshape(count, CHUNK, Q_OWN + HEAD_DIM)

    qkv_pairs = [qkv_product(other, 2), qkv_product(other + 2, 2)]
    normed_pair = rows_to_core(part_normed, core)
    normed_pair, qkv_pairs, grad_qkv_rows = join(normed_pair, qkv_pairs, grad_qkv_rows)
    qkv_z = scatter_z(qkv_pairs)
    qkv_mine = qkv_product(zl * 4, 4)
    normed_total = normed_pair[0].astype(F32) + normed_pair[1].astype(F32)
    qkv_z, qkv_mine, down_out_y, normed_total = join(qkv_z, qkv_mine, down_out_y, normed_total)
    qkv_y = scatter_y(qkv_mine, qkv_z, y)
    normed_first = far_rows_along_x(normed_total, x)
    down_out_zh = scatter_zh(down_out_y)
    qkv_y, down_out_zh, normed_total, normed_first, gate_up_grads = join(
        qkv_y, down_out_zh, normed_total, normed_first, gate_up_grads
    )
    qkv_zh = scatter_zh(qkv_y)
    normed_parts = near_rows_along_x(normed_total, normed_first, x)
    shard_down_out = both_halves(down_out_zh)
    turned_out = swap_roles(shard_down_out[SUB:])
    qkv_zh, turned_out, normed_parts, gate_up_grads = join(
        qkv_zh, turned_out, normed_parts, gate_up_grads
    )
    grad_gate, grad_up, mlp_products = put_gate_up(gate_up_grads, w_gate, w_up)
    down_out_all = gather_rows(jnp.concatenate([shard_down_out[:SUB], turned_out]))
    qkv_rail = rail_of(both_halves(qkv_zh))
    grad_normed = add_up(normed_parts)
    output = (residual + output_rows.astype(F32)).astype(BF16)
    scale_here = rms_scale(tokens_here)
    grad_inputs = grad_residual + norm_back(grad_normed, tokens_here, scale_here, full_gain_attn)

    grad_down, grad_out = split_down_out(down_out_all)
    kv_columns = KV_HEADS * HEAD_DIM
    grad_query, grad_key, grad_value, attn_products = assemble(
        qkv_kernel,
        group_places,
        with_other_core(qkv_rail),
        CHUNK,
        [w_query, w_key, w_value],
        [
            (CHUNK, CHUNK, HEADS * HEAD_DIM),
            (CHUNK, CHUNK, kv_columns),
            (CHUNK, CHUNK, kv_columns),
            (8, 8, CHUNK),
        ],
    )
    return (
        output,
        grad_inputs,
        grad_query,
        grad_key,
        grad_value,
        grad_out,
        grad_gate,
        grad_up,
        grad_down,
        attn_products[0] / gain_attn.astype(F32),
        mlp_products[:, 0] / gain_mlp.astype(F32),
    )


def solution(mesh):
    split = Mesh(mesh.devices.reshape(2, 4, 2, 4, 2), AXES)
    dp, tokens = ("zl", "y"), AXES
    matrix = P(dp, None)
    return jax.shard_map(
        shards,
        mesh=split,
        in_specs=(
            P(tokens, None),
            P(tokens),
            P(tokens, None),
            matrix,
            matrix,
            matrix,
            matrix,
            matrix,
            matrix,
            matrix,
            P(dp),
            P(dp),
        ),
        out_specs=(
            P(tokens, None),
            P(tokens, None),
            matrix,
            matrix,
            matrix,
            matrix,
            matrix,
            matrix,
            matrix,
            P(dp),
            P(dp),
        ),
        check_vma=False,
    )
```
